32 devices in a mesh: dp: 8 (over z, y), state: 4 (over x, core).
Axes of the slice: x: 2, y: 2, z: 4, core: 2. Of those that a mesh axis runs over, the one named last changes fastest.
Arguments:
- token_ids: int32 [8, 1024], P('dp'), may hold values from 0 to 31999
- doc_starts: int32 [8, 4], P('dp'), may hold values from 0 to 1023, as said below
- loss_positions: int32 [8, 128], P('dp'), may hold values from 0 to 1023
- loss_targets: int32 [8, 128], P('dp'), may hold values from -1 to 31999, as said below
- owners: int32 [32], replicated, may hold values from 0 to 7, as said below
- in_weight: float32 [4, 40, 64, 4352], P('state', 'dp'), may hold values from -0.125 to 0.125
- out_weight: float32 [4, 40, 64, 1920], P('state', 'dp'), may hold values from -0.125 to 0.125
- table_weight: float32 [4, 40, 64, 8000], P('state', 'dp')
- gain_weight: float32 [40, 4, 64], P('dp'), may hold values from 0.5 to 1.5
- in_first: float32 [4, 40, 64, 4352], P('state', 'dp'), may hold values from -2.670288e-05 to 2.670288e-05
- out_first: float32 [4, 40, 64, 1920], P('state', 'dp'), may hold values from -2.670288e-05 to 2.670288e-05
- table_first: float32 [4, 40, 64, 8000], P('state', 'dp'), may hold values from -2.670288e-05 to 2.670288e-05
- gain_first: float32 [40, 4, 64], P('dp'), may hold values from -0.00024414062 to 0.00024414062
- in_second: float32 [4, 40, 64, 4352], P('state', 'dp'), may hold values from 1.7105067e-12 to 2.7368108e-11
- out_second: float32 [4, 40, 64, 1920], P('state', 'dp'), may hold values from 1.7105067e-12 to 2.7368108e-11
- table_second: float32 [4, 40, 64, 8000], P('state', 'dp'), may hold values from 1.7105067e-12 to 2.7368108e-11
- gain_second: float32 [40, 4, 64], P('dp'), may hold values from 1.7105067e-10 to 2.7368108e-09
- in_average: float32 [4, 40, 64, 4352], P('state', 'dp'), may hold values from -0.125 to 0.125
- out_average: float32 [4, 40, 64, 1920], P('state', 'dp'), may hold values from -0.125 to 0.125
- table_average: float32 [4, 40, 64, 8000], P('state', 'dp'), may hold values from -0.125 to 0.125
- gain_average: float32 [40, 4, 64], P('dp'), may hold values from 0.5 to 1.5
Outputs:
- in_weight_new: float32 [4, 40, 64, 4352], P('state', 'dp')
- out_weight_new: float32 [4, 40, 64, 1920], P('state', 'dp')
- table_weight_new: float32 [4, 40, 64, 8000], P('state', 'dp')
- gain_weight_new: float32 [40, 4, 64], P('dp')
- in_first_new: float32 [4, 40, 64, 4352], P('state', 'dp')
- out_first_new: float32 [4, 40, 64, 1920], P('state', 'dp')
- table_first_new: float32 [4, 40, 64, 8000], P('state', 'dp')
- gain_first_new: float32 [40, 4, 64], P('dp')
- in_second_new: float32 [4, 40, 64, 4352], P('state', 'dp')
- out_second_new: float32 [4, 40, 64, 1920], P('state', 'dp')
- table_second_new: float32 [4, 40, 64, 8000], P('state', 'dp')
- gain_second_new: float32 [40, 4, 64], P('dp')
- in_average_new: float32 [4, 40, 64, 4352], P('state', 'dp')
- out_average_new: float32 [4, 40, 64, 1920], P('state', 'dp')
- table_average_new: float32 [4, 40, 64, 8000], P('state', 'dp')
- gain_average_new: float32 [40, 4, 64], P('dp')
- loss_sum: float32 [], replicated
- token_count: float32 [], replicated
- grad_norm: float32 [], replicated
The draws below stay inside these ranges and needn't reach their ends.
Inputs may be any that keep to these rules, and one draw needn't show every extreme that they name: `owners`: every index of dp owns between 3 and 5 blocks, and some index owns exactly 5. `doc_starts`: each row's first start is 0 and the starts rise strictly. `loss_targets`: between one and all of a row's slots count; in the last row all count.
All inputs are finite; a program needn't handle non-finite values.
Results may differ from the reference program's by a relative error of at most 0.0173.
Values may be sent and summed in bfloat16 or wider, within the bound.
A program may use at most 640 MiB of HBM per device.

```python
import math
import jax
import jax.numpy as jnp
import numpy as np
from jax import lax

D = 2048
HEADS = 16
KEY_DIM = 128
FF = 5632
VOCAB = 32000
SEQ = 1024
NLOSS = 128
NDOC = 4
GROUP = 128
BLK_DEV = 4
STEP = 5
VAL_DIM = 128
CAP = 5
NB = 32
RB = 64
SLOTS = 40
KS = 32
HS = 4
FS = 1408
VS = 8000
CIN = 4352
COUT = 1920
PARAMS = 116924416
N_DP = 8
N_STATE = 4


def draw_owners(key, part):
    pairs = N_DP // 2
    keys = jax.random.split(key, 4)
    shifts = jax.random.randint(keys[0], (pairs,), 0, 2)
    forced = jax.random.randint(keys[1], (), 0, pairs)
    shifts = jnp.where(jnp.arange(pairs) == forced, 1, shifts)
    signs = jax.random.randint(keys[2], (pairs,), 0, 2) * 2 - 1
    counts = jnp.stack([BLK_DEV - signs * shifts, BLK_DEV + signs * shifts], axis=1).reshape(N_DP)
    ends = jnp.cumsum(counts)
    ordered = jnp.sum((jnp.arange(NB)[:, None] >= ends[None, :]).astype(jnp.int32), axis=1)
    shuffle = jax.random.permutation(keys[3], NB)
    return ordered[shuffle].astype(jnp.int32)


def draw_doc_starts(key, part):
    keys = jax.random.split(key, N_DP)

    def one_row(row_key):
        picks = jax.random.permutation(row_key, SEQ - 1)[:NDOC - 1] + 1
        return jnp.concatenate([jnp.zeros((1,), jnp.int32), jnp.sort(picks).astype(jnp.int32)])
    return jax.vmap(one_row)(keys).astype(jnp.int32)


def draw_loss_targets(key, part):
    keys = jax.random.split(key, 3)
    row_ids = jnp.arange(N_DP)
    base = NLOSS // 3 + 2 * NLOSS // 3 * row_ids // max(N_DP - 1, 1)
    jitter = jax.random.randint(keys[0], (N_DP,), 0, NLOSS // 8 + 1)
    live = jnp.where(row_ids == N_DP - 1, NLOSS, jnp.maximum(base - jitter, 1))
    orders = jax.vmap(lambda row_key: jax.random.permutation(row_key, NLOSS))(jax.random.split(keys[1], N_DP))
    targets = jax.random.randint(keys[2], (N_DP, NLOSS), 0, VOCAB)
    return jnp.where(orders < live[:, None], targets, -1).astype(jnp.int32)


def draw_table_weight(key, part):
    shape = (N_STATE, SLOTS, RB, VS)
    steps = jnp.arange(N_STATE, dtype=jnp.float32) / max(N_STATE - 1, 1)
    rising = 1.0 + 2.0 * steps
    base = jax.random.normal(key, shape, jnp.float32)
    return base * rising[:, None, None, None] / math.sqrt(D)


def set_ends(drawn, stream_key, low, high):
    dims = drawn.shape
    place = [jax.random.randint(jax.random.fold_in(stream_key, axis), (), 0, dims[axis]) for axis in range(len(dims))]
    drawn = drawn.at[tuple(place)].set(low)
    longest = dims.index(max(dims))
    place[longest] = (place[longest] + 1) % dims[longest]
    return drawn.at[tuple(place)].set(high)


def block_scale(rng, shape, shards, least, top_value):
    loudness = 1.0
    for dim, parts in shards:
        draws = jax.random.uniform(jax.random.fold_in(jax.random.fold_in(rng, 6), dim), (parts,), jnp.float32, least / len(shards), top_value / len(shards))
        loudness = loudness * jnp.repeat(jnp.exp(draws), shape[dim] // parts).reshape((-1,) + (1,) * (len(shape) - 1 - dim))
    return loudness


def rank_table(number_of, slope):
    loads = [(1 << 20) // math.isqrt(standing ** slope) + 1 for standing in range(1, number_of + 1)]
    width = 1 + sum(loads) // (1 << 30)
    return np.cumsum(np.array([max(1, weight // width) for weight in loads]))


def ranked_ids(stream_key, dims, count, slope):
    table = rank_table(count, slope)
    pick = jax.random.randint(jax.random.fold_in(stream_key, 1), dims, 0, int(table[count - 1]))
    rank = jnp.searchsorted(jnp.asarray(table, jnp.int32), pick, side="right")
    return jax.random.permutation(jax.random.fold_in(stream_key, 2), count)[rank].astype(jnp.int32)


def centred(rng, shape, spread, most, cuts=(), kind=jnp.bfloat16):
    entries = jax.random.normal(rng, shape, jnp.float32) * spread
    if len(cuts) > 0:
        entries = block_scale(rng, shape, cuts, -0.22, 0.18) * entries
    return jnp.clip(entries, min=-most, max=most).astype(kind)


def setup_inputs(seed: int = 0) -> dict:
    streams_of = jax.random.split(jax.random.key(seed), 22)
    token_ids = set_ends(ranked_ids(streams_of[0], (N_DP, SEQ), VOCAB, 2), jax.random.fold_in(streams_of[0], 3), 0, VOCAB - 1).astype(jnp.int32)
    doc_starts = draw_doc_starts(jax.random.fold_in(streams_of[21], 71), 0)
    loss_positions = set_ends(jax.random.randint(streams_of[2], (N_DP, NLOSS), 0, SEQ), jax.random.fold_in(streams_of[2], 1), 0, SEQ - 1).astype(jnp.int32)
    loss_targets = draw_loss_targets(jax.random.fold_in(streams_of[21], 71), 0)
    owners = draw_owners(jax.random.fold_in(streams_of[21], 71), 0)
    in_weight = centred(streams_of[5], (N_STATE, SLOTS, RB, CIN), D ** -0.5, 0.125, ((0, 4), (1, 8)), jnp.float32)
    out_weight = centred(streams_of[6], (N_STATE, SLOTS, RB, COUT), D ** -0.5, 0.125, ((0, 4), (1, 8)), jnp.float32)
    table_weight = draw_table_weight(jax.random.fold_in(streams_of[21], 71), 0)
    gain_weight = jnp.clip(1.0 + 0.1 * jax.random.normal(streams_of[8], (SLOTS, 4, RB), jnp.float32), 0.5, 1.5)
    in_first = centred(streams_of[9], (N_STATE, SLOTS, RB, CIN), (0.02 / PARAMS ** 0.5), 2.6702880859375e-05, ((0, 4), (1, 8)), jnp.float32)
    out_first = centred(streams_of[10], (N_STATE, SLOTS, RB, COUT), (0.02 / PARAMS ** 0.5), 2.6702880859375e-05, ((0, 4), (1, 8)), jnp.float32)
    table_first = centred(streams_of[11], (N_STATE, SLOTS, RB, VS), (0.02 / PARAMS ** 0.5), 2.6702880859375e-05, ((0, 4), (1, 8)), jnp.float32)
    gain_first = centred(streams_of[12], (SLOTS, 4, RB), (0.2 / PARAMS ** 0.5), 0.00024414062, ((0, 8),), jnp.float32)
    in_second = jnp.clip(jnp.exp(math.log(2.7368107780034734e-11) - 2.7725887 * jax.random.uniform(streams_of[13], (N_STATE, SLOTS, RB, CIN), jnp.float32) ** block_scale(streams_of[13], (N_STATE, SLOTS, RB, CIN), ((0, 4), (1, 8)), -0.2, 0.2)), 1.7105067362521709e-12, 2.7368107780034734e-11)
    out_second = jnp.clip(jnp.exp(math.log(2.7368107780034734e-11) - 2.7725887 * jax.random.uniform(streams_of[14], (N_STATE, SLOTS, RB, COUT), jnp.float32) ** block_scale(streams_of[14], (N_STATE, SLOTS, RB, COUT), ((0, 4), (1, 8)), -0.2, 0.2)), 1.7105067362521709e-12, 2.7368107780034734e-11)
    table_second = jnp.clip(jnp.exp(math.log(2.7368107780034734e-11) - 2.7725887 * jax.random.uniform(streams_of[15], (N_STATE, SLOTS, RB, VS), jnp.float32) ** block_scale(streams_of[15], (N_STATE, SLOTS, RB, VS), ((0, 4), (1, 8)), -0.2, 0.2)), 1.7105067362521709e-12, 2.7368107780034734e-11)
    gain_second = jnp.clip(jnp.exp(math.log(2.7368107780034734e-09) - 2.7725887 * jax.random.uniform(streams_of[16], (SLOTS, 4, RB), jnp.float32) ** block_scale(streams_of[16], (SLOTS, 4, RB), ((0, 8),), -0.2, 0.2)), 1.7105067362521709e-10, 2.7368107780034734e-09)
    in_average = centred(streams_of[17], (N_STATE, SLOTS, RB, CIN), D ** -0.5, 0.125, ((0, 4), (1, 8)), jnp.float32)
    out_average = centred(streams_of[18], (N_STATE, SLOTS, RB, COUT), D ** -0.5, 0.125, ((0, 4), (1, 8)), jnp.float32)
    table_average = centred(streams_of[19], (N_STATE, SLOTS, RB, VS), D ** -0.5, 0.125, ((0, 4), (1, 8)), jnp.float32)
    gain_average = jnp.clip(1.0 + 0.1 * jax.random.normal(streams_of[20], (SLOTS, 4, RB), jnp.float32), 0.5, 1.5)
    return dict(token_ids=token_ids, doc_starts=doc_starts, loss_positions=loss_positions, loss_targets=loss_targets, owners=owners, in_weight=in_weight, out_weight=out_weight, table_weight=table_weight, gain_weight=gain_weight, in_first=in_first, out_first=out_first, table_first=table_first, gain_first=gain_first, in_second=in_second, out_second=out_second, table_second=table_second, gain_second=gain_second, in_average=in_average, out_average=out_average, table_average=table_average, gain_average=gain_average)


NORM_EPS = 1e-06
LOWER_BOUND = 0.9
CLIP_NORM = 0.02
BETA_FIRST = 0.5
BETA_SECOND = 0.5
ADAM_EPS = 1e-08
LEARN_RATE = 0.02
GAIN_RATE = 0.2
WEIGHT_DECAY = 0.1
AVERAGE_DECAY = 0.9
FULL_PRECISION = lax.Precision.HIGHEST

@jax.custom_vjp
def low(v):
    return lax.optimization_barrier(v.astype(jnp.bfloat16)).astype(jnp.float32)

@jax.custom_vjp
def low_back(v):
    return v

def low_keep(v):
    return (low(v), None)

def low_pass(kept, grad):
    return (grad,)

def back_keep(v):
    return (v, None)

def back_low(kept, grad):
    return (low(grad),)
low.defvjp(low_keep, low_pass)
low_back.defvjp(back_keep, back_low)

def rms_norm(values, gain):
    return values * lax.rsqrt(lax.optimization_barrier(jnp.mean(values * values, axis=-1, keepdims=True)) + NORM_EPS) * gain

def forget_gates(query_pre, forget_pre):
    query = jax.nn.silu(query_pre)
    key_gate = (1.0 - LOWER_BOUND) * jax.nn.sigmoid(-forget_pre)
    log_forget = jnp.log(LOWER_BOUND + (1.0 - LOWER_BOUND) * jax.nn.sigmoid(forget_pre))
    return (query, key_gate, log_forget)

def mixer(query, key_gate, log_forget, values, documents, block):
    blocks = query.shape[0] // block
    heads = query.shape[1]
    key_width = query.shape[2]
    value_width = values.shape[2]

    def split(array):
        return array.reshape((blocks, block) + array.shape[1:])
    causal = jnp.arange(block)[:, None] >= jnp.arange(block)[None, :]

    def advance(carry, inputs):
        running_state, previous = carry
        query_blk, key_blk, forget_blk, value_block, doc_blk = inputs
        cumulative = jnp.cumsum(forget_blk, axis=0)
        decayed_query = query_blk * jnp.exp(cumulative)
        key_decay = key_blk * jnp.exp(-cumulative)
        allowed = causal & (doc_blk[:, None] == doc_blk[None, :])
        scores = jnp.einsum('thk,shk->hts', decayed_query, key_decay, precision=FULL_PRECISION)
        scores = jnp.where(allowed[None], scores, 0.0)
        inner = jnp.einsum('hts,shv->thv', scores, value_block, precision=FULL_PRECISION)
        carried_state = (doc_blk == previous).astype(jnp.float32)
        outer_product = jnp.einsum('uwc,wcx->uwx', decayed_query, running_state, precision=FULL_PRECISION) * carried_state[:, None, None]
        total_amount = cumulative[-1]
        last_doc = doc_blk[-1]
        keep_factor = (last_doc == previous).astype(jnp.float32)
        same_last = (doc_blk == last_doc).astype(jnp.float32)
        weight_blocks = key_blk * jnp.exp(total_amount[None] - cumulative) * same_last[:, None, None]
        running_state = jnp.exp(total_amount)[:, :, None] * running_state * keep_factor + jnp.einsum('ayd,aye->yde', weight_blocks, value_block, precision=FULL_PRECISION)
        return ((running_state, last_doc), inner + outer_product)
    start = (jnp.zeros((heads, key_width, value_width), jnp.float32), jnp.array(-1, jnp.int32))
    _, output = lax.scan(jax.checkpoint(advance), start, (split(query), split(key_gate), split(log_forget), split(values), split(documents)))
    return output.reshape(query.shape[0], heads, value_width)

def slot_index(owners, capacity):
    order = jnp.arange(owners.shape[0])
    earlier = (owners[:, None] == owners[None, :]) & (order[None, :] < order[:, None])
    ranks = lax.optimization_barrier(jnp.sum(earlier.astype(jnp.int32), axis=1))
    return (owners * capacity + ranks).astype(jnp.int32)

def document_ids(starts, length):
    return (lax.optimization_barrier(jnp.sum((jnp.arange(length)[:, None] >= starts[None, :]).astype(jnp.int32), axis=1)) - 1).astype(jnp.int32)

def adam_update(weight, first, second, average, grad, scale, rate, decay, occupied):
    clipped = scale * grad
    first_new = BETA_FIRST * first + (1.0 - BETA_FIRST) * clipped
    second_new = BETA_SECOND * second + (1.0 - BETA_SECOND) * clipped * clipped
    first_hat = first_new / (1.0 - BETA_FIRST ** STEP)
    second_hat = second_new / (1.0 - BETA_SECOND ** STEP)
    weight_new = weight - rate * (first_hat / (jnp.sqrt(second_hat) + ADAM_EPS) + decay * weight)
    average_new = AVERAGE_DECAY * average + (1.0 - AVERAGE_DECAY) * weight_new
    return (weight_new * occupied, first_new * occupied, second_new * occupied, average_new * occupied)

def dense(left, right):
    return jnp.dot(left, right, precision=FULL_PRECISION)

def row_loss(params, ids, starts, positions, targets):
    w_in, w_out, table, gains = params
    key_cols = HEADS * KS
    value_width = HS * VAL_DIM

    def keys_of(offset):
        return w_in[:, :, offset:offset + key_cols].reshape(N_STATE, D, HEADS, KS).transpose(1, 2, 0, 3).reshape(D, HEADS * KEY_DIM)
    w_query = keys_of(0)
    w_forget = keys_of(key_cols)
    value_start = 2 * key_cols
    gate_start = value_start + value_width
    w_value = w_in[:, :, value_start:gate_start].transpose(1, 0, 2).reshape(D, D)
    w_gate = w_in[:, :, gate_start:gate_start + FS].transpose(1, 0, 2).reshape(D, FF)
    w_up = w_in[:, :, gate_start + FS:].transpose(1, 0, 2).reshape(D, FF)
    w_output = w_out[:, :, :value_width].transpose(0, 2, 1).reshape(D, D)
    w_down = w_out[:, :, value_width:].transpose(0, 2, 1).reshape(FF, D)
    embedding = table.transpose(0, 2, 1).reshape(VOCAB, D)
    documents = document_ids(starts, SEQ)
    stream_zero = low_back(embedding[ids])
    normed_one = low(rms_norm(stream_zero, gains[0]))
    query_pre = low_back(dense(normed_one, w_query))
    forget_pre = low_back(dense(normed_one, w_forget))
    value_pre = low_back(dense(normed_one, w_value))
    query, key_gate, log_forget = forget_gates(query_pre, forget_pre)
    query = low(query)
    key_gate = low(key_gate)
    values = low(value_pre)
    mixed = mixer(query.reshape(SEQ, HEADS, KEY_DIM), key_gate.reshape(SEQ, HEADS, KEY_DIM), log_forget.reshape(SEQ, HEADS, KEY_DIM), values.reshape(SEQ, HEADS, VAL_DIM), documents, GROUP)
    mixed = low_back(mixed.reshape(SEQ, D))
    gated = low(rms_norm(mixed.reshape(SEQ, HEADS, VAL_DIM), gains[1].reshape(HEADS, VAL_DIM)).reshape(SEQ, D))
    stream_one = stream_zero + low_back(dense(gated, w_output))
    normed_two = low(rms_norm(stream_one, gains[2]))
    gate_pre = low_back(dense(normed_two, w_gate))
    up_pre = low_back(dense(normed_two, w_up))
    hidden = low(jax.nn.silu(gate_pre) * up_pre)
    stream_two = stream_one + low_back(dense(hidden, w_down))
    normed_three = low(rms_norm(stream_two, gains[3]))
    logits = low_back(dense(normed_three[positions], embedding.T))
    live = (targets >= 0).astype(jnp.float32)
    lse = jax.nn.logsumexp(logits, axis=1)
    picked = jnp.take_along_axis(logits, jnp.maximum(targets, 0)[:, None], axis=1)[:, 0]
    return jnp.sum((lse - picked) * live)

def reference(token_ids, doc_starts, loss_positions, loss_targets, owners, in_weight, out_weight, table_weight, gain_weight, in_first, out_first, table_first, gain_first, in_second, out_second, table_second, gain_second, in_average, out_average, table_average, gain_average):
    index = slot_index(owners, CAP)

    def assemble(slots):
        lowered = slots.astype(jnp.bfloat16).astype(jnp.float32)
        return lowered[:, index].reshape(N_STATE, D, slots.shape[3])
    gain_values = gain_weight.astype(jnp.bfloat16).astype(jnp.float32)[index].transpose(1, 0, 2).reshape(4, D)
    params = (assemble(in_weight), assemble(out_weight), assemble(table_weight), gain_values)
    live_total = jnp.sum((loss_targets >= 0).astype(jnp.float32))

    def objective(weight_blocks):

        def one_row(running, inputs):
            return (running + jax.checkpoint(row_loss)(weight_blocks, *inputs), None)
        summed, _ = lax.scan(one_row, jnp.zeros((), jnp.float32), (token_ids, doc_starts, loss_positions, loss_targets))
        return (summed / live_total, summed)
    _, pullback, loss_sum = jax.vjp(objective, params, has_aux=True)
    grads, = pullback(jnp.ones((), jnp.float32))

    def to_slots(grad):
        blocks = grad.reshape(N_STATE, NB, RB, grad.shape[2])
        return jnp.zeros((N_STATE, SLOTS, RB, grad.shape[2]), jnp.float32).at[:, index].set(blocks)
    grad_in = to_slots(grads[0])
    grad_out = to_slots(grads[1])
    grad_table = to_slots(grads[2])
    grad_gain = jnp.zeros((SLOTS, 4, RB), jnp.float32).at[index].set(grads[3].reshape(4, NB, RB).transpose(1, 0, 2))
    squares = jnp.sum(grad_in * grad_in) + jnp.sum(grad_out * grad_out) + jnp.sum(grad_table * grad_table) + jnp.sum(grad_gain * grad_gain)
    grad_norm = jnp.sqrt(squares)
    scale = jnp.minimum(1.0, CLIP_NORM / (grad_norm + 1e-06))
    held = lax.optimization_barrier(jnp.sum((owners[None, :] == jnp.arange(N_DP)[:, None]).astype(jnp.int32), axis=1))
    occupied = (jnp.arange(CAP)[None, :] < held[:, None]).astype(jnp.float32).reshape(SLOTS)
    wide_occ = occupied[None, :, None, None]
    new_in = adam_update(in_weight, in_first, in_second, in_average, grad_in, scale, LEARN_RATE, WEIGHT_DECAY, wide_occ)
    new_out = adam_update(out_weight, out_first, out_second, out_average, grad_out, scale, LEARN_RATE, WEIGHT_DECAY, wide_occ)
    new_table = adam_update(table_weight, table_first, table_second, table_average, grad_table, scale, LEARN_RATE, WEIGHT_DECAY, wide_occ)
    new_gain = adam_update(gain_weight, gain_first, gain_second, gain_average, grad_gain, scale, GAIN_RATE, 0.0, occupied[:, None, None])
    return (new_in[0], new_out[0], new_table[0], new_gain[0], new_in[1], new_out[1], new_table[1], new_gain[1], new_in[2], new_out[2], new_table[2], new_gain[2], new_in[3], new_out[3], new_table[3], new_gain[3], loss_sum, live_total, grad_norm)
```

```python
import functools

import jax
import jax.numpy as jnp
from jax import lax
from jax.experimental import pallas as pl
from jax.experimental.pallas import tpu as pltpu
from jax.sharding import PartitionSpec as P

HEADS = 16
KEY_DIM = 128
GROUP = 128
STEP = 5
VAL_DIM = 128


NORM_EPS = 1e-06
LOWER_BOUND = 0.9
CLIP_NORM = 0.02
BETA_FIRST = 0.5
BETA_SECOND = 0.5
ADAM_EPS = 1e-08
LEARN_RATE = 0.02
GAIN_RATE = 0.2
WEIGHT_DECAY = 0.1
AVERAGE_DECAY = 0.9
FULL_PRECISION = lax.Precision.HIGHEST
LANES = 128


def rms_norm(values, gain, width):
    mean = jnp.sum(values * values, axis=-1, keepdims=True) * (1.0 / width)
    return values * lax.rsqrt(mean + NORM_EPS) * gain


def forget_gates(forget_pre):
    key_gate = (1.0 - LOWER_BOUND) * jax.nn.sigmoid(-forget_pre)
    log_forget = jnp.log(LOWER_BOUND + (1.0 - LOWER_BOUND) * jax.nn.sigmoid(forget_pre))
    return key_gate, log_forget


def slot_mixer(query, key_gate, log_forget, values, pick, allowed, heads):
    slots = query.shape[0]
    tokens = key_gate.shape[0]
    blocks = tokens // GROUP
    order = jnp.arange(GROUP)
    lower = (order[:, None] >= order[None, :]).astype(jnp.float32)
    number = jnp.arange(blocks)
    before = (number[:, None] > number[None, :]).astype(jnp.float32)
    inside = jnp.einsum(
        "ts,bsk->btk", lower, log_forget.reshape(blocks, GROUP, -1), precision=FULL_PRECISION
    )
    total = inside[:, -1]
    offset = jnp.dot(before, total, precision=FULL_PRECISION)
    ends = offset + total
    along = (inside + offset[:, None]).reshape(tokens, -1)
    at_slots = jnp.dot(pick, along, precision=FULL_PRECISION)
    key_decay = key_gate * jnp.exp(total[:, None] - inside).reshape(tokens, -1)
    grown = query[None] * jnp.exp(jnp.minimum(at_slots[None] - ends[:, None], 16.0))
    grown = grown.reshape(blocks, slots, heads, KEY_DIM)
    key_decay = key_decay.reshape(blocks, GROUP, heads, KEY_DIM)
    scores = jnp.einsum("bnhk,bghk->hnbg", grown, key_decay, precision=FULL_PRECISION)
    scores = jnp.where(allowed[None], scores.reshape(heads, slots, tokens), 0.0)
    mixed = jnp.einsum(
        "hns,shv->nhv", scores, values.reshape(tokens, heads, VAL_DIM), precision=FULL_PRECISION
    )
    return mixed.reshape(slots, -1)


def document_ids(starts, length):
    return jnp.sum((jnp.arange(length)[:, None] >= starts[None, :]).astype(jnp.int32), axis=1) - 1


def slot_index(owners, capacity):
    order = jnp.arange(owners.shape[0])
    earlier = (owners[:, None] == owners[None, :]) & (order[None, :] < order[:, None])
    ranks = jnp.sum(earlier.astype(jnp.int32), axis=1)
    return owners * capacity + ranks


def adam_update(weight, first, second, average, grad, scale, rate, decay, occupied):
    clipped = scale * grad
    first_new = BETA_FIRST * first + (1.0 - BETA_FIRST) * clipped
    second_new = BETA_SECOND * second + (1.0 - BETA_SECOND) * clipped * clipped
    first_hat = first_new / (1.0 - BETA_FIRST**STEP)
    second_hat = second_new / (1.0 - BETA_SECOND**STEP)
    weight_new = weight - rate * (first_hat / (jnp.sqrt(second_hat) + ADAM_EPS) + decay * weight)
    average_new = AVERAGE_DECAY * average + (1.0 - AVERAGE_DECAY) * weight_new
    return (
        weight_new * occupied,
        first_new * occupied,
        second_new * occupied,
        average_new * occupied,
    )


def times_plain(left, right):
    return jnp.dot(left, right, preferred_element_type=jnp.float32)


def times_right(left, right):
    return lax.dot_general(
        left, right, (((1,), (1,)), ((), ())), preferred_element_type=jnp.float32
    )


def times_left(left, right):
    return lax.dot_general(
        left, right, (((0,), (0,)), ((), ())), preferred_element_type=jnp.float32
    )


def swiglu(joined):
    half_width = joined.shape[1] // 2
    return jax.nn.silu(joined[:, :half_width]) * joined[:, half_width:]


EVERY = ("dp", "state")


def gather_state(values, axis=0):
    return lax.all_gather(values, "state", axis=axis, tiled=True)


def scatter_state(values, axis=0):
    return lax.psum_scatter(values, "state", scatter_dimension=axis, tiled=True)


def swap_dp(values):
    return lax.all_to_all(values, "dp", split_axis=0, concat_axis=0, tiled=True)


def spread_columns(own, parts):
    return own.reshape(own.shape[0], parts, -1).transpose(1, 0, 2)


def join_columns(split):
    return split.transpose(1, 0, 2).reshape(split.shape[1], -1)


MESH = pl.DeviceIdType.MESH


class Links:
    def __init__(self, sends, recvs):
        self.sends, self.recvs, self.used, self.open = sends, recvs, 0, []

    def copy(self, src, dst, dp, state):
        number = self.used
        self.used += 1
        made = pltpu.make_async_remote_copy(
            src_ref=src,
            dst_ref=dst,
            send_sem=self.sends.at[number],
            recv_sem=self.recvs.at[number],
            device_id=(dp, state),
            device_id_type=MESH,
        )
        made.start()
        self.open.append(made)
        return made

    def finish(self):
        for made in self.open:
            made.wait_send()


def greet(peers):
    barrier = pltpu.get_barrier_semaphore()
    for dp, state in peers:
        pl.semaphore_signal(barrier, inc=1, device_id=(dp, state), device_id_type=MESH)
    pl.semaphore_wait(barrier, len(peers))


def places(nd, ns):
    dp, st = lax.axis_index("dp"), lax.axis_index("state")
    return dp, st, lax.div(dp, 2), lax.rem(dp, 2), lax.div(st, 2), lax.rem(st, 2)


def near_peers(nd, ns):
    dp, st, z, y, x, c = places(nd, ns)
    deep, across = nd // 2, ns // 2
    peers = [(lax.rem(z + k, deep) * 2 + y, st) for k in range(1, deep)]
    peers.append((dp + 1 - 2 * y, st))
    peers += [(dp, lax.rem(x + k, across) * 2 + c) for k in range(1, across)]
    peers.append((dp, st + 1 - 2 * c))
    return peers


def small_gather_kernel(nd, ns, everyone, count, *refs):
    sources, outs, (sends, recvs) = refs[:count], refs[count : 2 * count], refs[2 * count :]
    dp, st = lax.axis_index("dp"), lax.axis_index("state")
    peers = []
    for a in range(nd):
        for b in range(ns if everyone else 1):
            if a or b:
                peers.append((lax.rem(dp + a, nd), lax.rem(st + b, ns)))
    greet(peers)
    me = dp * ns + st if everyone else dp
    links = Links(sends, recvs)
    for source, out in zip(sources, outs):
        out[me] = source[...]
        for there, far in peers:
            links.copy(source, out.at[me], there, far)
    for made in links.open:
        made.wait_recv()
    links.finish()


def small_gather(arrays, everyone, number):
    nd, ns = lax.axis_size("dp"), lax.axis_size("state")
    members = nd * ns if everyone else nd
    copies = (members - 1) * len(arrays)
    vmem = pl.BlockSpec(memory_space=pltpu.VMEM)
    return pl.pallas_call(
        functools.partial(small_gather_kernel, nd, ns, everyone, len(arrays)),
        out_shape=[jax.ShapeDtypeStruct((members,) + a.shape, a.dtype) for a in arrays],
        in_specs=[vmem] * len(arrays),
        out_specs=[vmem] * len(arrays),
        scratch_shapes=[pltpu.SemaphoreType.DMA((copies,)), pltpu.SemaphoreType.DMA((copies,))],
        compiler_params=pltpu.CompilerParams(collective_id=number, has_side_effects=True),
    )(*arrays)


def gather_all_kernel(nd, ns, in_ref, out_ref, sends, recvs):
    dp, st, z, y, x, c = places(nd, ns)
    deep, across = nd // 2, ns // 2
    half = in_ref.shape[1] // 2
    cols = (pl.ds(0, half), pl.ds(half, half))
    greet(near_peers(nd, ns))
    links = Links(sends, recvs)
    to_y = (dp + 1 - 2 * y, st)
    to_core = (dp, st + 1 - 2 * c)
    other_y = 1 - y

    def x_at(k):
        return lax.rem(x + k, across)

    def to_x(k):
        return (dp, x_at(k) * 2 + c)

    def group(xx, yy, part):
        return out_ref.at[c, xx, yy, :, :, cols[part]]

    def send(xx, yy, part, place):
        return links.copy(group(xx, yy, part), group(xx, yy, part), *place)

    out_ref[c, x, y, z] = in_ref[...]
    first = []
    for part in range(2):
        for k in range(1, deep):
            there = (lax.rem(z + k, deep) * 2 + y, st)
            first.append(
                links.copy(
                    in_ref.at[:, cols[part]], out_ref.at[c, x, y, z, :, cols[part]], *there
                )
            )
    for made in first[: deep - 1]:
        made.wait_recv()
    a_y = send(x, y, 0, to_y)
    for made in first[deep - 1 :]:
        made.wait_recv()
    b_x = [send(x, y, 1, to_x(k)) for k in range(1, across)]
    a_x = [send(x, y, 0, to_x(k)) for k in range(1, across)]
    b_y = send(x, y, 1, to_y)
    arriving = [send(x, y, 0, to_core), send(x, y, 1, to_core)]
    a_y.wait_recv()
    a_xy = [send(x, other_y, 0, to_x(k)) for k in range(1, across)]
    arriving.append(send(x, other_y, 0, to_core))
    b_xy = []
    for k in range(1, across):
        b_x[k - 1].wait_recv()
        from_x = lax.rem(x - k + across, across)
        b_xy.append(send(from_x, y, 1, to_y))
        arriving.append(send(from_x, y, 1, to_core))
    for k in range(1, across):
        a_x[k - 1].wait_recv()
        arriving.append(send(lax.rem(x - k + across, across), y, 0, to_core))
    b_y.wait_recv()
    arriving.append(send(x, other_y, 1, to_core))
    for k in range(1, across):
        from_x = lax.rem(x - k + across, across)
        a_xy[k - 1].wait_recv()
        arriving.append(send(from_x, other_y, 0, to_core))
        b_xy[k - 1].wait_recv()
        arriving.append(send(from_x, other_y, 1, to_core))
    for made in arriving:
        made.wait_recv()
    links.finish()


def gather_all(values, number):
    nd, ns = lax.axis_size("dp"), lax.axis_size("state")
    rows, wide = values.shape
    deep, across = nd // 2, ns // 2
    copies = 2 * (deep - 1) + 2 + 4 * (across - 1) + 4 * across
    vmem = pl.BlockSpec(memory_space=pltpu.VMEM)
    out = pl.pallas_call(
        functools.partial(gather_all_kernel, nd, ns),
        out_shape=jax.ShapeDtypeStruct((2, across, 2, deep, rows, wide), values.dtype),
        in_specs=[vmem],
        out_specs=vmem,
        scratch_shapes=[pltpu.SemaphoreType.DMA((copies,)), pltpu.SemaphoreType.DMA((copies,))],
        compiler_params=pltpu.CompilerParams(
            collective_id=number, has_side_effects=True, vmem_limit_bytes=40 * 2**20
        ),
    )(values)
    return out.reshape(nd * ns * rows, wide)


def scatter_all_kernel(
    nd, ns, in_ref, out_ref, rc, acc, rx_a, ry_a, rz_a, ry_b, rx_b, rz_b, sends, recvs
):
    dp, st, z, y, x, c = places(nd, ns)
    deep, across = nd // 2, ns // 2
    half = in_ref.shape[5] // 2
    cols = (pl.ds(0, half), pl.ds(half, half))
    greet(near_peers(nd, ns))
    links = Links(sends, recvs)
    to_y = (dp + 1 - 2 * y, st)
    to_core = (dp, st + 1 - 2 * c)
    ys = (y, 1 - y)

    def x_at(k):
        return lax.rem(x + k, across)

    def to_x(k):
        return (dp, x_at(k) * 2 + c)

    core = {}
    order = [(k, ky, 0) for k in range(1, across) for ky in (1, 0)]
    order += [(k, 1, 1) for k in range(across)]
    order += [(0, 1, 0)] + [(k, 0, 1) for k in range(1, across)] + [(0, 0, 0), (0, 0, 1)]
    for k, ky, part in order:
        core[k, ky, part] = links.copy(
            in_ref.at[1 - c, x_at(k), ys[ky], :, :, cols[part]],
            rc.at[x_at(k), ys[ky], :, :, cols[part]],
            *to_core,
        )

    def total(k, ky, part, zz, others):
        found = in_ref[c, x_at(k), ys[ky], zz, :, cols[part]].astype(jnp.float32)
        found += rc[x_at(k), ys[ky], zz, :, cols[part]].astype(jnp.float32)
        for other in others:
            found += other[zz].astype(jnp.float32)
        return found

    def add(k, ky, part, others):
        core[k, ky, part].wait_recv()

        @pl.loop(0, deep)
        def _(zz):
            acc[x_at(k), ys[ky], zz, :, cols[part]] = total(k, ky, part, zz, others).astype(
                acc.dtype
            )

        return acc.at[x_at(k), ys[ky], :, :, cols[part]]

    a_x, b_y = {}, {}
    for k in range(1, across):
        for ky in (1, 0):
            a_x[k, ky] = links.copy(add(k, ky, 0, []), rx_a.at[k - 1, ky], *to_x(k))
    for k in range(across):
        b_y[k] = links.copy(add(k, 1, 1, []), ry_b.at[k], *to_y)
    for k in range(1, across):
        a_x[k, 1].wait_recv()
    a_y = links.copy(
        add(0, 1, 0, [rx_a.at[k - 1, 1] for k in range(1, across)]), ry_a, *to_y
    )
    b_x = {}
    for k in range(1, across):
        b_y[k].wait_recv()
        b_x[k] = links.copy(add(k, 0, 1, [ry_b.at[k]]), rx_b.at[k - 1], *to_x(k))
    for k in range(1, across):
        a_x[k, 0].wait_recv()
    a_y.wait_recv()
    left = [rx_a.at[k - 1, 0] for k in range(1, across)] + [ry_a]
    add(0, 0, 0, left)

    def send_z(part, land):
        return [
            links.copy(
                acc.at[x, y, lax.rem(z + k, deep), :, cols[part]],
                land.at[k - 1],
                lax.rem(z + k, deep) * 2 + y,
                st,
            )
            for k in range(1, deep)
        ]

    a_z = send_z(0, rz_a)
    b_y[0].wait_recv()
    for k in range(1, across):
        b_x[k].wait_recv()
    right = [ry_b.at[0]] + [rx_b.at[k - 1] for k in range(1, across)]
    add(0, 0, 1, right)
    b_z = send_z(1, rz_b)
    for part, made, others, land in ((0, a_z, left, rz_a), (1, b_z, right, rz_b)):
        found = total(0, 0, part, z, others)
        for k in range(1, deep):
            made[k - 1].wait_recv()
            found += land[k - 1].astype(jnp.float32)
        out_ref[:, cols[part]] = found
    links.finish()


def scatter_all(values, number):
    nd, ns = lax.axis_size("dp"), lax.axis_size("state")
    deep, across = nd // 2, ns // 2
    rows, wide = values.shape[0] // (nd * ns), values.shape[1]
    half = wide // 2
    copies = 4 * across + 2 * (across - 1) + across + 1 + (across - 1) + 2 * (deep - 1)
    vmem = pl.BlockSpec(memory_space=pltpu.VMEM)
    kind = values.dtype
    return pl.pallas_call(
        functools.partial(scatter_all_kernel, nd, ns),
        out_shape=jax.ShapeDtypeStruct((rows, wide), jnp.float32),
        in_specs=[vmem],
        out_specs=vmem,
        scratch_shapes=[
            pltpu.VMEM((across, 2, deep, rows, wide), kind),
            pltpu.VMEM((across, 2, deep, rows, wide), kind),
            pltpu.VMEM((across - 1, 2, deep, rows, half), kind),
            pltpu.VMEM((deep, rows, half), kind),
            pltpu.VMEM((deep - 1, rows, half), kind),
            pltpu.VMEM((across, deep, rows, half), kind),
            pltpu.VMEM((across - 1, deep, rows, half), kind),
            pltpu.VMEM((deep - 1, rows, half), kind),
            pltpu.SemaphoreType.DMA((copies,)),
            pltpu.SemaphoreType.DMA((copies,)),
        ],
        compiler_params=pltpu.CompilerParams(
            collective_id=number, has_side_effects=True, vmem_limit_bytes=40 * 2**20
        ),
    )(values.reshape(2, across, 2, deep, rows, wide))


def lookup_kernel(nd, ns, in_ref, out_ref, rc, acc, rx, fin, sends, recvs):
    dp, st, z, y, x, c = places(nd, ns)
    across = ns // 2
    own = in_ref.shape[0]
    tokens = in_ref.shape[1] // nd
    part = tokens // ns
    to_core = (dp, st + 1 - 2 * c)
    peers = [(lax.rem(dp + k, nd), st) for k in range(1, nd)]
    peers += [(dp, lax.rem(x + k, across) * 2 + c) for k in range(1, across)]
    peers.append(to_core)
    greet(peers)
    links = Links(sends, recvs)

    def x_at(k):
        return lax.rem(x + k, across)

    def row_at(k):
        return lax.rem(dp + k, nd)

    def block(k, kx, cc):
        start = row_at(k) * tokens + (x_at(kx) * 2 + cc) * part
        return in_ref.at[:, pl.ds(pl.multiple_of(start, part), part)]

    def place(owner, share):
        return out_ref.at[
            pl.ds(pl.multiple_of(owner * own, own), own),
            pl.ds(pl.multiple_of(share * part, part), part),
        ]

    def add(sources, target):
        @pl.loop(0, own // 32)
        def _(i):
            rows = pl.ds(pl.multiple_of(i * 32, 32), 32)
            found = sources[0][rows, :].astype(jnp.float32)
            for source in sources[1:]:
                found += source[rows, :].astype(jnp.float32)
            target[rows, :] = found.astype(target.dtype)

    turn = list(range(1, nd)) + [0]
    core, across_x, across_dp = {}, {}, {}
    for k in turn:
        for kx in list(range(1, across)) + [0]:
            core[k, kx] = links.copy(block(k, kx, 1 - c), rc.at[k, kx], *to_core)
    for k in turn:
        for kx in range(1, across):
            core[k, kx].wait_recv()
            add([block(k, kx, c), rc.at[k, kx]], acc.at[k, kx - 1])
            across_x[k, kx] = links.copy(
                acc.at[k, kx - 1], rx.at[k, kx - 1], dp, x_at(kx) * 2 + c
            )
    for k in turn:
        core[k, 0].wait_recv()
        sources = [block(k, 0, c), rc.at[k, 0]]
        for kx in range(1, across):
            across_x[k, kx].wait_recv()
            sources.append(rx.at[k, kx - 1])
        if k:
            add(sources, fin.at[k - 1])
            across_dp[k] = links.copy(fin.at[k - 1], place(dp, st), row_at(k), st)
        else:
            add(sources, place(dp, st))
    later, last = {}, []
    for k in [0] + list(range(1, nd)):
        owner = lax.rem(dp - k + nd, nd)
        if k:
            across_dp[k].wait_recv()
        for kx in range(1, across):
            later[k, kx] = links.copy(
                place(owner, st), place(owner, st), dp, x_at(kx) * 2 + c
            )
        last.append(links.copy(place(owner, st), place(owner, st), *to_core))
    for k in range(nd):
        owner = lax.rem(dp - k + nd, nd)
        for kx in range(1, across):
            later[k, kx].wait_recv()
            share = lax.rem(x - kx + across, across) * 2 + c
            last.append(links.copy(place(owner, share), place(owner, share), *to_core))
    for made in last:
        made.wait_recv()
    links.finish()


def lookup_rows(values, number):
    nd, ns = lax.axis_size("dp"), lax.axis_size("state")
    across = ns // 2
    own, total = values.shape
    tokens = total // nd
    part = tokens // ns
    copies = nd * across + nd * (across - 1) + nd - 1 + nd * across + nd * (across - 1)
    vmem = pl.BlockSpec(memory_space=pltpu.VMEM)
    kind = values.dtype
    return pl.pallas_call(
        functools.partial(lookup_kernel, nd, ns),
        out_shape=jax.ShapeDtypeStruct((nd * own, tokens), kind),
        in_specs=[vmem],
        out_specs=vmem,
        scratch_shapes=[
            pltpu.VMEM((nd, across, own, part), kind),
            pltpu.VMEM((nd, across - 1, own, part), kind),
            pltpu.VMEM((nd, across - 1, own, part), kind),
            pltpu.VMEM((nd - 1, own, part), kind),
            pltpu.SemaphoreType.DMA((copies,)),
            pltpu.SemaphoreType.DMA((copies,)),
        ],
        compiler_params=pltpu.CompilerParams(
            collective_id=number, has_side_effects=True, vmem_limit_bytes=48 * 2**20
        ),
    )(values)


def swap_parts(values):
    nd = lax.axis_size("dp")
    me = lax.axis_index("dp")
    mine = lax.dynamic_index_in_dim(values, me, 0)
    found = lax.dynamic_update_index_in_dim(jnp.zeros_like(values), mine, me, 0)
    for k in range(1, nd):
        sent = lax.dynamic_index_in_dim(values, lax.rem(me + k, nd), 0)
        got = lax.ppermute(sent, "dp", [(i, (i + k) % nd) for i in range(nd)])
        found = lax.dynamic_update_index_in_dim(found, got, lax.rem(me - k + nd, nd), 0)
    return found


def on_device(
    token_ids,
    doc_starts,
    loss_positions,
    loss_targets,
    owners,
    in_weight,
    out_weight,
    table_weight,
    gain_weight,
    in_first,
    out_first,
    table_first,
    gain_first,
    in_second,
    out_second,
    table_second,
    gain_second,
    in_average,
    out_average,
    table_average,
    gain_average,
):
    f32 = jnp.float32
    bf16 = jnp.bfloat16
    nd = lax.axis_size("dp")
    ns = lax.axis_size("state")
    me_dp = lax.axis_index("dp")
    me_state = lax.axis_index("state")
    tokens = token_ids.shape[1]
    slots = loss_positions.shape[1]
    capacity = in_weight.shape[1]
    block_rows = in_weight.shape[2]
    block_count = owners.shape[0]
    width = block_rows * block_count
    own = capacity * block_rows
    wide = nd * own
    key_share = KEY_DIM // ns
    heads = HEADS // ns
    key_cols = HEADS * key_share
    value_width = heads * VAL_DIM
    mixer_cols = 2 * key_cols + value_width
    units = out_weight.shape[3] - value_width
    unit_part = units // nd
    vocab_share = table_weight.shape[3]
    vocab_part = -(-vocab_share // (nd * LANES)) * LANES
    quarter = tokens // ns
    slot_part = slots // ns

    held_all = jnp.sum((owners[None, :] == jnp.arange(nd)[:, None]).astype(jnp.int32), axis=1)
    occupied_all = jnp.arange(capacity)[None, :] < held_all[:, None]
    held = jnp.sum((owners == me_dp).astype(jnp.int32))
    occupied_here = jnp.arange(capacity) < held
    rows_here = jnp.repeat(occupied_here, block_rows)[:, None]

    def lowered(array):
        return jnp.where(rows_here, array[0].reshape(own, -1), 0.0).astype(bf16)

    in_own = lowered(in_weight)
    out_own = lowered(out_weight)
    table_own = lowered(table_weight)

    def in_rows(flat, multiple):
        flat = jnp.pad(flat, (0, -flat.shape[0] % (multiple * LANES)))
        return flat.reshape(-1, LANES)

    small, gains_all = small_gather(
        [
            in_rows(jnp.concatenate([token_ids[0], loss_targets[0]]), 8),
            in_rows(gain_weight.astype(bf16).reshape(-1), 16),
        ],
        False,
        1,
    )
    small = small.reshape(nd, -1)
    ids_all = small[:, :tokens]
    slot_targets = small[:, tokens : tokens + slots].reshape(nd // 2, 2, ns // 2, 2, slot_part)
    targets_all = slot_targets.transpose(3, 2, 1, 0, 4).reshape(-1)
    gains_all = gains_all.reshape(nd, -1)[:, : capacity * 4 * block_rows].astype(f32)
    gains_all = gains_all.reshape(nd * capacity, 4, block_rows)
    gains = jnp.where(occupied_all.reshape(-1)[:, None, None], gains_all, 0.0)
    gains = gains.transpose(1, 0, 2).reshape(4, wide)
    index = slot_index(owners, capacity)
    head_gain = lax.dynamic_slice_in_dim(
        gains_all[index][:, 1].reshape(width), me_state * value_width, value_width
    )
    live = (targets_all >= 0).astype(f32)
    count = jnp.sum(live)

    local_ids = ids_all.reshape(-1) - me_state * vocab_share
    hit = jnp.arange(vocab_share)[:, None] == local_ids[None, :]
    looked = times_plain(table_own, hit.astype(bf16)).astype(bf16)
    stream = lookup_rows(looked, 2)
    stream_mine = lax.dynamic_slice_in_dim(stream, me_state * quarter, quarter, axis=1)

    exchanged = in_own[:, : 2 * key_cols].reshape(own, 2, ns, heads * key_share)
    exchanged = exchanged.transpose(2, 0, 1, 3).reshape(ns, own * 2, heads, key_share)
    exchanged = lax.all_to_all(exchanged, "state", split_axis=0, concat_axis=0, tiled=True)
    exchanged = exchanged.transpose(1, 2, 0, 3).reshape(own, 2 * heads * KEY_DIM)
    mixer_own = jnp.concatenate(
        [exchanged, in_own[:, 2 * key_cols : mixer_cols], out_own[:, :value_width]], axis=1
    )
    mixer_weights = lax.all_gather(mixer_own, "dp", axis=0, tiled=True)
    qcols = heads * KEY_DIM
    w_qfv = mixer_weights[:, : 2 * qcols + value_width]
    w_q = mixer_weights[:, :qcols]
    w_fv = mixer_weights[:, qcols : 2 * qcols + value_width]
    w_o = mixer_weights[:, 2 * qcols + value_width :]
    ffn_own = jnp.stack(
        [
            in_own[:, mixer_cols : mixer_cols + units].reshape(own, nd, unit_part),
            in_own[:, mixer_cols + units :].reshape(own, nd, unit_part),
            out_own[:, value_width:].reshape(own, nd, unit_part),
        ],
        axis=2,
    ).reshape(own, nd * 3 * unit_part)
    ffn = swap_parts(spread_columns(ffn_own, nd)).reshape(wide, 3 * unit_part)
    w_gu = ffn[:, : 2 * unit_part]
    w_d = ffn[:, 2 * unit_part :]
    table_padded = jnp.pad(table_own, ((0, 0), (0, nd * vocab_part - vocab_share)))
    table = swap_parts(spread_columns(table_padded, nd)).reshape(wide, vocab_part)

    positions = loss_positions[0]
    pick_hit = positions[:, None] == jnp.arange(tokens)[None, :]
    pick = pick_hit.astype(f32)
    pick_low = pick_hit.astype(bf16)
    documents = document_ids(doc_starts[0], tokens)
    doc_at = jnp.sum(jnp.where(pick_hit, documents[None, :], 0), axis=1)
    allowed = (positions[:, None] >= jnp.arange(tokens)[None, :]) & (
        doc_at[:, None] == documents[None, :]
    )

    def tall_norm(values, gain):
        mean = jnp.sum(values * values, axis=0, keepdims=True) * (1.0 / width)
        return values * lax.rsqrt(mean + NORM_EPS) * gain[:, None]

    normed_one = tall_norm(stream.astype(f32), gains[0]).astype(bf16)
    normed_at = times_right(pick_low, normed_one).astype(bf16)
    stream_at = times_right(
        lax.dynamic_slice_in_dim(pick_low, me_state * slot_part, slot_part), stream
    )
    forget_value = times_left(normed_one, w_fv)
    query_pre = times_plain(normed_at, w_q)
    query, back_query = jax.vjp(jax.nn.silu, query_pre)
    (key_gate, log_forget), back_gates = jax.vjp(forget_gates, forget_value[:, :qcols])

    def mix(query_in, key_in, forget_in, value_in):
        return slot_mixer(query_in, key_in, forget_in, value_in, pick, allowed, heads)

    mixed, back_mix = jax.vjp(
        mix,
        query.astype(bf16).astype(f32),
        key_gate.astype(bf16).astype(f32),
        log_forget,
        forget_value[:, qcols:].astype(bf16).astype(f32),
    )

    def head_norm(mixed_in, gain_in):
        return rms_norm(
            mixed_in.reshape(slots, heads, VAL_DIM), gain_in.reshape(heads, VAL_DIM), VAL_DIM
        ).reshape(slots, value_width)

    gated_f, back_head = jax.vjp(head_norm, mixed, head_gain)
    gated = gated_f.astype(bf16)
    stream_one = stream_at + scatter_state(times_right(gated, w_o))

    def wide_norm(values, gain):
        return rms_norm(values, gain, width)

    normed_two, back_two = jax.vjp(wide_norm, stream_one, gains[2])
    rows_two = gather_all(normed_two.astype(bf16), 3)
    gate_up = times_plain(rows_two, w_gu)
    hidden_f, back_glu = jax.vjp(swiglu, gate_up)
    hidden = hidden_f.astype(bf16)
    stream_two = stream_one + scatter_all(times_right(hidden, w_d).astype(bf16), 4)
    normed_three, back_three = jax.vjp(wide_norm, stream_two, gains[3])
    rows_three = gather_all(normed_three.astype(bf16), 5)

    logits = times_plain(rows_three, table)
    column = jnp.arange(vocab_part)[None, :] + me_dp * vocab_part
    target_hit = (column + me_state * vocab_share == targets_all[:, None]) & (
        column < vocab_share
    )
    logits = jnp.where(column < vocab_share, logits, -1e30)
    top_here = jnp.max(logits, axis=1)
    sum_here = jnp.sum(jnp.exp(logits - top_here[:, None]), axis=1)
    picked_here = jnp.sum(jnp.where(target_hit, logits, 0.0), axis=1)
    shares = small_gather(
        [jnp.stack([top_here, sum_here, picked_here]).reshape(-1, LANES)], True, 6
    )[0].reshape(nd * ns, 3, -1)
    top = jnp.max(shares[:, 0], axis=0)
    lse = top + jnp.log(jnp.sum(shares[:, 1] * jnp.exp(shares[:, 0] - top[None]), axis=0))
    loss_sum = jnp.sum((lse - jnp.sum(shares[:, 2], axis=0)) * live)
    probs = jnp.exp(logits - lse[:, None])
    dlogits = ((probs - target_hit.astype(f32)) * (live / count)[:, None]).astype(bf16)
    grad_three = scatter_all(times_right(dlogits, table).astype(bf16), 7)
    grad_table_part = times_left(rows_three, dlogits).astype(bf16)
    grad_table_own = join_columns(swap_parts(grad_table_part.reshape(nd, own, vocab_part)))
    grad_table_own = grad_table_own[:, :vocab_share].astype(f32)

    grad_two, grad_gain_four = back_three(grad_three)
    down_rows = gather_all(grad_two.astype(bf16), 8)
    grad_hidden = times_plain(down_rows, w_d)
    grad_down = times_left(down_rows, hidden)
    (grad_gate_up,) = back_glu(grad_hidden)
    grad_gate_up = grad_gate_up.astype(bf16)
    grad_gu = times_left(rows_two, grad_gate_up)
    grad_norm_two = scatter_all(times_right(grad_gate_up, w_gu).astype(bf16), 9)
    grad_stream_one, grad_gain_three = back_two(grad_norm_two)
    grad_one = gather_state((grad_two + grad_stream_one).astype(bf16))
    grad_ffn = jnp.concatenate([grad_gu, grad_down], axis=1).astype(bf16)
    grad_ffn = join_columns(swap_parts(grad_ffn.reshape(nd, own, 3 * unit_part)))
    grad_ffn = grad_ffn.reshape(own, nd, 3, unit_part)

    grad_gated = times_plain(grad_one, w_o)
    grad_w_o = times_left(grad_one, gated)
    grad_mixed, grad_gain_two = back_head(grad_gated)
    grad_query, grad_key, grad_forget, grad_value = back_mix(
        grad_mixed.astype(bf16).astype(f32)
    )
    (grad_query_pre,) = back_query(grad_query)
    grad_query_pre = times_left(pick, grad_query_pre)
    (grad_forget_pre,) = back_gates((grad_key, grad_forget))
    grad_qfv = jnp.concatenate([grad_query_pre, grad_forget_pre, grad_value], axis=1).astype(bf16)
    grad_w_qfv = times_plain(normed_one, grad_qfv)
    grad_norm_one = scatter_state(times_right(w_qfv, grad_qfv).astype(bf16), 1).astype(f32)
    _, back_one = jax.vjp(tall_norm, stream_mine.astype(f32), gains[0])
    grad_stream_zero, grad_gain_one = back_one(grad_norm_one)
    pick_mine = lax.dynamic_slice_in_dim(pick_low, me_state * quarter, quarter, axis=1)
    grad_zero = (grad_stream_zero + times_left(grad_one, pick_mine)).astype(bf16)
    grad_mixer_own = lax.psum_scatter(
        jnp.concatenate([grad_w_qfv, grad_w_o], axis=1).astype(bf16),
        "dp",
        scatter_dimension=0,
        tiled=True,
    )

    embed = swap_dp(grad_zero.reshape(nd, own, quarter))
    embed = gather_state(embed, 2).transpose(1, 0, 2).reshape(own, nd * tokens)
    grad_lookup = times_right(embed, hit.astype(bf16))
    own_table = grad_table_own + grad_lookup

    returned = grad_mixer_own[:, : 2 * qcols].reshape(own * 2, heads, ns, key_share)
    returned = returned.transpose(2, 0, 1, 3)
    returned = lax.all_to_all(returned, "state", split_axis=0, concat_axis=0, tiled=True)
    returned = returned.reshape(ns, own, 2, heads * key_share).transpose(1, 2, 0, 3)
    returned = returned.reshape(own, 2 * key_cols)
    own_in = jnp.concatenate(
        [
            returned,
            grad_mixer_own[:, 2 * qcols : 2 * qcols + value_width],
            grad_ffn[:, :, 0].reshape(own, units),
            grad_ffn[:, :, 1].reshape(own, units),
        ],
        axis=1,
    ).astype(f32)
    own_out = jnp.concatenate(
        [grad_mixer_own[:, 2 * qcols + value_width :], grad_ffn[:, :, 2].reshape(own, units)],
        axis=1,
    ).astype(f32)

    head_full = lax.dynamic_update_slice_in_dim(
        jnp.zeros((width,), f32), grad_gain_two, me_state * value_width, 0
    )
    gain_sums = lax.psum(
        jnp.concatenate([grad_gain_one, grad_gain_three, grad_gain_four, head_full]), EVERY
    )
    head_slots = (
        jnp.zeros((nd * capacity, block_rows), f32)
        .at[index]
        .set(gain_sums[3 * wide :].reshape(block_count, block_rows))
    )
    gain_slots = gain_sums[: 3 * wide].reshape(3, nd * capacity, block_rows)
    gain_slots = jnp.stack([gain_slots[0], head_slots, gain_slots[1], gain_slots[2]], axis=1)
    own_gain = lax.dynamic_slice_in_dim(gain_slots, me_dp * capacity, capacity)

    squares = jnp.sum(own_in * own_in) + jnp.sum(own_out * own_out) + jnp.sum(own_table * own_table)
    squares = small_gather([jnp.full((8, LANES), squares)], True, 10)[0][:, 0, 0]
    squares_all = jnp.sum(squares) + jnp.sum(gain_sums * gain_sums)
    grad_norm = jnp.sqrt(squares_all)
    scale = jnp.minimum(1.0, CLIP_NORM / (grad_norm + 1e-06))
    occupied = occupied_here.astype(f32)
    wide_occ = occupied[None, :, None, None]
    new_in = adam_update(
        in_weight,
        in_first,
        in_second,
        in_average,
        own_in.reshape(in_weight.shape),
        scale,
        LEARN_RATE,
        WEIGHT_DECAY,
        wide_occ,
    )
    new_out = adam_update(
        out_weight,
        out_first,
        out_second,
        out_average,
        own_out.reshape(out_weight.shape),
        scale,
        LEARN_RATE,
        WEIGHT_DECAY,
        wide_occ,
    )
    new_table = adam_update(
        table_weight,
        table_first,
        table_second,
        table_average,
        own_table.reshape(table_weight.shape),
        scale,
        LEARN_RATE,
        WEIGHT_DECAY,
        wide_occ,
    )
    new_gain = adam_update(
        gain_weight,
        gain_first,
        gain_second,
        gain_average,
        own_gain,
        scale,
        GAIN_RATE,
        0.0,
        occupied[:, None, None],
    )
    return (
        new_in[0],
        new_out[0],
        new_table[0],
        new_gain[0],
        new_in[1],
        new_out[1],
        new_table[1],
        new_gain[1],
        new_in[2],
        new_out[2],
        new_table[2],
        new_gain[2],
        new_in[3],
        new_out[3],
        new_table[3],
        new_gain[3],
        loss_sum,
        count,
        grad_norm,
    )


def solution(mesh):
    return jax.shard_map(
        on_device,
        mesh=mesh,
        in_specs=(
            P("dp", None),
            P("dp", None),
            P("dp", None),
            P("dp", None),
            P(),
            P("state", "dp", None, None),
            P("state", "dp", None, None),
            P("state", "dp", None, None),
            P("dp", None, None),
            P("state", "dp", None, None),
            P("state", "dp", None, None),
            P("state", "dp", None, None),
            P("dp", None, None),
            P("state", "dp", None, None),
            P("state", "dp", None, None),
            P("state", "dp", None, None),
            P("dp", None, None),
            P("state", "dp", None, None),
            P("state", "dp", None, None),
            P("state", "dp", None, None),
            P("dp", None, None),
        ),
        out_specs=(
            P("state", "dp", None, None),
            P("state", "dp", None, None),
            P("state", "dp", None, None),
            P("dp", None, None),
            P("state", "dp", None, None),
            P("state", "dp", None, None),
            P("state", "dp", None, None),
            P("dp", None, None),
            P("state", "dp", None, None),
            P("state", "dp", None, None),
            P("state", "dp", None, None),
            P("dp", None, None),
            P("state", "dp", None, None),
            P("state", "dp", None, None),
            P("state", "dp", None, None),
            P("dp", None, None),
            P(),
            P(),
            P(),
        ),
        check_vma=False,
    )
```

```python
import functools

import jax
import jax.numpy as jnp
from jax import lax
from jax.experimental import pallas as pl
from jax.experimental.pallas import tpu as pltpu
from jax.sharding import PartitionSpec as P

HEADS = 16
KEY_DIM = 128
GROUP = 128
STEP = 5
VAL_DIM = 128


NORM_EPS = 1e-06
LOWER_BOUND = 0.9
CLIP_NORM = 0.02
BETA_FIRST = 0.5
BETA_SECOND = 0.5
ADAM_EPS = 1e-08
LEARN_RATE = 0.02
GAIN_RATE = 0.2
WEIGHT_DECAY = 0.1
AVERAGE_DECAY = 0.9
FULL_PRECISION = lax.Precision.HIGHEST
LANES = 128


def rms_norm(values, gain, width):
    mean = jnp.sum(values * values, axis=-1, keepdims=True) * (1.0 / width)
    return values * lax.rsqrt(mean + NORM_EPS) * gain


def forget_gates(forget_pre):
    key_gate = (1.0 - LOWER_BOUND) * jax.nn.sigmoid(-forget_pre)
    log_forget = jnp.log(LOWER_BOUND + (1.0 - LOWER_BOUND) * jax.nn.sigmoid(forget_pre))
    return key_gate, log_forget


def slot_mixer(query, key_gate, log_forget, values, pick, allowed, heads, key_part):
    slots = query.shape[0]
    tokens = key_gate.shape[0]
    blocks = tokens // GROUP
    order = jnp.arange(GROUP)
    lower = (order[:, None] >= order[None, :]).astype(jnp.float32)
    number = jnp.arange(blocks)
    before = (number[:, None] > number[None, :]).astype(jnp.float32)
    inside = jnp.einsum(
        "ts,bsk->btk", lower, log_forget.reshape(blocks, GROUP, -1), precision=FULL_PRECISION
    )
    total = inside[:, -1]
    offset = jnp.dot(before, total, precision=FULL_PRECISION)
    ends = offset + total
    along = (inside + offset[:, None]).reshape(tokens, -1)
    at_slots = jnp.dot(pick, along, precision=FULL_PRECISION)
    key_decay = key_gate * jnp.exp(total[:, None] - inside).reshape(tokens, -1)
    grown = query[None] * jnp.exp(jnp.minimum(at_slots[None] - ends[:, None], 16.0))
    key_decay = key_decay.reshape(blocks, GROUP, heads * KEY_DIM)
    column = jnp.arange(heads * KEY_DIM)
    of_head = (column % key_part) // (key_part // heads) == jnp.arange(heads)[:, None]
    grown = jnp.where(of_head[:, None, None], grown[None], 0.0)
    scores = jnp.einsum("hbnk,bgk->hnbg", grown, key_decay, precision=FULL_PRECISION)
    scores = jnp.where(allowed[None], scores.reshape(heads, slots, tokens), 0.0)
    mixed = jnp.einsum(
        "hns,shv->nhv", scores, values.reshape(tokens, heads, VAL_DIM), precision=FULL_PRECISION
    )
    return mixed.reshape(slots, -1)


def document_ids(starts, length):
    return jnp.sum((jnp.arange(length)[:, None] >= starts[None, :]).astype(jnp.int32), axis=1) - 1


def slot_index(owners, capacity):
    order = jnp.arange(owners.shape[0])
    earlier = (owners[:, None] == owners[None, :]) & (order[None, :] < order[:, None])
    ranks = jnp.sum(earlier.astype(jnp.int32), axis=1)
    return owners * capacity + ranks


def adam_update(weight, first, second, average, grad, scale, rate, decay, occupied):
    clipped = scale * grad
    first_new = BETA_FIRST * first + (1.0 - BETA_FIRST) * clipped
    second_new = BETA_SECOND * second + (1.0 - BETA_SECOND) * clipped * clipped
    first_hat = first_new / (1.0 - BETA_FIRST**STEP)
    second_hat = second_new / (1.0 - BETA_SECOND**STEP)
    weight_new = weight - rate * (first_hat / (jnp.sqrt(second_hat) + ADAM_EPS) + decay * weight)
    average_new = AVERAGE_DECAY * average + (1.0 - AVERAGE_DECAY) * weight_new
    return (
        weight_new * occupied,
        first_new * occupied,
        second_new * occupied,
        average_new * occupied,
    )


def times_plain(left, right):
    return jnp.dot(left, right, preferred_element_type=jnp.float32)


def times_right(left, right):
    return lax.dot_general(
        left, right, (((1,), (1,)), ((), ())), preferred_element_type=jnp.float32
    )


def times_left(left, right):
    return lax.dot_general(
        left, right, (((0,), (0,)), ((), ())), preferred_element_type=jnp.float32
    )


def swiglu(joined, units, cols):
    gate = joined[:, :units]
    up = joined[:, units : 2 * units]
    return jnp.pad(jax.nn.silu(gate) * up, ((0, 0), (0, cols - units)))


EVERY = ("dp", "state")


def gather_state(values, axis=0):
    return lax.all_gather(values, "state", axis=axis, tiled=True)


def scatter_state(values, axis=0):
    return lax.psum_scatter(values, "state", scatter_dimension=axis, tiled=True)


def swap_dp(values):
    return lax.all_to_all(values, "dp", split_axis=0, concat_axis=0, tiled=True)


def spread_columns(own, parts):
    return own.reshape(own.shape[0], parts, -1).transpose(1, 0, 2)


def join_columns(split):
    return split.transpose(1, 0, 2).reshape(split.shape[1], -1)


MESH = pl.DeviceIdType.MESH


class Links:
    def __init__(self, sends, recvs):
        self.sends, self.recvs, self.used, self.open = sends, recvs, 0, []

    def copy(self, src, dst, dp, state):
        number = self.used
        self.used += 1
        made = pltpu.make_async_remote_copy(
            src_ref=src,
            dst_ref=dst,
            send_sem=self.sends.at[number],
            recv_sem=self.recvs.at[number],
            device_id=(dp, state),
            device_id_type=MESH,
        )
        made.start()
        self.open.append(made)
        return made

    def settle(self, copies):
        for made in copies:
            made.wait_send()
        self.open = [made for made in self.open if not any(made is one for one in copies)]

    def finish(self):
        for made in self.open:
            made.wait_send()


def greet(peers):
    barrier = pltpu.get_barrier_semaphore()
    for dp, state in peers:
        pl.semaphore_signal(barrier, inc=1, device_id=(dp, state), device_id_type=MESH)
    pl.semaphore_wait(barrier, len(peers))


def places(nd, ns):
    dp, st = lax.axis_index("dp"), lax.axis_index("state")
    return dp, st, lax.div(dp, 2), lax.rem(dp, 2), lax.div(st, 2), lax.rem(st, 2)


def near_peers(nd, ns):
    dp, st, z, y, x, c = places(nd, ns)
    deep, across = nd // 2, ns // 2
    peers = [(lax.rem(z + k, deep) * 2 + y, st) for k in range(1, deep)]
    peers.append((dp + 1 - 2 * y, st))
    peers += [(dp, lax.rem(x + k, across) * 2 + c) for k in range(1, across)]
    peers.append((dp, st + 1 - 2 * c))
    return peers


def small_gather_kernel(nd, ns, everyone, count, *refs):
    sources, outs, (sends, recvs) = refs[:count], refs[count : 2 * count], refs[2 * count :]
    dp, st = lax.axis_index("dp"), lax.axis_index("state")
    peers = []
    for a in range(nd):
        for b in range(ns if everyone else 1):
            if a or b:
                peers.append((lax.rem(dp + a, nd), lax.rem(st + b, ns)))
    greet(peers)
    me = dp * ns + st if everyone else dp
    links = Links(sends, recvs)
    for source, out in zip(sources, outs):
        out[me] = source[...]
        for there, far in peers:
            links.copy(source, out.at[me], there, far)
    for made in links.open:
        made.wait_recv()
    links.finish()


def small_gather(arrays, everyone, number):
    nd, ns = lax.axis_size("dp"), lax.axis_size("state")
    members = nd * ns if everyone else nd
    copies = (members - 1) * len(arrays)
    vmem = pl.BlockSpec(memory_space=pltpu.VMEM)
    return pl.pallas_call(
        functools.partial(small_gather_kernel, nd, ns, everyone, len(arrays)),
        out_shape=[jax.ShapeDtypeStruct((members,) + a.shape, a.dtype) for a in arrays],
        in_specs=[vmem] * len(arrays),
        out_specs=[vmem] * len(arrays),
        scratch_shapes=[pltpu.SemaphoreType.DMA((copies,)), pltpu.SemaphoreType.DMA((copies,))],
        compiler_params=pltpu.CompilerParams(collective_id=number, has_side_effects=True),
    )(*arrays)


def gather_all_kernel(nd, ns, in_ref, out_ref, sends, recvs):
    greet(near_peers(nd, ns))
    links = Links(sends, recvs)
    gather_body(nd, ns, links, in_ref, out_ref)
    links.finish()


def gather_body(nd, ns, links, in_ref, out_ref):
    dp, st, z, y, x, c = places(nd, ns)
    deep, across = nd // 2, ns // 2
    half = in_ref.shape[1] // 2
    cols = (pl.ds(0, half), pl.ds(half, half))
    to_y = (dp + 1 - 2 * y, st)
    to_core = (dp, st + 1 - 2 * c)
    other_y = 1 - y

    def x_at(k):
        return lax.rem(x + k, across)

    def to_x(k):
        return (dp, x_at(k) * 2 + c)

    def group(xx, yy, part):
        return out_ref.at[c, xx, yy, :, :, cols[part]]

    def send(xx, yy, part, place):
        return links.copy(group(xx, yy, part), group(xx, yy, part), *place)

    out_ref[c, x, y, z] = in_ref[...]
    first = []
    for part in range(2):
        for k in range(1, deep):
            there = (lax.rem(z + k, deep) * 2 + y, st)
            first.append(
                links.copy(
                    in_ref.at[:, cols[part]], out_ref.at[c, x, y, z, :, cols[part]], *there
                )
            )
    for made in first[: deep - 1]:
        made.wait_recv()
    a_y = send(x, y, 0, to_y)
    for made in first[deep - 1 :]:
        made.wait_recv()
    b_x = [send(x, y, 1, to_x(k)) for k in range(1, across)]
    a_x = [send(x, y, 0, to_x(k)) for k in range(1, across)]
    b_y = send(x, y, 1, to_y)
    arriving = [send(x, y, 0, to_core), send(x, y, 1, to_core)]
    a_y.wait_recv()
    a_xy = [send(x, other_y, 0, to_x(k)) for k in range(1, across)]
    arriving.append(send(x, other_y, 0, to_core))
    b_xy = []
    for k in range(1, across):
        b_x[k - 1].wait_recv()
        from_x = lax.rem(x - k + across, across)
        b_xy.append(send(from_x, y, 1, to_y))
        arriving.append(send(from_x, y, 1, to_core))
    for k in range(1, across):
        a_x[k - 1].wait_recv()
        arriving.append(send(lax.rem(x - k + across, across), y, 0, to_core))
    b_y.wait_recv()
    arriving.append(send(x, other_y, 1, to_core))
    for k in range(1, across):
        from_x = lax.rem(x - k + across, across)
        a_xy[k - 1].wait_recv()
        arriving.append(send(from_x, other_y, 0, to_core))
        b_xy[k - 1].wait_recv()
        arriving.append(send(from_x, other_y, 1, to_core))
    for made in arriving:
        made.wait_recv()
    links.settle(first + [a_y, b_y] + b_x + a_x + a_xy + b_xy + arriving)


def gather_copies(nd, ns):
    deep, across = nd // 2, ns // 2
    return 2 * (deep - 1) + 2 + 4 * (across - 1) + 4 * across


def gather_all(values, number):
    nd, ns = lax.axis_size("dp"), lax.axis_size("state")
    rows, wide = values.shape
    deep, across = nd // 2, ns // 2
    copies = gather_copies(nd, ns)
    vmem = pl.BlockSpec(memory_space=pltpu.VMEM)
    out = pl.pallas_call(
        functools.partial(gather_all_kernel, nd, ns),
        out_shape=jax.ShapeDtypeStruct((2, across, 2, deep, rows, wide), values.dtype),
        in_specs=[vmem],
        out_specs=vmem,
        scratch_shapes=[pltpu.SemaphoreType.DMA((copies,)), pltpu.SemaphoreType.DMA((copies,))],
        compiler_params=pltpu.CompilerParams(
            collective_id=number, has_side_effects=True, vmem_limit_bytes=40 * 2**20
        ),
    )(values)
    return out.reshape(nd * ns * rows, wide)


def scatter_all_kernel(nd, ns, in_ref, out_ref, *scratch):
    sends, recvs = scratch[-2:]
    greet(near_peers(nd, ns))
    links = Links(sends, recvs)
    scatter_body(nd, ns, links, in_ref, out_ref, scratch[:-2])
    links.finish()


def scatter_body(nd, ns, links, in_ref, out_ref, scratch, meanwhile=None):
    rc, acc, rx_a, ry_a, rz_a, ry_b, rx_b, rz_b = scratch
    dp, st, z, y, x, c = places(nd, ns)
    deep, across = nd // 2, ns // 2
    half = in_ref.shape[5] // 2
    cols = (pl.ds(0, half), pl.ds(half, half))
    to_y = (dp + 1 - 2 * y, st)
    to_core = (dp, st + 1 - 2 * c)
    ys = (y, 1 - y)

    def x_at(k):
        return lax.rem(x + k, across)

    def to_x(k):
        return (dp, x_at(k) * 2 + c)

    core = {}
    order = [(k, ky, 0) for k in range(1, across) for ky in (1, 0)]
    order += [(k, 1, 1) for k in range(across)]
    order += [(0, 1, 0)] + [(k, 0, 1) for k in range(1, across)] + [(0, 0, 0), (0, 0, 1)]
    for k, ky, part in order:
        core[k, ky, part] = links.copy(
            in_ref.at[1 - c, x_at(k), ys[ky], :, :, cols[part]],
            rc.at[x_at(k), ys[ky], :, :, cols[part]],
            *to_core,
        )

    def total(k, ky, part, zz, others):
        found = in_ref[c, x_at(k), ys[ky], zz, :, cols[part]].astype(jnp.float32)
        found += rc[x_at(k), ys[ky], zz, :, cols[part]].astype(jnp.float32)
        for other in others:
            found += other[zz].astype(jnp.float32)
        return found

    def add(k, ky, part, others):
        core[k, ky, part].wait_recv()

        @pl.loop(0, deep)
        def _(zz):
            acc[x_at(k), ys[ky], zz, :, cols[part]] = total(k, ky, part, zz, others).astype(
                acc.dtype
            )

        return acc.at[x_at(k), ys[ky], :, :, cols[part]]

    if meanwhile is not None:
        meanwhile()
    a_x, b_y = {}, {}
    for k in range(1, across):
        for ky in (1, 0):
            a_x[k, ky] = links.copy(add(k, ky, 0, []), rx_a.at[k - 1, ky], *to_x(k))
    for k in range(across):
        b_y[k] = links.copy(add(k, 1, 1, []), ry_b.at[k], *to_y)
    for k in range(1, across):
        a_x[k, 1].wait_recv()
    a_y = links.copy(
        add(0, 1, 0, [rx_a.at[k - 1, 1] for k in range(1, across)]), ry_a, *to_y
    )
    b_x = {}
    for k in range(1, across):
        b_y[k].wait_recv()
        b_x[k] = links.copy(add(k, 0, 1, [ry_b.at[k]]), rx_b.at[k - 1], *to_x(k))
    for k in range(1, across):
        a_x[k, 0].wait_recv()
    a_y.wait_recv()
    left = [rx_a.at[k - 1, 0] for k in range(1, across)] + [ry_a]
    add(0, 0, 0, left)

    def send_z(part, land):
        return [
            links.copy(
                acc.at[x, y, lax.rem(z + k, deep), :, cols[part]],
                land.at[k - 1],
                lax.rem(z + k, deep) * 2 + y,
                st,
            )
            for k in range(1, deep)
        ]

    a_z = send_z(0, rz_a)
    b_y[0].wait_recv()
    for k in range(1, across):
        b_x[k].wait_recv()
    right = [ry_b.at[0]] + [rx_b.at[k - 1] for k in range(1, across)]
    add(0, 0, 1, right)
    b_z = send_z(1, rz_b)
    for part, made, others, land in ((0, a_z, left, rz_a), (1, b_z, right, rz_b)):
        found = total(0, 0, part, z, others)
        for k in range(1, deep):
            made[k - 1].wait_recv()
            found += land[k - 1].astype(jnp.float32)
        out_ref[:, cols[part]] = found
    links.settle(
        list(core.values()) + list(a_x.values()) + list(b_y.values()) + list(b_x.values())
        + [a_y] + a_z + b_z
    )


def scatter_copies(nd, ns):
    deep, across = nd // 2, ns // 2
    return 4 * across + 2 * (across - 1) + across + 1 + (across - 1) + 2 * (deep - 1)


def scatter_scratch(nd, ns, rows, wide, kind):
    deep, across = nd // 2, ns // 2
    half = wide // 2
    return [
        pltpu.VMEM((across, 2, deep, rows, wide), kind),
        pltpu.VMEM((across, 2, deep, rows, wide), kind),
        pltpu.VMEM((across - 1, 2, deep, rows, half), kind),
        pltpu.VMEM((deep, rows, half), kind),
        pltpu.VMEM((deep - 1, rows, half), kind),
        pltpu.VMEM((across, deep, rows, half), kind),
        pltpu.VMEM((across - 1, deep, rows, half), kind),
        pltpu.VMEM((deep - 1, rows, half), kind),
    ]


def scatter_all(values, number):
    nd, ns = lax.axis_size("dp"), lax.axis_size("state")
    deep, across = nd // 2, ns // 2
    rows, wide = values.shape[0] // (nd * ns), values.shape[1]
    copies = scatter_copies(nd, ns)
    vmem = pl.BlockSpec(memory_space=pltpu.VMEM)
    kind = values.dtype
    return pl.pallas_call(
        functools.partial(scatter_all_kernel, nd, ns),
        out_shape=jax.ShapeDtypeStruct((rows, wide), jnp.float32),
        in_specs=[vmem],
        out_specs=vmem,
        scratch_shapes=scatter_scratch(nd, ns, rows, wide, kind)
        + [pltpu.SemaphoreType.DMA((copies,)), pltpu.SemaphoreType.DMA((copies,))],
        compiler_params=pltpu.CompilerParams(
            collective_id=number, has_side_effects=True, vmem_limit_bytes=40 * 2**20
        ),
    )(values.reshape(2, across, 2, deep, rows, wide))


def front_kernel(
    nd,
    ns,
    depth_used,
    small_ref,
    gain_ref,
    table_ref,
    keys_ref,
    rest_ref,
    parts_ref,
    small_out,
    gain_out,
    rows_out,
    keys_out,
    rest_out,
    parts_out,
    looked,
    rc,
    acc,
    rx,
    fin,
    sums,
    sends,
    recvs,
    local,
):
    dp, st, z, y, x, c = places(nd, ns)
    deep, across = nd // 2, ns // 2
    own = table_ref.shape[0]
    tokens = rows_out.shape[1]
    part = tokens // ns
    to_core = (dp, st + 1 - 2 * c)
    to_y = (dp + 1 - 2 * y, st)
    other_y = dp + 1 - 2 * y
    dp_peers = [(lax.rem(dp + k, nd), st) for k in range(1, nd)]
    state_peers = [(dp, lax.rem(st + k, ns)) for k in range(1, ns)]
    greet(dp_peers + state_peers)
    links = Links(sends, recvs)

    ids_made = {}
    small_out[dp] = small_ref[...]
    gain_out[dp] = gain_ref[...]
    for k in range(1, nd):
        ids_made[k] = links.copy(small_ref, small_out.at[dp], *dp_peers[k - 1])
    gain_made = [links.copy(gain_ref, gain_out.at[dp], *peer) for peer in dp_peers]

    here = [
        pltpu.make_async_copy(keys_ref.at[st], keys_out.at[st, dp], local.at[0]),
        pltpu.make_async_copy(rest_ref, rest_out.at[dp], local.at[1]),
        pltpu.make_async_copy(parts_ref.at[dp], parts_out.at[dp], local.at[2]),
    ]
    for made in here:
        made.start()
    key_made = [
        links.copy(keys_ref.at[peer[1]], keys_out.at[st, dp], *peer) for peer in state_peers
    ]

    class Gather:
        def __init__(self, view):
            self.view = view
            self.base = links.used
            links.used += 2 * (deep - 1) + 1 + 2 * (deep - 1)

        def copy(self, number, owner, place):
            return pltpu.make_async_remote_copy(
                src_ref=self.view(owner),
                dst_ref=self.view(owner),
                send_sem=sends.at[self.base + number],
                recv_sem=recvs.at[self.base + number],
                device_id=place,
                device_id_type=MESH,
            )

        def pass_on(self, way, step):
            behind = z - way * step
            ahead = z + way
            number = step if way > 0 else deep - 1 + step

            def go(made):
                @pl.when((behind >= 0) & (behind < deep) & (ahead >= 0) & (ahead < deep))
                def _():
                    made(self.copy(number, behind * 2 + y, (ahead * 2 + y, st)))

            return go

        def begin(self):
            self.copy(2 * (deep - 1), dp, to_y).start()
            for way in (1, -1):
                self.pass_on(way, 0)(lambda made: made.start())

        def arrive(self, way, step):
            began = z - way * (step + 1)
            number = step if way > 0 else deep - 1 + step

            @pl.when((began >= 0) & (began < deep))
            def _():
                self.copy(number, began * 2 + y, to_y).wait_recv()
                self.copy(2 * (deep - 1) + 1 + number, began * 2 + y, to_y).start()

            if step + 1 < deep - 1:
                self.pass_on(way, step + 1)(lambda made: made.start())

        def finish(self):
            self.copy(2 * (deep - 1), other_y, to_y).wait_recv()
            self.copy(2 * (deep - 1), dp, to_y).wait_send()
            for way in (1, -1):
                for step in range(deep - 1):
                    began = z - way * (step + 1)
                    number = step if way > 0 else deep - 1 + step
                    self.pass_on(way, step)(lambda made: made.wait_send())

                    @pl.when((began >= 0) & (began < deep))
                    def _():
                        made = self.copy(2 * (deep - 1) + 1 + number, began * 2 + y, to_y)
                        made.wait_send()
                        made.wait_recv()

    rest = Gather(lambda owner: rest_out.at[owner])
    keys = Gather(lambda owner: keys_out.at[:, owner])
    here[1].wait()
    rest.begin()

    def swap(k):
        there = lax.rem(dp + k, nd)
        return links.copy(parts_ref.at[there], parts_out.at[dp], there, st)

    swapped = [swap(k) for k in range(1, nd // 2)]
    here[0].wait()
    for made in key_made:
        made.wait_recv()
    keys.begin()

    def x_at(k):
        return lax.rem(x + k, across)

    def row_at(k):
        return lax.rem(dp + k, nd)

    def block(k, kx, cc):
        start = (x_at(kx) * 2 + cc) * part
        return looked.at[k, :, pl.ds(pl.multiple_of(start, part), part)]

    def place(owner, share):
        return rows_out.at[
            pl.ds(pl.multiple_of(owner * own, own), own),
            pl.ds(pl.multiple_of(share * part, part), part),
        ]

    def add(sources, target):
        @pl.loop(0, own // 32)
        def _(i):
            rows = pl.ds(pl.multiple_of(i * 32, 32), 32)
            found = sources[0][rows, :].astype(jnp.float32)
            for source in sources[1:]:
                found += source[rows, :].astype(jnp.float32)
            target[rows, :] = found.astype(target.dtype)

    depth = table_ref.shape[1]
    piece = min(1024, depth)
    span = 2 * LANES

    def look(k):
        row = row_at(k)

        @pl.loop(0, tokens // span)
        def _(i):
            ids = jnp.concatenate(
                [small_out[row, pl.ds(2 * i, 1), :], small_out[row, pl.ds(2 * i + 1, 1), :]],
                axis=1,
            )
            ids = ids - st * depth_used
            sums[...] = jnp.zeros_like(sums)

            @pl.loop(0, depth // piece)
            def _(j):
                number = lax.broadcasted_iota(jnp.int32, (piece, span), 0)
                hit = jnp.where(number == ids - j * piece, 1.0, 0.0).astype(jnp.bfloat16)
                cols = pl.ds(pl.multiple_of(j * piece, piece), piece)
                sums[...] += jnp.dot(
                    table_ref[:, cols], hit, preferred_element_type=jnp.float32
                )

            cols = pl.ds(pl.multiple_of(i * span, span), span)
            looked[k, :, cols] = sums[...].astype(looked.dtype)

    turn = list(range(1, nd)) + [0]
    core, across_x, across_dp = {}, {}, {}

    def start_core(k):
        for kx in list(range(1, across)) + [0]:
            core[k, kx] = links.copy(block(k, kx, 1 - c), rc.at[k, kx], *to_core)

    def start_x(k):
        for kx in range(1, across):
            core[k, kx].wait_recv()
            add([block(k, kx, c), rc.at[k, kx]], acc.at[k, kx - 1])
            across_x[k, kx] = links.copy(
                acc.at[k, kx - 1], rx.at[k, kx - 1], dp, x_at(kx) * 2 + c
            )

    def start_dp(k):
        core[k, 0].wait_recv()
        sources = [block(k, 0, c), rc.at[k, 0]]
        for kx in range(1, across):
            across_x[k, kx].wait_recv()
            sources.append(rx.at[k, kx - 1])
        if k:
            add(sources, fin.at[k - 1])
            across_dp[k] = links.copy(fin.at[k - 1], place(dp, st), row_at(k), st)
        else:
            add(sources, place(dp, st))

    chores = []
    for step in range(deep - 1):
        for way in (1, -1):
            chores.append(functools.partial(rest.arrive, way, step))
    for step in range(deep - 1):
        for way in (1, -1):
            chores.append(functools.partial(keys.arrive, way, step))
    each = -(-len(chores) // nd)
    for number, k in enumerate(turn):
        if k:
            ids_made[nd - k].wait_recv()
        look(k)
        start_core(k)
        if number >= 1:
            start_x(turn[number - 1])
        if number >= 2:
            start_dp(turn[number - 2])
        for _ in range(each):
            if number >= 2 and chores:
                chores.pop(0)()
    start_x(turn[-1])
    start_dp(turn[-2])
    start_dp(turn[-1])
    swapped += [swap(k) for k in range(nd // 2, nd)]
    later, last = {}, []
    for number, k in enumerate([0] + list(range(1, nd))):
        owner = lax.rem(dp - k + nd, nd)
        if k:
            across_dp[k].wait_recv()
        for kx in range(1, across):
            later[k, kx] = links.copy(
                place(owner, st), place(owner, st), dp, x_at(kx) * 2 + c
            )
        last.append(links.copy(place(owner, st), place(owner, st), *to_core))
        if chores:
            chores.pop(0)()
    for k in range(nd):
        owner = lax.rem(dp - k + nd, nd)
        for kx in range(1, across):
            later[k, kx].wait_recv()
            share = lax.rem(x - kx + across, across) * 2 + c
            last.append(links.copy(place(owner, share), place(owner, share), *to_core))
    while chores:
        chores.pop(0)()
    for made in last + swapped + gain_made:
        made.wait_recv()
    here[2].wait()
    links.finish()
    rest.finish()
    keys.finish()


def front(small, gain, table, keys, rest, parts, tokens, vocab, number):
    nd, ns = lax.axis_size("dp"), lax.axis_size("state")
    deep, across = nd // 2, ns // 2
    own = table.shape[0]
    part = tokens // ns
    kind = table.dtype
    copies = 2 * (nd - 1) + ns - 1 + 2 * (4 * (deep - 1) + 1) + nd - 1
    copies += nd * across + nd * (across - 1) + nd - 1 + nd * across + nd * (across - 1)
    vmem = pl.BlockSpec(memory_space=pltpu.VMEM)
    hbm = pl.BlockSpec(memory_space=pl.ANY)
    return pl.pallas_call(
        functools.partial(front_kernel, nd, ns, vocab),
        out_shape=[
            jax.ShapeDtypeStruct((nd,) + small.shape, small.dtype),
            jax.ShapeDtypeStruct((nd,) + gain.shape, gain.dtype),
            jax.ShapeDtypeStruct((nd * own, tokens), kind),
            jax.ShapeDtypeStruct((ns, nd) + keys.shape[1:], kind),
            jax.ShapeDtypeStruct((nd,) + rest.shape, kind),
            jax.ShapeDtypeStruct(parts.shape, kind),
        ],
        in_specs=[vmem, vmem, vmem, hbm, hbm, hbm],
        out_specs=[vmem, vmem, vmem, hbm, hbm, hbm],
        scratch_shapes=[
            pltpu.VMEM((nd, own, tokens), kind),
            pltpu.VMEM((nd, across, own, part), kind),
            pltpu.VMEM((nd, across - 1, own, part), kind),
            pltpu.VMEM((nd, across - 1, own, part), kind),
            pltpu.VMEM((nd - 1, own, part), kind),
            pltpu.VMEM((own, 2 * LANES), jnp.float32),
            pltpu.SemaphoreType.DMA((copies,)),
            pltpu.SemaphoreType.DMA((copies,)),
            pltpu.SemaphoreType.DMA((3,)),
        ],
        compiler_params=pltpu.CompilerParams(
            collective_id=number, has_side_effects=True, vmem_limit_bytes=52 * 2**20
        ),
        cost_estimate=pl.CostEstimate(
            flops=2 * table.size * nd * tokens, bytes_accessed=4 * parts.size, transcendentals=0
        ),
    )(small, gain, table, keys, rest, parts)


def slots_back_kernel(
    nd,
    ns,
    width,
    units,
    part_hbm,
    table_ref,
    two_ref,
    one_ref,
    gain_ref,
    wd_ref,
    wgu_ref,
    gu_ref,
    hidden_ref,
    rows_ref,
    one_out,
    table_out,
    ffn_out,
    gains_out,
    part_ref,
    summed,
    low,
    down,
    dgu,
    dffn,
    local,
    *scratch,
):
    sends, recvs = scratch[-2:]
    dp, st, z, y, x, c = places(nd, ns)
    deep, across = nd // 2, ns // 2
    count, wide = two_ref.shape
    every = nd * ns * count
    dp_peers = [(lax.rem(dp + k, nd), st) for k in range(1, nd)]
    state_peers = [(dp, lax.rem(st + k, ns)) for k in range(1, ns)]
    fill = pltpu.make_async_copy(part_hbm, part_ref, local.at[2])
    fill.start()
    greet(dp_peers + state_peers)
    links = Links(sends, recvs)
    own_copy = pltpu.make_async_copy(table_ref.at[dp], table_out.at[dp], local.at[0])
    own_copy.start()
    local_copies = [own_copy]
    swapped = [
        links.copy(table_ref.at[peer[0]], table_out.at[dp], *peer) for peer in dp_peers
    ]

    def norm_back(grad, values, gain, row):
        mean = jnp.sum(values * values, axis=1, keepdims=True) * (1.0 / width)
        root = lax.rsqrt(mean + NORM_EPS)
        scaled = grad * gain
        inner = jnp.sum(scaled * values, axis=1, keepdims=True) * (1.0 / width)
        gains_out[pl.ds(row, 1), :] = jnp.sum(grad * values * root, axis=0, keepdims=True)
        return scaled * root - values * (root * root * root * inner)

    fill.wait()
    scatter_body(nd, ns, links, part_ref, summed, scratch[:-2])
    summed[...] = norm_back(summed[...], two_ref[...], gain_ref[pl.ds(1, 1), :], 1)
    low[...] = summed[...].astype(low.dtype)
    gather_body(nd, ns, links, low, down)

    inner_cols = gu_ref.shape[1]
    step = deep * count
    flat_down = down

    @pl.loop(0, 2 * across * 2)
    def _(i):
        cc, rest = lax.div(i, 2 * across), lax.rem(i, 2 * across)
        xx, yy = lax.div(rest, 2), lax.rem(rest, 2)
        rows = pl.ds(pl.multiple_of(i * step, step), step)
        grad = jnp.dot(
            flat_down[cc, xx, yy].reshape(step, wide),
            wd_ref[...],
            preferred_element_type=jnp.float32,
        )
        grad = jnp.concatenate(
            [grad, jnp.zeros((step, inner_cols - grad.shape[1]), jnp.float32)], axis=1
        ) if inner_cols > grad.shape[1] else grad[:, :inner_cols]
        gate = gu_ref[rows, :]
        up = pltpu.roll(gate, inner_cols - units, 1)
        gated = 1.0 / (1.0 + jnp.exp(-gate))
        grad_gate = grad * up * (gated * (1.0 + gate * (1.0 - gated)))
        grad_up = pltpu.roll(grad * gate * gated, units, 1)
        lanes = lax.broadcasted_iota(jnp.int32, grad_gate.shape, 1)
        joined = jnp.where(lanes < units, grad_gate, grad_up).astype(dgu.dtype)
        dgu[rows, :] = joined
        part_ref[cc, xx, yy] = (
            lax.dot_general(
                joined, wgu_ref[...], (((1,), (1,)), ((), ())), preferred_element_type=jnp.float32
            )
            .astype(part_ref.dtype)
            .reshape(deep, count, wide)
        )

    def weight_grads():
        span = 2 * LANES

        @pl.loop(0, wide // span)
        def _(i):
            cols = pl.ds(pl.multiple_of(i * span, span), span)
            dffn[cols, :inner_cols] = lax.dot_general(
                rows_ref[:, cols], dgu[...], (((0,), (0,)), ((), ())),
                preferred_element_type=jnp.float32,
            ).astype(dffn.dtype)
            dffn[cols, inner_cols:] = lax.dot_general(
                flat_down[:, :, :, :, :, cols].reshape(every, span), hidden_ref[...],
                (((0,), (0,)), ((), ())),
                preferred_element_type=jnp.float32,
            ).astype(dffn.dtype)

        own = ffn_out.shape[1]

        def block(owner):
            return dffn.at[pl.ds(pl.multiple_of(owner * own, own), own), :]

        mine = pltpu.make_async_copy(block(dp), ffn_out.at[dp], local.at[1])
        mine.start()
        swapped.extend(links.copy(block(peer[0]), ffn_out.at[dp], *peer) for peer in dp_peers)
        local_copies.append(mine)

    grad_two = summed[...]
    scatter_body(nd, ns, links, part_ref, summed, scratch[:-2], weight_grads)
    grad_one = grad_two + norm_back(summed[...], one_ref[...], gain_ref[pl.ds(0, 1), :], 0)
    one_out[st] = grad_one.astype(one_out.dtype)
    low[...] = grad_one.astype(low.dtype)
    made = [links.copy(low, one_out.at[st], *peer) for peer in state_peers]
    for copy in made:
        copy.wait_recv()
    for copy in swapped:
        copy.wait_recv()
    for copy in local_copies:
        copy.wait()
    links.finish()


def slots_back(part, table, two, one, gain, wd, wgu, gu, hidden, rows, width, units, number):
    nd, ns = lax.axis_size("dp"), lax.axis_size("state")
    deep, across = nd // 2, ns // 2
    count, wide = two.shape
    kind = part.dtype
    own = wide // nd
    cols = wgu.shape[1] + wd.shape[1]
    copies = 2 * scatter_copies(nd, ns) + gather_copies(nd, ns) + 2 * (nd - 1) + ns - 1
    vmem = pl.BlockSpec(memory_space=pltpu.VMEM)
    hbm = pl.BlockSpec(memory_space=pl.ANY)
    six = (2, across, 2, deep, count, wide)
    out = pl.pallas_call(
        functools.partial(slots_back_kernel, nd, ns, width, units),
        out_shape=[
            jax.ShapeDtypeStruct((ns, count, wide), kind),
            jax.ShapeDtypeStruct(table.shape, kind),
            jax.ShapeDtypeStruct((nd, own, cols), kind),
            jax.ShapeDtypeStruct((2, wide), jnp.float32),
        ],
        in_specs=[hbm, hbm] + [vmem] * 8,
        out_specs=[vmem, hbm, hbm, vmem],
        scratch_shapes=[
            pltpu.VMEM(six, kind),
            pltpu.VMEM((count, wide), jnp.float32),
            pltpu.VMEM((count, wide), kind),
            pltpu.VMEM(six, kind),
            pltpu.VMEM((nd * ns * count, wgu.shape[1]), kind),
            pltpu.VMEM((wide, cols), kind),
            pltpu.SemaphoreType.DMA((3,)),
        ]
        + scatter_scratch(nd, ns, count, wide, kind)
        + [pltpu.SemaphoreType.DMA((copies,)), pltpu.SemaphoreType.DMA((copies,))],
        compiler_params=pltpu.CompilerParams(
            collective_id=number, has_side_effects=True, vmem_limit_bytes=58 * 2**20
        ),
        cost_estimate=pl.CostEstimate(
            flops=8 * rows.size * cols, bytes_accessed=100 * part.size, transcendentals=0
        ),
    )(part.reshape(six), table, two, one, gain, wd, wgu, gu, hidden, rows)
    return (out[0].reshape(ns * count, wide),) + tuple(out[1:])


def state_sum_kernel(nd, ns, in_ref, out_ref, land, sends, recvs):
    dp, st = lax.axis_index("dp"), lax.axis_index("state")
    peers = [(dp, lax.rem(st + k, ns)) for k in range(1, ns)]
    greet(peers)
    links = Links(sends, recvs)
    made = [
        links.copy(in_ref.at[there[1]], land.at[k], *there) for k, there in enumerate(peers)
    ]
    found = in_ref[st].astype(jnp.float32)
    for k in range(ns - 1):
        made[k].wait_recv()
        found += land[k].astype(jnp.float32)
    out_ref[...] = found
    links.finish()


def state_sum(values, number):
    nd, ns = lax.axis_size("dp"), lax.axis_size("state")
    rows, wide = values.shape[0] // ns, values.shape[1]
    vmem = pl.BlockSpec(memory_space=pltpu.VMEM)
    return pl.pallas_call(
        functools.partial(state_sum_kernel, nd, ns),
        out_shape=jax.ShapeDtypeStruct((rows, wide), jnp.float32),
        in_specs=[vmem],
        out_specs=vmem,
        scratch_shapes=[
            pltpu.VMEM((ns - 1, rows, wide), values.dtype),
            pltpu.SemaphoreType.DMA((ns - 1,)),
            pltpu.SemaphoreType.DMA((ns - 1,)),
        ],
        compiler_params=pltpu.CompilerParams(collective_id=number, has_side_effects=True),
    )(values.reshape(ns, rows, wide))


def on_device(
    token_ids,
    doc_starts,
    loss_positions,
    loss_targets,
    owners,
    in_weight,
    out_weight,
    table_weight,
    gain_weight,
    in_first,
    out_first,
    table_first,
    gain_first,
    in_second,
    out_second,
    table_second,
    gain_second,
    in_average,
    out_average,
    table_average,
    gain_average,
):
    f32 = jnp.float32
    bf16 = jnp.bfloat16
    nd = lax.axis_size("dp")
    ns = lax.axis_size("state")
    me_dp = lax.axis_index("dp")
    me_state = lax.axis_index("state")
    tokens = token_ids.shape[1]
    slots = loss_positions.shape[1]
    capacity = in_weight.shape[1]
    block_rows = in_weight.shape[2]
    block_count = owners.shape[0]
    width = block_rows * block_count
    own = capacity * block_rows
    wide = nd * own
    key_share = KEY_DIM // ns
    heads = HEADS // ns
    key_cols = HEADS * key_share
    value_width = heads * VAL_DIM
    mixer_cols = 2 * key_cols + value_width
    units = out_weight.shape[3] - value_width
    unit_part = units // nd
    vocab_share = table_weight.shape[3]
    vocab_part = -(-vocab_share // (nd * LANES)) * LANES
    quarter = tokens // ns
    slot_part = slots // ns

    held_all = jnp.sum((owners[None, :] == jnp.arange(nd)[:, None]).astype(jnp.int32), axis=1)
    occupied_all = jnp.arange(capacity)[None, :] < held_all[:, None]
    held = jnp.sum((owners == me_dp).astype(jnp.int32))
    occupied_here = jnp.arange(capacity) < held
    rows_here = jnp.repeat(occupied_here, block_rows)[:, None]

    def lowered(array):
        return jnp.where(rows_here, array[0].reshape(own, -1), 0.0).astype(bf16)

    in_own = lowered(in_weight)
    out_own = lowered(out_weight)
    table_own = lowered(table_weight)

    def in_rows(flat):
        flat = jnp.pad(flat, (0, -flat.shape[0] % (16 * LANES)))
        return flat.reshape(-1, LANES)

    key_part = heads * key_share
    keys_sent = in_own[:, : 2 * key_cols].reshape(own, 2, ns, key_part)
    keys_sent = keys_sent.transpose(2, 0, 1, 3).reshape(ns, own, 2 * key_part)
    rest_sent = jnp.concatenate(
        [in_own[:, 2 * key_cols : mixer_cols], out_own[:, :value_width]], axis=1
    )
    table_padded = jnp.pad(table_own, ((0, 0), (0, nd * vocab_part - vocab_share)))

    def by_part(columns, parts):
        return columns.reshape(own, nd, parts)

    def zeros(parts):
        return jnp.zeros((own, nd, parts), bf16)

    gu_cols = -(-2 * unit_part // LANES) * LANES
    down_cols = -(-unit_part // LANES) * LANES
    parts_sent = jnp.concatenate(
        [
            by_part(table_padded, vocab_part),
            by_part(in_own[:, mixer_cols : mixer_cols + units], unit_part),
            by_part(in_own[:, mixer_cols + units :], unit_part),
            zeros(gu_cols - 2 * unit_part),
            by_part(out_own[:, value_width:], unit_part),
            zeros(down_cols - unit_part),
        ],
        axis=2,
    ).transpose(1, 0, 2)
    small, gains_all, stream, keys_all, rest_all, parts_all = front(
        in_rows(jnp.concatenate([token_ids[0], loss_targets[0]])),
        in_rows(gain_weight.astype(bf16).reshape(-1)),
        table_padded,
        keys_sent,
        rest_sent,
        parts_sent,
        tokens,
        vocab_share,
        1,
    )
    small = small.reshape(nd, -1)
    ids_all = small[:, :tokens]
    slot_targets = small[:, tokens : tokens + slots].reshape(nd // 2, 2, ns // 2, 2, slot_part)
    targets_all = slot_targets.transpose(3, 2, 1, 0, 4).reshape(-1)
    gains_all = gains_all.reshape(nd, -1)[:, : capacity * 4 * block_rows].astype(f32)
    gains_all = gains_all.reshape(nd * capacity, 4, block_rows)
    gains = jnp.where(occupied_all.reshape(-1)[:, None, None], gains_all, 0.0)
    gains = gains.transpose(1, 0, 2).reshape(4, wide)
    index = slot_index(owners, capacity)
    head_gain = lax.dynamic_slice_in_dim(
        gains_all[index][:, 1].reshape(width), me_state * value_width, value_width
    )
    live = (targets_all >= 0).astype(f32)
    count = jnp.sum(live)
    local_ids = ids_all.reshape(-1) - me_state * vocab_share
    hit = jnp.arange(vocab_share)[:, None] == local_ids[None, :]
    stream_mine = lax.dynamic_slice_in_dim(stream, me_state * quarter, quarter, axis=1)

    qcols = heads * KEY_DIM
    keys_all = keys_all.reshape(ns, wide, 2 * key_part)
    w_q = keys_all[:, :, :key_part].transpose(1, 0, 2).reshape(wide, qcols)
    w_f = keys_all[:, :, key_part:].transpose(1, 0, 2).reshape(wide, qcols)
    rest_all = rest_all.reshape(wide, 2 * value_width)
    w_v = rest_all[:, :value_width]
    w_o = rest_all[:, value_width:]
    w_fv = jnp.concatenate([w_f, w_v], axis=1)
    w_qfv = jnp.concatenate([w_q, w_fv], axis=1)
    parts_all = parts_all.reshape(wide, -1)
    table = parts_all[:, :vocab_part]
    w_gu = parts_all[:, vocab_part : vocab_part + gu_cols]
    w_d = parts_all[:, vocab_part + gu_cols :]

    positions = loss_positions[0]
    pick_hit = positions[:, None] == jnp.arange(tokens)[None, :]
    pick = pick_hit.astype(f32)
    pick_low = pick_hit.astype(bf16)
    documents = document_ids(doc_starts[0], tokens)
    doc_at = jnp.sum(jnp.where(pick_hit, documents[None, :], 0), axis=1)
    allowed = (positions[:, None] >= jnp.arange(tokens)[None, :]) & (
        doc_at[:, None] == documents[None, :]
    )

    def tall_norm(values, gain):
        mean = jnp.sum(values * values, axis=0, keepdims=True) * (1.0 / width)
        return values * lax.rsqrt(mean + NORM_EPS) * gain[:, None]

    normed_one = tall_norm(stream.astype(f32), gains[0]).astype(bf16)
    normed_at = times_right(pick_low, normed_one).astype(bf16)
    stream_at = times_right(
        lax.dynamic_slice_in_dim(pick_low, me_state * slot_part, slot_part), stream
    )
    forget_value = times_left(normed_one, w_fv)
    query_pre = times_plain(normed_at, w_q)
    query, back_query = jax.vjp(jax.nn.silu, query_pre)
    (key_gate, log_forget), back_gates = jax.vjp(forget_gates, forget_value[:, :qcols])

    def mix(query_in, key_in, forget_in, value_in):
        return slot_mixer(query_in, key_in, forget_in, value_in, pick, allowed, heads, key_part)

    mixed, back_mix = jax.vjp(
        mix,
        query.astype(bf16).astype(f32),
        key_gate.astype(bf16).astype(f32),
        log_forget,
        forget_value[:, qcols:].astype(bf16).astype(f32),
    )

    def head_norm(mixed_in, gain_in):
        return rms_norm(
            mixed_in.reshape(slots, heads, VAL_DIM), gain_in.reshape(heads, VAL_DIM), VAL_DIM
        ).reshape(slots, value_width)

    gated_f, back_head = jax.vjp(head_norm, mixed, head_gain)
    gated = gated_f.astype(bf16)
    stream_one = stream_at + state_sum(times_right(gated, w_o).astype(bf16), 2)

    def wide_norm(values, gain):
        return rms_norm(values, gain, width)

    normed_two = wide_norm(stream_one, gains[2])
    rows_two = gather_all(normed_two.astype(bf16), 3)
    gate_up = times_plain(rows_two, w_gu)
    hidden = swiglu(gate_up, unit_part, down_cols).astype(bf16)
    stream_two = stream_one + scatter_all(times_right(hidden, w_d).astype(bf16), 4)
    normed_three = wide_norm(stream_two, gains[3])
    rows_three = gather_all(normed_three.astype(bf16), 5)

    logits = times_plain(rows_three, table)
    column = jnp.arange(vocab_part)[None, :] + me_dp * vocab_part
    target_hit = (column + me_state * vocab_share == targets_all[:, None]) & (
        column < vocab_share
    )
    logits = jnp.where(column < vocab_share, logits, -1e30)
    top_here = jnp.max(logits, axis=1)
    sum_here = jnp.sum(jnp.exp(logits - top_here[:, None]), axis=1)
    picked_here = jnp.sum(jnp.where(target_hit, logits, 0.0), axis=1)
    shares = small_gather(
        [jnp.stack([top_here, sum_here, picked_here]).reshape(-1, LANES)], True, 6
    )[0].reshape(nd * ns, 3, -1)
    top = jnp.max(shares[:, 0], axis=0)
    lse = top + jnp.log(jnp.sum(shares[:, 1] * jnp.exp(shares[:, 0] - top[None]), axis=0))
    loss_sum = jnp.sum((lse - jnp.sum(shares[:, 2], axis=0)) * live)
    probs = jnp.exp(logits - lse[:, None])
    dlogits = ((probs - target_hit.astype(f32)) * (live / count)[:, None]).astype(bf16)
    grad_table_part = times_left(rows_three, dlogits).astype(bf16)
    grad_one, grad_table_back, grad_ffn, gain_pair = slots_back(
        times_right(dlogits, table).astype(bf16),
        grad_table_part.reshape(nd, own, vocab_part),
        stream_two,
        stream_one,
        gains[2:],
        w_d,
        w_gu,
        gate_up,
        hidden,
        rows_two,
        width,
        unit_part,
        7,
    )
    grad_gain_three, grad_gain_four = gain_pair
    grad_table_own = join_columns(grad_table_back)[:, :vocab_share].astype(f32)

    grad_gated = times_plain(grad_one, w_o)
    grad_w_o = times_left(grad_one, gated)
    grad_mixed, grad_gain_two = back_head(grad_gated)
    grad_query, grad_key, grad_forget, grad_value = back_mix(
        grad_mixed.astype(bf16).astype(f32)
    )
    (grad_query_pre,) = back_query(grad_query)
    grad_query_pre = times_left(pick, grad_query_pre)
    (grad_forget_pre,) = back_gates((grad_key, grad_forget))
    grad_qfv = jnp.concatenate([grad_query_pre, grad_forget_pre, grad_value], axis=1).astype(bf16)
    grad_w_qfv = times_plain(normed_one, grad_qfv)
    grad_norm_one = scatter_state(times_right(w_qfv, grad_qfv).astype(bf16), 1).astype(f32)
    _, back_one = jax.vjp(tall_norm, stream_mine.astype(f32), gains[0])
    grad_stream_zero, grad_gain_one = back_one(grad_norm_one)
    pick_mine = lax.dynamic_slice_in_dim(pick_low, me_state * quarter, quarter, axis=1)
    grad_zero = (grad_stream_zero + times_left(grad_one, pick_mine)).astype(bf16)
    grad_mixer_own = lax.psum_scatter(
        jnp.concatenate([grad_w_qfv, grad_w_o], axis=1).astype(bf16),
        "dp",
        scatter_dimension=0,
        tiled=True,
    )

    embed = swap_dp(grad_zero.reshape(nd, own, quarter))
    embed = gather_state(embed, 2).transpose(1, 0, 2).reshape(own, nd * tokens)
    grad_lookup = times_right(embed, hit.astype(bf16))
    grad_mixer_own, grad_lookup = lax.optimization_barrier((grad_mixer_own, grad_lookup))
    own_table = grad_table_own + grad_lookup

    grad_keys = grad_mixer_own[:, : 2 * qcols].reshape(own, 2, ns, key_part)
    grad_keys = grad_keys.transpose(2, 0, 1, 3).reshape(ns, own, 2 * key_part)
    grad_keys = lax.all_to_all(grad_keys, "state", split_axis=0, concat_axis=0, tiled=True)
    grad_keys = grad_keys.reshape(ns, own, 2, key_part).transpose(1, 2, 0, 3)
    grad_gate = grad_ffn[:, :, :unit_part]
    grad_up = grad_ffn[:, :, unit_part : 2 * unit_part]
    grad_down = grad_ffn[:, :, gu_cols : gu_cols + unit_part]
    own_in = jnp.concatenate(
        [
            grad_keys.reshape(own, 2 * key_cols),
            grad_mixer_own[:, 2 * qcols : 2 * qcols + value_width],
            join_columns(grad_gate),
            join_columns(grad_up),
        ],
        axis=1,
    ).astype(f32)
    own_out = jnp.concatenate(
        [grad_mixer_own[:, 2 * qcols + value_width :], join_columns(grad_down)],
        axis=1,
    ).astype(f32)

    head_full = lax.dynamic_update_slice_in_dim(
        jnp.zeros((width,), f32), grad_gain_two, me_state * value_width, 0
    )
    gain_parts = jnp.concatenate([grad_gain_one, grad_gain_three, grad_gain_four, head_full])
    gain_parts = small_gather([in_rows(gain_parts.astype(bf16))], True, 11)[0]
    gain_sums = jnp.sum(gain_parts.reshape(nd * ns, -1)[:, : 3 * wide + width].astype(f32), axis=0)
    head_slots = (
        jnp.zeros((nd * capacity, block_rows), f32)
        .at[index]
        .set(gain_sums[3 * wide :].reshape(block_count, block_rows))
    )
    gain_slots = gain_sums[: 3 * wide].reshape(3, nd * capacity, block_rows)
    gain_slots = jnp.stack([gain_slots[0], head_slots, gain_slots[1], gain_slots[2]], axis=1)
    own_gain = lax.dynamic_slice_in_dim(gain_slots, me_dp * capacity, capacity)

    squares = jnp.sum(own_in * own_in) + jnp.sum(own_out * own_out) + jnp.sum(own_table * own_table)
    squares = small_gather([jnp.full((8, LANES), squares)], True, 10)[0][:, 0, 0]
    squares_all = jnp.sum(squares) + jnp.sum(gain_sums * gain_sums)
    grad_norm = jnp.sqrt(squares_all)
    scale = jnp.minimum(1.0, CLIP_NORM / (grad_norm + 1e-06))
    occupied = occupied_here.astype(f32)
    wide_occ = occupied[None, :, None, None]
    new_in = adam_update(
        in_weight,
        in_first,
        in_second,
        in_average,
        own_in.reshape(in_weight.shape),
        scale,
        LEARN_RATE,
        WEIGHT_DECAY,
        wide_occ,
    )
    new_out = adam_update(
        out_weight,
        out_first,
        out_second,
        out_average,
        own_out.reshape(out_weight.shape),
        scale,
        LEARN_RATE,
        WEIGHT_DECAY,
        wide_occ,
    )
    new_table = adam_update(
        table_weight,
        table_first,
        table_second,
        table_average,
        own_table.reshape(table_weight.shape),
        scale,
        LEARN_RATE,
        WEIGHT_DECAY,
        wide_occ,
    )
    new_gain = adam_update(
        gain_weight,
        gain_first,
        gain_second,
        gain_average,
        own_gain,
        scale,
        GAIN_RATE,
        0.0,
        occupied[:, None, None],
    )
    return (
        new_in[0],
        new_out[0],
        new_table[0],
        new_gain[0],
        new_in[1],
        new_out[1],
        new_table[1],
        new_gain[1],
        new_in[2],
        new_out[2],
        new_table[2],
        new_gain[2],
        new_in[3],
        new_out[3],
        new_table[3],
        new_gain[3],
        loss_sum,
        count,
        grad_norm,
    )


def solution(mesh):
    return jax.shard_map(
        on_device,
        mesh=mesh,
        in_specs=(
            P("dp", None),
            P("dp", None),
            P("dp", None),
            P("dp", None),
            P(),
            P("state", "dp", None, None),
            P("state", "dp", None, None),
            P("state", "dp", None, None),
            P("dp", None, None),
            P("state", "dp", None, None),
            P("state", "dp", None, None),
            P("state", "dp", None, None),
            P("dp", None, None),
            P("state", "dp", None, None),
            P("state", "dp", None, None),
            P("state", "dp", None, None),
            P("dp", None, None),
            P("state", "dp", None, None),
            P("state", "dp", None, None),
            P("state", "dp", None, None),
            P("dp", None, None),
        ),
        out_specs=(
            P("state", "dp", None, None),
            P("state", "dp", None, None),
            P("state", "dp", None, None),
            P("dp", None, None),
            P("state", "dp", None, None),
            P("state", "dp", None, None),
            P("state", "dp", None, None),
            P("dp", None, None),
            P("state", "dp", None, None),
            P("state", "dp", None, None),
            P("state", "dp", None, None),
            P("dp", None, None),
            P("state", "dp", None, None),
            P("state", "dp", None, None),
            P("state", "dp", None, None),
            P("dp", None, None),
            P(),
            P(),
            P(),
        ),
        check_vma=False,
    )
```

```python
import functools

import jax
import jax.numpy as jnp
from jax import lax
from jax.experimental import pallas as pl
from jax.experimental.pallas import tpu as pltpu
from jax.sharding import PartitionSpec as P

HEADS = 16
KEY_DIM = 128
GROUP = 128
STEP = 5
VAL_DIM = 128


NORM_EPS = 1e-06
LOWER_BOUND = 0.9
CLIP_NORM = 0.02
BETA_FIRST = 0.5
BETA_SECOND = 0.5
ADAM_EPS = 1e-08
LEARN_RATE = 0.02
GAIN_RATE = 0.2
WEIGHT_DECAY = 0.1
AVERAGE_DECAY = 0.9
FULL_PRECISION = lax.Precision.HIGHEST
LANES = 128
CHUNKS = 5
FEED = ((2, 3, 3), (6, 4), 6, (5, 6, 0))


def rms_norm(values, gain, width):
    mean = jnp.sum(values * values, axis=-1, keepdims=True) * (1.0 / width)
    return values * lax.rsqrt(mean + NORM_EPS) * gain


def forget_gates(forget_pre):
    key_gate = (1.0 - LOWER_BOUND) * jax.nn.sigmoid(-forget_pre)
    log_forget = jnp.log(LOWER_BOUND + (1.0 - LOWER_BOUND) * jax.nn.sigmoid(forget_pre))
    return key_gate, log_forget


def slot_mixer(query, key_gate, log_forget, values, pick, allowed, heads, key_part):
    slots = query.shape[0]
    tokens = key_gate.shape[0]
    blocks = tokens // GROUP
    order = jnp.arange(GROUP)
    lower = (order[:, None] >= order[None, :]).astype(jnp.float32)
    number = jnp.arange(blocks)
    before = (number[:, None] > number[None, :]).astype(jnp.float32)
    inside = jnp.einsum(
        "ts,bsk->btk", lower, log_forget.reshape(blocks, GROUP, -1), precision=FULL_PRECISION
    )
    total = inside[:, -1]
    offset = jnp.dot(before, total, precision=FULL_PRECISION)
    ends = offset + total
    along = (inside + offset[:, None]).reshape(tokens, -1)
    at_slots = jnp.dot(pick, along, precision=FULL_PRECISION)
    key_decay = key_gate * jnp.exp(total[:, None] - inside).reshape(tokens, -1)
    grown = query[None] * jnp.exp(jnp.minimum(at_slots[None] - ends[:, None], 16.0))
    key_decay = key_decay.reshape(blocks, GROUP, heads * KEY_DIM)
    column = jnp.arange(heads * KEY_DIM)
    of_head = (column % key_part) // (key_part // heads) == jnp.arange(heads)[:, None]
    grown = jnp.where(of_head[:, None, None], grown[None], 0.0)
    scores = jnp.einsum("hbnk,bgk->hnbg", grown, key_decay, precision=FULL_PRECISION)
    scores = jnp.where(allowed[None], scores.reshape(heads, slots, tokens), 0.0)
    mixed = jnp.einsum(
        "hns,shv->nhv", scores, values.reshape(tokens, heads, VAL_DIM), precision=FULL_PRECISION
    )
    return mixed.reshape(slots, -1)


def document_ids(starts, length):
    return jnp.sum((jnp.arange(length)[:, None] >= starts[None, :]).astype(jnp.int32), axis=1) - 1


def slot_index(owners, capacity):
    order = jnp.arange(owners.shape[0])
    earlier = (owners[:, None] == owners[None, :]) & (order[None, :] < order[:, None])
    ranks = jnp.sum(earlier.astype(jnp.int32), axis=1)
    return owners * capacity + ranks


def adam_update(weight, first, second, average, grad, scale, rate, decay, occupied):
    clipped = scale * grad
    first_new = BETA_FIRST * first + (1.0 - BETA_FIRST) * clipped
    second_new = BETA_SECOND * second + (1.0 - BETA_SECOND) * clipped * clipped
    first_hat = first_new / (1.0 - BETA_FIRST**STEP)
    second_hat = second_new / (1.0 - BETA_SECOND**STEP)
    weight_new = weight - rate * (first_hat / (jnp.sqrt(second_hat) + ADAM_EPS) + decay * weight)
    average_new = AVERAGE_DECAY * average + (1.0 - AVERAGE_DECAY) * weight_new
    return (
        weight_new * occupied,
        first_new * occupied,
        second_new * occupied,
        average_new * occupied,
    )


def adam_kernel(
    rate, decay, scale_ref, held_ref, weight, first, second, average, grad,
    weight_out, first_out, second_out, average_out
):
    occupied = held_ref[pl.program_id(0)]
    found = adam_update(
        weight[...],
        first[...],
        second[...],
        average[...],
        grad[...],
        scale_ref[0],
        rate,
        decay,
        occupied,
    )
    for out, value in zip((weight_out, first_out, second_out, average_out), found):
        out[...] = value


def adam_blocks(weight, first, second, average, grad, scale, rate, decay, occupied):
    capacity, block_rows, cols = weight.shape[1:]
    rows = 16
    block = pl.BlockSpec((1, 1, rows, cols), lambda i, j: (0, i, j, 0))
    scalar = pl.BlockSpec(memory_space=pltpu.SMEM)
    return pl.pallas_call(
        functools.partial(adam_kernel, rate, decay),
        grid=(capacity, block_rows // rows),
        out_shape=[jax.ShapeDtypeStruct(weight.shape, weight.dtype)] * 4,
        in_specs=[scalar, scalar] + [block] * 5,
        out_specs=[block] * 4,
        compiler_params=pltpu.CompilerParams(vmem_limit_bytes=40 * 2**20),
    )(scale.reshape(1), occupied, weight, first, second, average, grad)


def times_plain(left, right):
    return jnp.dot(left, right, preferred_element_type=jnp.float32)


def times_right(left, right):
    return lax.dot_general(
        left, right, (((1,), (1,)), ((), ())), preferred_element_type=jnp.float32
    )


def times_left(left, right):
    return lax.dot_general(
        left, right, (((0,), (0,)), ((), ())), preferred_element_type=jnp.float32
    )


def swiglu(joined, units, cols):
    gate = joined[:, :units]
    up = joined[:, units : 2 * units]
    return jnp.pad(jax.nn.silu(gate) * up, ((0, 0), (0, cols - units)))


EVERY = ("dp", "state")


def gather_state(values, axis=0):
    return lax.all_gather(values, "state", axis=axis, tiled=True)


def scatter_state(values, axis=0):
    return lax.psum_scatter(values, "state", scatter_dimension=axis, tiled=True)


def swap_dp(values):
    return lax.all_to_all(values, "dp", split_axis=0, concat_axis=0, tiled=True)


def spread_columns(own, parts):
    return own.reshape(own.shape[0], parts, -1).transpose(1, 0, 2)


def join_columns(split):
    return split.transpose(1, 0, 2).reshape(split.shape[1], -1)


MESH = pl.DeviceIdType.MESH


class Links:
    def __init__(self, sends, recvs):
        self.sends, self.recvs, self.used, self.open = sends, recvs, 0, []

    def copy(self, src, dst, dp, state):
        number = self.used
        self.used += 1
        made = pltpu.make_async_remote_copy(
            src_ref=src,
            dst_ref=dst,
            send_sem=self.sends.at[number],
            recv_sem=self.recvs.at[number],
            device_id=(dp, state),
            device_id_type=MESH,
        )
        made.start()
        self.open.append(made)
        return made

    def settle(self, copies):
        for made in copies:
            made.wait_send()
        self.open = [made for made in self.open if not any(made is one for one in copies)]

    def finish(self):
        for made in self.open:
            made.wait_send()


def nothing(place):
    del place


def greet(peers):
    barrier = pltpu.get_barrier_semaphore()
    for dp, state in peers:
        pl.semaphore_signal(barrier, inc=1, device_id=(dp, state), device_id_type=MESH)
    pl.semaphore_wait(barrier, len(peers))


def places(nd, ns):
    dp, st = lax.axis_index("dp"), lax.axis_index("state")
    return dp, st, lax.div(dp, 2), lax.rem(dp, 2), lax.div(st, 2), lax.rem(st, 2)


def near_peers(nd, ns):
    dp, st, z, y, x, c = places(nd, ns)
    deep, across = nd // 2, ns // 2
    peers = [(lax.rem(z + k, deep) * 2 + y, st) for k in range(1, deep)]
    peers.append((dp + 1 - 2 * y, st))
    peers += [(dp, lax.rem(x + k, across) * 2 + c) for k in range(1, across)]
    peers.append((dp, st + 1 - 2 * c))
    return peers


def small_gather_kernel(nd, ns, everyone, count, *refs):
    sources, outs, (sends, recvs) = refs[:count], refs[count : 2 * count], refs[2 * count :]
    dp, st = lax.axis_index("dp"), lax.axis_index("state")
    peers = []
    for a in range(nd):
        for b in range(ns if everyone else 1):
            if a or b:
                peers.append((lax.rem(dp + a, nd), lax.rem(st + b, ns)))
    greet(peers)
    me = dp * ns + st if everyone else dp
    links = Links(sends, recvs)
    for source, out in zip(sources, outs):
        out[me] = source[...]
        for there, far in peers:
            links.copy(source, out.at[me], there, far)
    for made in links.open:
        made.wait_recv()
    links.finish()


def small_gather(arrays, everyone, number):
    nd, ns = lax.axis_size("dp"), lax.axis_size("state")
    members = nd * ns if everyone else nd
    copies = (members - 1) * len(arrays)
    vmem = pl.BlockSpec(memory_space=pltpu.VMEM)
    return pl.pallas_call(
        functools.partial(small_gather_kernel, nd, ns, everyone, len(arrays)),
        out_shape=[jax.ShapeDtypeStruct((members,) + a.shape, a.dtype) for a in arrays],
        in_specs=[vmem] * len(arrays),
        out_specs=[vmem] * len(arrays),
        scratch_shapes=[pltpu.SemaphoreType.DMA((copies,)), pltpu.SemaphoreType.DMA((copies,))],
        compiler_params=pltpu.CompilerParams(collective_id=number, has_side_effects=True),
    )(*arrays)


def gather_all_kernel(nd, ns, in_ref, out_ref, sends, recvs):
    greet(near_peers(nd, ns))
    links = Links(sends, recvs)
    gather_body(nd, ns, links, in_ref, out_ref)
    links.finish()


def gather_body(nd, ns, links, in_ref, out_ref, meanwhile=nothing):
    dp, st, z, y, x, c = places(nd, ns)
    deep, across = nd // 2, ns // 2
    half = in_ref.shape[1] // 2
    cols = (pl.ds(0, half), pl.ds(half, half))
    to_y = (dp + 1 - 2 * y, st)
    to_core = (dp, st + 1 - 2 * c)
    other_y = 1 - y

    def x_at(k):
        return lax.rem(x + k, across)

    def to_x(k):
        return (dp, x_at(k) * 2 + c)

    def group(xx, yy, part):
        return out_ref.at[c, xx, yy, :, :, cols[part]]

    def send(xx, yy, part, place):
        return links.copy(group(xx, yy, part), group(xx, yy, part), *place)

    out_ref[c, x, y, z] = in_ref[...]
    first = []
    for part in range(2):
        for k in range(1, deep):
            there = (lax.rem(z + k, deep) * 2 + y, st)
            first.append(
                links.copy(
                    in_ref.at[:, cols[part]], out_ref.at[c, x, y, z, :, cols[part]], *there
                )
            )
    for made in first[: deep - 1]:
        made.wait_recv()
    a_y = send(x, y, 0, to_y)
    for made in first[deep - 1 :]:
        made.wait_recv()
    b_x = [send(x, y, 1, to_x(k)) for k in range(1, across)]
    a_x = [send(x, y, 0, to_x(k)) for k in range(1, across)]
    b_y = send(x, y, 1, to_y)
    arriving = [send(x, y, 0, to_core), send(x, y, 1, to_core)]
    meanwhile(0)
    a_y.wait_recv()
    a_xy = [send(x, other_y, 0, to_x(k)) for k in range(1, across)]
    arriving.append(send(x, other_y, 0, to_core))
    b_xy = []
    for k in range(1, across):
        b_x[k - 1].wait_recv()
        from_x = lax.rem(x - k + across, across)
        b_xy.append(send(from_x, y, 1, to_y))
        arriving.append(send(from_x, y, 1, to_core))
    meanwhile(1)
    for k in range(1, across):
        a_x[k - 1].wait_recv()
        arriving.append(send(lax.rem(x - k + across, across), y, 0, to_core))
    b_y.wait_recv()
    arriving.append(send(x, other_y, 1, to_core))
    for k in range(1, across):
        from_x = lax.rem(x - k + across, across)
        a_xy[k - 1].wait_recv()
        arriving.append(send(from_x, other_y, 0, to_core))
        b_xy[k - 1].wait_recv()
        arriving.append(send(from_x, other_y, 1, to_core))
    for made in arriving:
        made.wait_recv()
    links.settle(first + [a_y, b_y] + b_x + a_x + a_xy + b_xy + arriving)


def gather_copies(nd, ns):
    deep, across = nd // 2, ns // 2
    return 2 * (deep - 1) + 2 + 4 * (across - 1) + 4 * across


def gather_all(values, number):
    nd, ns = lax.axis_size("dp"), lax.axis_size("state")
    rows, wide = values.shape
    deep, across = nd // 2, ns // 2
    copies = gather_copies(nd, ns)
    vmem = pl.BlockSpec(memory_space=pltpu.VMEM)
    out = pl.pallas_call(
        functools.partial(gather_all_kernel, nd, ns),
        out_shape=jax.ShapeDtypeStruct((2, across, 2, deep, rows, wide), values.dtype),
        in_specs=[vmem],
        out_specs=vmem,
        scratch_shapes=[pltpu.SemaphoreType.DMA((copies,)), pltpu.SemaphoreType.DMA((copies,))],
        compiler_params=pltpu.CompilerParams(
            collective_id=number, has_side_effects=True, vmem_limit_bytes=40 * 2**20
        ),
    )(values)
    return out.reshape(nd * ns * rows, wide)


def scatter_all_kernel(nd, ns, in_ref, out_ref, *scratch):
    sends, recvs = scratch[-2:]
    greet(near_peers(nd, ns))
    links = Links(sends, recvs)
    scatter_body(nd, ns, links, in_ref, out_ref, scratch[:-2])
    links.finish()


def scatter_body(nd, ns, links, in_ref, out_ref, scratch, meanwhile=nothing):
    rc, acc, rx_a, ry_a, rz_a, ry_b, rx_b, rz_b = scratch
    dp, st, z, y, x, c = places(nd, ns)
    deep, across = nd // 2, ns // 2
    half = in_ref.shape[5] // 2
    cols = (pl.ds(0, half), pl.ds(half, half))
    to_y = (dp + 1 - 2 * y, st)
    to_core = (dp, st + 1 - 2 * c)
    ys = (y, 1 - y)

    def x_at(k):
        return lax.rem(x + k, across)

    def to_x(k):
        return (dp, x_at(k) * 2 + c)

    core = {}
    order = [(k, ky, 0) for k in range(1, across) for ky in (1, 0)]
    order += [(k, 1, 1) for k in range(across)]
    order += [(0, 1, 0)] + [(k, 0, 1) for k in range(1, across)] + [(0, 0, 0), (0, 0, 1)]
    for k, ky, part in order:
        core[k, ky, part] = links.copy(
            in_ref.at[1 - c, x_at(k), ys[ky], :, :, cols[part]],
            rc.at[x_at(k), ys[ky], :, :, cols[part]],
            *to_core,
        )

    def total(k, ky, part, zz, others):
        found = in_ref[c, x_at(k), ys[ky], zz, :, cols[part]].astype(jnp.float32)
        found += rc[x_at(k), ys[ky], zz, :, cols[part]].astype(jnp.float32)
        for other in others:
            found += other[zz].astype(jnp.float32)
        return found

    def add(k, ky, part, others):
        core[k, ky, part].wait_recv()

        @pl.loop(0, deep)
        def _(zz):
            acc[x_at(k), ys[ky], zz, :, cols[part]] = total(k, ky, part, zz, others).astype(
                acc.dtype
            )

        return acc.at[x_at(k), ys[ky], :, :, cols[part]]

    meanwhile(0)
    a_x, b_y = {}, {}
    for k in range(1, across):
        for ky in (1, 0):
            a_x[k, ky] = links.copy(add(k, ky, 0, []), rx_a.at[k - 1, ky], *to_x(k))
    for k in range(across):
        b_y[k] = links.copy(add(k, 1, 1, []), ry_b.at[k], *to_y)
    meanwhile(1)
    for k in range(1, across):
        a_x[k, 1].wait_recv()
    a_y = links.copy(
        add(0, 1, 0, [rx_a.at[k - 1, 1] for k in range(1, across)]), ry_a, *to_y
    )
    b_x = {}
    for k in range(1, across):
        b_y[k].wait_recv()
        b_x[k] = links.copy(add(k, 0, 1, [ry_b.at[k]]), rx_b.at[k - 1], *to_x(k))
    meanwhile(2)
    for k in range(1, across):
        a_x[k, 0].wait_recv()
    a_y.wait_recv()
    left = [rx_a.at[k - 1, 0] for k in range(1, across)] + [ry_a]
    add(0, 0, 0, left)

    def send_z(part, land):
        return [
            links.copy(
                acc.at[x, y, lax.rem(z + k, deep), :, cols[part]],
                land.at[k - 1],
                lax.rem(z + k, deep) * 2 + y,
                st,
            )
            for k in range(1, deep)
        ]

    a_z = send_z(0, rz_a)
    b_y[0].wait_recv()
    for k in range(1, across):
        b_x[k].wait_recv()
    right = [ry_b.at[0]] + [rx_b.at[k - 1] for k in range(1, across)]
    add(0, 0, 1, right)
    b_z = send_z(1, rz_b)
    for part, made, others, land in ((0, a_z, left, rz_a), (1, b_z, right, rz_b)):
        found = total(0, 0, part, z, others)
        for k in range(1, deep):
            made[k - 1].wait_recv()
            found += land[k - 1].astype(jnp.float32)
        out_ref[:, cols[part]] = found
    links.settle(
        list(core.values()) + list(a_x.values()) + list(b_y.values()) + list(b_x.values())
        + [a_y] + a_z + b_z
    )


def scatter_copies(nd, ns):
    deep, across = nd // 2, ns // 2
    return 4 * across + 2 * (across - 1) + across + 1 + (across - 1) + 2 * (deep - 1)


def scatter_scratch(nd, ns, rows, wide, kind):
    deep, across = nd // 2, ns // 2
    half = wide // 2
    return [
        pltpu.VMEM((across, 2, deep, rows, wide), kind),
        pltpu.VMEM((across, 2, deep, rows, wide), kind),
        pltpu.VMEM((across - 1, 2, deep, rows, half), kind),
        pltpu.VMEM((deep, rows, half), kind),
        pltpu.VMEM((deep - 1, rows, half), kind),
        pltpu.VMEM((across, deep, rows, half), kind),
        pltpu.VMEM((across - 1, deep, rows, half), kind),
        pltpu.VMEM((deep - 1, rows, half), kind),
    ]


def scatter_all(values, number):
    nd, ns = lax.axis_size("dp"), lax.axis_size("state")
    deep, across = nd // 2, ns // 2
    rows, wide = values.shape[0] // (nd * ns), values.shape[1]
    copies = scatter_copies(nd, ns)
    vmem = pl.BlockSpec(memory_space=pltpu.VMEM)
    kind = values.dtype
    return pl.pallas_call(
        functools.partial(scatter_all_kernel, nd, ns),
        out_shape=jax.ShapeDtypeStruct((rows, wide), jnp.float32),
        in_specs=[vmem],
        out_specs=vmem,
        scratch_shapes=scatter_scratch(nd, ns, rows, wide, kind)
        + [pltpu.SemaphoreType.DMA((copies,)), pltpu.SemaphoreType.DMA((copies,))],
        compiler_params=pltpu.CompilerParams(
            collective_id=number, has_side_effects=True, vmem_limit_bytes=40 * 2**20
        ),
    )(values.reshape(2, across, 2, deep, rows, wide))


def front_kernel(
    nd,
    ns,
    depth_used,
    small_ref,
    gain_ref,
    table_ref,
    keys_ref,
    rest_ref,
    parts_ref,
    small_out,
    gain_out,
    rows_out,
    keys_out,
    rest_out,
    parts_out,
    looked,
    rc,
    acc,
    rx,
    fin,
    sums,
    sends,
    recvs,
    local,
):
    dp, st, z, y, x, c = places(nd, ns)
    deep, across = nd // 2, ns // 2
    own = table_ref.shape[0]
    tokens = rows_out.shape[1]
    part = tokens // ns
    to_core = (dp, st + 1 - 2 * c)
    to_y = (dp + 1 - 2 * y, st)
    other_y = dp + 1 - 2 * y
    dp_peers = [(lax.rem(dp + k, nd), st) for k in range(1, nd)]
    state_peers = [(dp, lax.rem(st + k, ns)) for k in range(1, ns)]
    greet(dp_peers + state_peers)
    links = Links(sends, recvs)

    ids_made = {}
    small_out[dp] = small_ref[...]
    gain_out[dp] = gain_ref[...]
    for k in range(1, nd):
        ids_made[k] = links.copy(small_ref, small_out.at[dp], *dp_peers[k - 1])
    gain_made = [links.copy(gain_ref, gain_out.at[dp], *peer) for peer in dp_peers]

    here = [
        pltpu.make_async_copy(keys_ref.at[st], keys_out.at[st, dp], local.at[0]),
        pltpu.make_async_copy(rest_ref, rest_out.at[dp], local.at[1]),
        pltpu.make_async_copy(parts_ref.at[dp], parts_out.at[dp], local.at[2]),
    ]
    for made in here:
        made.start()
    key_made = [
        links.copy(keys_ref.at[peer[1]], keys_out.at[st, dp], *peer) for peer in state_peers
    ]

    class Gather:
        def __init__(self, view):
            self.view = view
            self.base = links.used
            links.used += 2 * (deep - 1) + 1 + 2 * (deep - 1)

        def copy(self, number, owner, place):
            return pltpu.make_async_remote_copy(
                src_ref=self.view(owner),
                dst_ref=self.view(owner),
                send_sem=sends.at[self.base + number],
                recv_sem=recvs.at[self.base + number],
                device_id=place,
                device_id_type=MESH,
            )

        def pass_on(self, way, step):
            behind = z - way * step
            ahead = z + way
            number = step if way > 0 else deep - 1 + step

            def go(made):
                @pl.when((behind >= 0) & (behind < deep) & (ahead >= 0) & (ahead < deep))
                def _():
                    made(self.copy(number, behind * 2 + y, (ahead * 2 + y, st)))

            return go

        def begin(self):
            self.copy(2 * (deep - 1), dp, to_y).start()
            for way in (1, -1):
                self.pass_on(way, 0)(lambda made: made.start())

        def arrive(self, way, step):
            began = z - way * (step + 1)
            number = step if way > 0 else deep - 1 + step

            @pl.when((began >= 0) & (began < deep))
            def _():
                self.copy(number, began * 2 + y, to_y).wait_recv()
                self.copy(2 * (deep - 1) + 1 + number, began * 2 + y, to_y).start()

            if step + 1 < deep - 1:
                self.pass_on(way, step + 1)(lambda made: made.start())

        def finish(self):
            self.copy(2 * (deep - 1), other_y, to_y).wait_recv()
            self.copy(2 * (deep - 1), dp, to_y).wait_send()
            for way in (1, -1):
                for step in range(deep - 1):
                    began = z - way * (step + 1)
                    number = step if way > 0 else deep - 1 + step
                    self.pass_on(way, step)(lambda made: made.wait_send())

                    @pl.when((began >= 0) & (began < deep))
                    def _():
                        made = self.copy(2 * (deep - 1) + 1 + number, began * 2 + y, to_y)
                        made.wait_send()
                        made.wait_recv()

    rest = Gather(lambda owner: rest_out.at[owner])
    keys = Gather(lambda owner: keys_out.at[:, owner])
    here[1].wait()
    rest.begin()

    def swap(k):
        there = lax.rem(dp + k, nd)
        return links.copy(parts_ref.at[there], parts_out.at[dp], there, st)

    swapped = [swap(k) for k in range(1, nd // 2)]
    here[0].wait()
    for made in key_made:
        made.wait_recv()
    keys.begin()

    def x_at(k):
        return lax.rem(x + k, across)

    def row_at(k):
        return lax.rem(dp + k, nd)

    def block(k, kx, cc):
        start = (x_at(kx) * 2 + cc) * part
        return looked.at[k, :, pl.ds(pl.multiple_of(start, part), part)]

    def place(owner, share):
        return rows_out.at[
            pl.ds(pl.multiple_of(owner * own, own), own),
            pl.ds(pl.multiple_of(share * part, part), part),
        ]

    def add(sources, target):
        @pl.loop(0, own // 32)
        def _(i):
            rows = pl.ds(pl.multiple_of(i * 32, 32), 32)
            found = sources[0][rows, :].astype(jnp.float32)
            for source in sources[1:]:
                found += source[rows, :].astype(jnp.float32)
            target[rows, :] = found.astype(target.dtype)

    depth = table_ref.shape[1]
    piece = min(1024, depth)
    span = 2 * LANES

    def look(k):
        row = row_at(k)

        @pl.loop(0, tokens // span)
        def _(i):
            ids = jnp.concatenate(
                [small_out[row, pl.ds(2 * i, 1), :], small_out[row, pl.ds(2 * i + 1, 1), :]],
                axis=1,
            )
            ids = ids - st * depth_used
            sums[...] = jnp.zeros_like(sums)

            @pl.loop(0, depth // piece)
            def _(j):
                number = lax.broadcasted_iota(jnp.int32, (piece, span), 0)
                hit = jnp.where(number == ids - j * piece, 1.0, 0.0).astype(jnp.bfloat16)
                cols = pl.ds(pl.multiple_of(j * piece, piece), piece)
                sums[...] += jnp.dot(
                    table_ref[:, cols], hit, preferred_element_type=jnp.float32
                )

            cols = pl.ds(pl.multiple_of(i * span, span), span)
            looked[k, :, cols] = sums[...].astype(looked.dtype)

    turn = list(range(1, nd)) + [0]
    core, across_x, across_dp = {}, {}, {}

    def start_core(k):
        for kx in list(range(1, across)) + [0]:
            core[k, kx] = links.copy(block(k, kx, 1 - c), rc.at[k, kx], *to_core)

    def start_x(k):
        for kx in range(1, across):
            core[k, kx].wait_recv()
            add([block(k, kx, c), rc.at[k, kx]], acc.at[k, kx - 1])
            across_x[k, kx] = links.copy(
                acc.at[k, kx - 1], rx.at[k, kx - 1], dp, x_at(kx) * 2 + c
            )

    def start_dp(k):
        core[k, 0].wait_recv()
        sources = [block(k, 0, c), rc.at[k, 0]]
        for kx in range(1, across):
            across_x[k, kx].wait_recv()
            sources.append(rx.at[k, kx - 1])
        if k:
            add(sources, fin.at[k - 1])
            across_dp[k] = links.copy(fin.at[k - 1], place(dp, st), row_at(k), st)
        else:
            add(sources, place(dp, st))

    chores = []
    for step in range(deep - 1):
        for way in (1, -1):
            chores.append(functools.partial(rest.arrive, way, step))
    for step in range(deep - 1):
        for way in (1, -1):
            chores.append(functools.partial(keys.arrive, way, step))
    each = -(-len(chores) // nd)
    for number, k in enumerate(turn):
        if k:
            ids_made[nd - k].wait_recv()
        look(k)
        start_core(k)
        if number >= 1:
            start_x(turn[number - 1])
        if number >= 2:
            start_dp(turn[number - 2])
        for _ in range(each):
            if number >= 2 and chores:
                chores.pop(0)()
    start_x(turn[-1])
    start_dp(turn[-2])
    start_dp(turn[-1])
    swapped += [swap(k) for k in range(nd // 2, nd)]
    later, last = {}, []
    for number, k in enumerate([0] + list(range(1, nd))):
        owner = lax.rem(dp - k + nd, nd)
        if k:
            across_dp[k].wait_recv()
        for kx in range(1, across):
            later[k, kx] = links.copy(
                place(owner, st), place(owner, st), dp, x_at(kx) * 2 + c
            )
        last.append(links.copy(place(owner, st), place(owner, st), *to_core))
        if chores:
            chores.pop(0)()
    for k in range(nd):
        owner = lax.rem(dp - k + nd, nd)
        for kx in range(1, across):
            later[k, kx].wait_recv()
            share = lax.rem(x - kx + across, across) * 2 + c
            last.append(links.copy(place(owner, share), place(owner, share), *to_core))
    while chores:
        chores.pop(0)()
    for made in last + swapped + gain_made:
        made.wait_recv()
    here[2].wait()
    links.finish()
    rest.finish()
    keys.finish()


def front(small, gain, table, keys, rest, parts, tokens, vocab, number):
    nd, ns = lax.axis_size("dp"), lax.axis_size("state")
    deep, across = nd // 2, ns // 2
    own = table.shape[0]
    part = tokens // ns
    kind = table.dtype
    copies = 2 * (nd - 1) + ns - 1 + 2 * (4 * (deep - 1) + 1) + nd - 1
    copies += nd * across + nd * (across - 1) + nd - 1 + nd * across + nd * (across - 1)
    vmem = pl.BlockSpec(memory_space=pltpu.VMEM)
    hbm = pl.BlockSpec(memory_space=pl.ANY)
    return pl.pallas_call(
        functools.partial(front_kernel, nd, ns, vocab),
        out_shape=[
            jax.ShapeDtypeStruct((nd,) + small.shape, small.dtype),
            jax.ShapeDtypeStruct((nd,) + gain.shape, gain.dtype),
            jax.ShapeDtypeStruct((nd * own, tokens), kind),
            jax.ShapeDtypeStruct((ns, nd) + keys.shape[1:], kind),
            jax.ShapeDtypeStruct((nd,) + rest.shape, kind),
            jax.ShapeDtypeStruct(parts.shape, kind),
        ],
        in_specs=[vmem, vmem, vmem, hbm, hbm, hbm],
        out_specs=[vmem, vmem, vmem, hbm, hbm, hbm],
        scratch_shapes=[
            pltpu.VMEM((nd, own, tokens), kind),
            pltpu.VMEM((nd, across, own, part), kind),
            pltpu.VMEM((nd, across - 1, own, part), kind),
            pltpu.VMEM((nd, across - 1, own, part), kind),
            pltpu.VMEM((nd - 1, own, part), kind),
            pltpu.VMEM((own, 2 * LANES), jnp.float32),
            pltpu.SemaphoreType.DMA((copies,)),
            pltpu.SemaphoreType.DMA((copies,)),
            pltpu.SemaphoreType.DMA((3,)),
        ],
        compiler_params=pltpu.CompilerParams(
            collective_id=number, has_side_effects=True, vmem_limit_bytes=52 * 2**20
        ),
        cost_estimate=pl.CostEstimate(
            flops=2 * table.size * nd * tokens, bytes_accessed=4 * parts.size, transcendentals=0
        ),
    )(small, gain, table, keys, rest, parts)


def slots_back_kernel(
    nd,
    ns,
    width,
    units,
    part_hbm,
    table_ref,
    two_ref,
    one_ref,
    gain_ref,
    wd_ref,
    wgu_ref,
    gu_ref,
    hidden_ref,
    rows_ref,
    one_out,
    table_out,
    ffn_out,
    gains_out,
    part_ref,
    summed,
    low,
    down,
    dgu,
    dffn,
    local,
    *scratch,
):
    sends, recvs = scratch[-2:]
    dp, st, z, y, x, c = places(nd, ns)
    deep, across = nd // 2, ns // 2
    count, wide = two_ref.shape
    every = nd * ns * count
    dp_peers = [(lax.rem(dp + k, nd), st) for k in range(1, nd)]
    state_peers = [(dp, lax.rem(st + k, ns)) for k in range(1, ns)]
    fill = pltpu.make_async_copy(part_hbm, part_ref, local.at[2])
    fill.start()
    greet(dp_peers + state_peers)
    links = Links(sends, recvs)
    own_copy = pltpu.make_async_copy(table_ref.at[dp], table_out.at[dp], local.at[0])
    own_copy.start()
    local_copies = [own_copy]
    own = table_ref.shape[1]
    chunk = own // CHUNKS
    queue = [(peer, i) for i in range(CHUNKS) for peer in dp_peers]
    swapped = []

    def feed(amount):
        for _ in range(min(amount, len(queue))):
            peer, i = queue.pop(0)
            rows = pl.ds(i * chunk, chunk)
            swapped.append(
                links.copy(table_ref.at[peer[0], rows], table_out.at[dp, rows], *peer)
            )

    def feeding(amounts):
        return lambda place: feed(amounts[place])

    def norm_back(grad, values, gain, row):
        mean = jnp.sum(values * values, axis=1, keepdims=True) * (1.0 / width)
        root = lax.rsqrt(mean + NORM_EPS)
        scaled = grad * gain
        inner = jnp.sum(scaled * values, axis=1, keepdims=True) * (1.0 / width)
        gains_out[pl.ds(row, 1), :] = jnp.sum(grad * values * root, axis=0, keepdims=True)
        return scaled * root - values * (root * root * root * inner)

    fill.wait()
    scatter_body(nd, ns, links, part_ref, summed, scratch[:-2], feeding(FEED[0]))
    summed[...] = norm_back(summed[...], two_ref[...], gain_ref[pl.ds(1, 1), :], 1)
    low[...] = summed[...].astype(low.dtype)
    gather_body(nd, ns, links, low, down, feeding(FEED[1]))
    feed(FEED[2])

    inner_cols = gu_ref.shape[1]
    step = deep * count
    flat_down = down

    @pl.loop(0, 2 * across * 2)
    def _(i):
        cc, rest = lax.div(i, 2 * across), lax.rem(i, 2 * across)
        xx, yy = lax.div(rest, 2), lax.rem(rest, 2)
        rows = pl.ds(pl.multiple_of(i * step, step), step)
        grad = jnp.dot(
            flat_down[cc, xx, yy].reshape(step, wide),
            wd_ref[...],
            preferred_element_type=jnp.float32,
        )
        grad = jnp.concatenate(
            [grad, jnp.zeros((step, inner_cols - grad.shape[1]), jnp.float32)], axis=1
        ) if inner_cols > grad.shape[1] else grad[:, :inner_cols]
        gate = gu_ref[rows, :]
        up = pltpu.roll(gate, inner_cols - units, 1)
        gated = 1.0 / (1.0 + jnp.exp(-gate))
        grad_gate = grad * up * (gated * (1.0 + gate * (1.0 - gated)))
        grad_up = pltpu.roll(grad * gate * gated, units, 1)
        lanes = lax.broadcasted_iota(jnp.int32, grad_gate.shape, 1)
        joined = jnp.where(lanes < units, grad_gate, grad_up).astype(dgu.dtype)
        dgu[rows, :] = joined
        part_ref[cc, xx, yy] = (
            lax.dot_general(
                joined, wgu_ref[...], (((1,), (1,)), ((), ())), preferred_element_type=jnp.float32
            )
            .astype(part_ref.dtype)
            .reshape(deep, count, wide)
        )

    def weight_grads(place):
        feed(FEED[3][place])
        if place:
            return
        span = 2 * LANES

        @pl.loop(0, wide // span)
        def _(i):
            cols = pl.ds(pl.multiple_of(i * span, span), span)
            dffn[cols, :inner_cols] = lax.dot_general(
                rows_ref[:, cols], dgu[...], (((0,), (0,)), ((), ())),
                preferred_element_type=jnp.float32,
            ).astype(dffn.dtype)
            dffn[cols, inner_cols:] = lax.dot_general(
                flat_down[:, :, :, :, :, cols].reshape(every, span), hidden_ref[...],
                (((0,), (0,)), ((), ())),
                preferred_element_type=jnp.float32,
            ).astype(dffn.dtype)

        home = pltpu.make_async_copy(dffn, ffn_out, local.at[1])
        home.start()
        local_copies.append(home)

    grad_two = summed[...]
    scatter_body(nd, ns, links, part_ref, summed, scratch[:-2], weight_grads)
    grad_one = grad_two + norm_back(summed[...], one_ref[...], gain_ref[pl.ds(0, 1), :], 0)
    one_out[st] = grad_one.astype(one_out.dtype)
    low[...] = grad_one.astype(low.dtype)
    made = [links.copy(low, one_out.at[st], *peer) for peer in state_peers]
    for copy in made:
        copy.wait_recv()
    feed(len(queue))
    for copy in swapped:
        copy.wait_recv()
    for copy in local_copies:
        copy.wait()
    links.finish()


def slots_back(part, table, two, one, gain, wd, wgu, gu, hidden, rows, width, units, number):
    nd, ns = lax.axis_size("dp"), lax.axis_size("state")
    deep, across = nd // 2, ns // 2
    count, wide = two.shape
    kind = part.dtype
    cols = wgu.shape[1] + wd.shape[1]
    copies = 2 * scatter_copies(nd, ns) + gather_copies(nd, ns) + (nd - 1) * CHUNKS + ns - 1
    vmem = pl.BlockSpec(memory_space=pltpu.VMEM)
    hbm = pl.BlockSpec(memory_space=pl.ANY)
    six = (2, across, 2, deep, count, wide)
    out = pl.pallas_call(
        functools.partial(slots_back_kernel, nd, ns, width, units),
        out_shape=[
            jax.ShapeDtypeStruct((ns, count, wide), kind),
            jax.ShapeDtypeStruct(table.shape, kind),
            jax.ShapeDtypeStruct((wide, cols), kind),
            jax.ShapeDtypeStruct((2, wide), jnp.float32),
        ],
        in_specs=[hbm, hbm] + [vmem] * 8,
        out_specs=[vmem, hbm, hbm, vmem],
        scratch_shapes=[
            pltpu.VMEM(six, kind),
            pltpu.VMEM((count, wide), jnp.float32),
            pltpu.VMEM((count, wide), kind),
            pltpu.VMEM(six, kind),
            pltpu.VMEM((nd * ns * count, wgu.shape[1]), kind),
            pltpu.VMEM((wide, cols), kind),
            pltpu.SemaphoreType.DMA((3,)),
        ]
        + scatter_scratch(nd, ns, count, wide, kind)
        + [pltpu.SemaphoreType.DMA((copies,)), pltpu.SemaphoreType.DMA((copies,))],
        compiler_params=pltpu.CompilerParams(
            collective_id=number, has_side_effects=True, vmem_limit_bytes=58 * 2**20
        ),
        cost_estimate=pl.CostEstimate(
            flops=8 * rows.size * cols, bytes_accessed=100 * part.size, transcendentals=0
        ),
    )(part.reshape(six), table, two, one, gain, wd, wgu, gu, hidden, rows)
    return (out[0].reshape(ns * count, wide),) + tuple(out[1:])


def rows_back_kernel(
    nd, ns, width, in_ref, stream_ref, gain_ref, more_ref, out_ref, gain_out, rc, acc, rx, fin, low,
    sends, recvs
):
    dp, st, z, y, x, c = places(nd, ns)
    across = ns // 2
    tokens = in_ref.shape[1]
    own = in_ref.shape[0] // nd
    part = tokens // ns
    to_core = (dp, st + 1 - 2 * c)
    dp_peers = [(lax.rem(dp + k, nd), st) for k in range(1, nd)]
    peers = dp_peers + [(dp, lax.rem(x + k, across) * 2 + c) for k in range(1, across)]
    greet(peers + [to_core])
    links = Links(sends, recvs)

    def x_at(k):
        return lax.rem(x + k, across)

    def rows_of(owner):
        return pl.ds(pl.multiple_of(owner * own, own), own)

    def block(k, kx, cc):
        start = (x_at(kx) * 2 + cc) * part
        return in_ref.at[pl.ds(k * own, own), pl.ds(pl.multiple_of(start, part), part)]

    def place(row, share):
        return out_ref.at[:, pl.ds(pl.multiple_of(row * tokens + share * part, part), part)]

    def add(sources, target):
        @pl.loop(0, own // 32)
        def _(i):
            rows = pl.ds(pl.multiple_of(i * 32, 32), 32)
            found = sources[0][rows, :].astype(jnp.float32)
            for source in sources[1:]:
                found += source[rows, :].astype(jnp.float32)
            target[rows, :] = found.astype(target.dtype)

    core, across_x = {}, {}
    for kx in list(range(1, across)) + [0]:
        for k in range(nd):
            core[k, kx] = links.copy(block(k, kx, 1 - c), rc.at[k, kx], *to_core)
    for kx in range(1, across):
        for k in range(nd):
            core[k, kx].wait_recv()
            add([block(k, kx, c), rc.at[k, kx]], acc.at[k, kx - 1])
            across_x[k, kx] = links.copy(
                acc.at[k, kx - 1], rx.at[k, kx - 1], dp, x_at(kx) * 2 + c
            )
    for k in range(nd):
        core[k, 0].wait_recv()
        sources = [block(k, 0, c), rc.at[k, 0]]
        for kx in range(1, across):
            across_x[k, kx].wait_recv()
            sources.append(rx.at[k, kx - 1])
        add(sources, fin.at[pl.ds(k * own, own), :])

    step = 32
    pieces = in_ref.shape[0] // step

    def at(i):
        return pl.ds(pl.multiple_of(i * step, step), step)

    def gather_sums(i, carry):
        square, inner = carry
        values = stream_ref[at(i), :].astype(jnp.float32)
        scaled = fin[at(i), :] * gain_ref[at(i), :] * values
        square = square + jnp.sum(values * values, axis=0, keepdims=True)
        return square, inner + jnp.sum(scaled, axis=0, keepdims=True)

    none = jnp.zeros((1, part), jnp.float32)
    square, inner = lax.fori_loop(0, pieces, gather_sums, (none, none))
    root = lax.rsqrt(square * (1.0 / width) + NORM_EPS)
    inner = inner * (1.0 / width) * root * root * root

    @pl.loop(0, pieces)
    def _(i):
        values = stream_ref[at(i), :].astype(jnp.float32)
        grad = fin[at(i), :]
        gain_out[at(i), :] = jnp.sum(grad * values * root, axis=1, keepdims=True)
        found = grad * gain_ref[at(i), :] * root - values * inner + more_ref[at(i), :]
        low[at(i), :] = found.astype(low.dtype)

    swapped = [links.copy(low.at[rows_of(p[0]), :], place(dp, st), *p) for p in dp_peers]
    place(dp, st)[...] = low[rows_of(dp), :]
    later, last = {}, []
    for k in range(nd):
        row = lax.rem(dp - k + nd, nd)
        if k:
            swapped[k - 1].wait_recv()
        for kx in range(1, across):
            later[k, kx] = links.copy(place(row, st), place(row, st), dp, x_at(kx) * 2 + c)
        last.append(links.copy(place(row, st), place(row, st), *to_core))
    for k in range(nd):
        row = lax.rem(dp - k + nd, nd)
        for kx in range(1, across):
            later[k, kx].wait_recv()
            share = lax.rem(x - kx + across, across) * 2 + c
            last.append(links.copy(place(row, share), place(row, share), *to_core))
    for made in last:
        made.wait_recv()
    links.finish()


def rows_back(values, stream, gain, more, width, number):
    nd, ns = lax.axis_size("dp"), lax.axis_size("state")
    across = ns // 2
    wide, tokens = values.shape
    own, part = wide // nd, tokens // ns
    copies = nd * across + nd * (across - 1) + nd - 1 + nd * across + nd * (across - 1)
    vmem = pl.BlockSpec(memory_space=pltpu.VMEM)
    kind = values.dtype
    return pl.pallas_call(
        functools.partial(rows_back_kernel, nd, ns, width),
        out_shape=[
            jax.ShapeDtypeStruct((own, nd * tokens), kind),
            jax.ShapeDtypeStruct((wide, 1), jnp.float32),
        ],
        in_specs=[vmem] * 4,
        out_specs=[vmem] * 2,
        scratch_shapes=[
            pltpu.VMEM((nd, across, own, part), kind),
            pltpu.VMEM((nd, across - 1, own, part), kind),
            pltpu.VMEM((nd, across - 1, own, part), kind),
            pltpu.VMEM((wide, part), jnp.float32),
            pltpu.VMEM((wide, part), kind),
            pltpu.SemaphoreType.DMA((copies,)),
            pltpu.SemaphoreType.DMA((copies,)),
        ],
        compiler_params=pltpu.CompilerParams(
            collective_id=number, has_side_effects=True, vmem_limit_bytes=48 * 2**20
        ),
        cost_estimate=pl.CostEstimate(
            flops=0, bytes_accessed=60 * values.size, transcendentals=0
        ),
    )(values, stream, gain, more)


def state_sum_kernel(nd, ns, in_ref, out_ref, land, sends, recvs):
    dp, st = lax.axis_index("dp"), lax.axis_index("state")
    peers = [(dp, lax.rem(st + k, ns)) for k in range(1, ns)]
    greet(peers)
    links = Links(sends, recvs)
    made = [
        links.copy(in_ref.at[there[1]], land.at[k], *there) for k, there in enumerate(peers)
    ]
    found = in_ref[st].astype(jnp.float32)
    for k in range(ns - 1):
        made[k].wait_recv()
        found += land[k].astype(jnp.float32)
    out_ref[...] = found
    links.finish()


def state_sum(values, number):
    nd, ns = lax.axis_size("dp"), lax.axis_size("state")
    rows, wide = values.shape[0] // ns, values.shape[1]
    vmem = pl.BlockSpec(memory_space=pltpu.VMEM)
    return pl.pallas_call(
        functools.partial(state_sum_kernel, nd, ns),
        out_shape=jax.ShapeDtypeStruct((rows, wide), jnp.float32),
        in_specs=[vmem],
        out_specs=vmem,
        scratch_shapes=[
            pltpu.VMEM((ns - 1, rows, wide), values.dtype),
            pltpu.SemaphoreType.DMA((ns - 1,)),
            pltpu.SemaphoreType.DMA((ns - 1,)),
        ],
        compiler_params=pltpu.CompilerParams(collective_id=number, has_side_effects=True),
    )(values.reshape(ns, rows, wide))


def on_device(
    token_ids,
    doc_starts,
    loss_positions,
    loss_targets,
    owners,
    in_weight,
    out_weight,
    table_weight,
    gain_weight,
    in_first,
    out_first,
    table_first,
    gain_first,
    in_second,
    out_second,
    table_second,
    gain_second,
    in_average,
    out_average,
    table_average,
    gain_average,
):
    f32 = jnp.float32
    bf16 = jnp.bfloat16
    nd = lax.axis_size("dp")
    ns = lax.axis_size("state")
    me_dp = lax.axis_index("dp")
    me_state = lax.axis_index("state")
    tokens = token_ids.shape[1]
    slots = loss_positions.shape[1]
    capacity = in_weight.shape[1]
    block_rows = in_weight.shape[2]
    block_count = owners.shape[0]
    width = block_rows * block_count
    own = capacity * block_rows
    wide = nd * own
    key_share = KEY_DIM // ns
    heads = HEADS // ns
    key_cols = HEADS * key_share
    value_width = heads * VAL_DIM
    mixer_cols = 2 * key_cols + value_width
    units = out_weight.shape[3] - value_width
    unit_part = units // nd
    vocab_share = table_weight.shape[3]
    vocab_part = -(-vocab_share // (nd * LANES)) * LANES
    quarter = tokens // ns
    slot_part = slots // ns

    held_all = jnp.sum((owners[None, :] == jnp.arange(nd)[:, None]).astype(jnp.int32), axis=1)
    occupied_all = jnp.arange(capacity)[None, :] < held_all[:, None]
    held = jnp.sum((owners == me_dp).astype(jnp.int32))
    occupied_here = jnp.arange(capacity) < held
    rows_here = jnp.repeat(occupied_here, block_rows)[:, None]

    def lowered(array):
        return jnp.where(rows_here, array[0].reshape(own, -1), 0.0).astype(bf16)

    in_own = lowered(in_weight)
    out_own = lowered(out_weight)
    table_own = lowered(table_weight)

    def in_rows(flat):
        flat = jnp.pad(flat, (0, -flat.shape[0] % (16 * LANES)))
        return flat.reshape(-1, LANES)

    key_part = heads * key_share
    keys_sent = in_own[:, : 2 * key_cols].reshape(own, 2, ns, key_part)
    keys_sent = keys_sent.transpose(2, 0, 1, 3).reshape(ns, own, 2 * key_part)
    rest_sent = jnp.concatenate(
        [in_own[:, 2 * key_cols : mixer_cols], out_own[:, :value_width]], axis=1
    )
    table_padded = jnp.pad(table_own, ((0, 0), (0, nd * vocab_part - vocab_share)))

    def by_part(columns, parts):
        return columns.reshape(own, nd, parts)

    def zeros(parts):
        return jnp.zeros((own, nd, parts), bf16)

    gu_cols = -(-2 * unit_part // LANES) * LANES
    down_cols = -(-unit_part // LANES) * LANES
    parts_sent = jnp.concatenate(
        [
            by_part(in_own[:, mixer_cols : mixer_cols + units], unit_part),
            by_part(in_own[:, mixer_cols + units :], unit_part),
            zeros(gu_cols - 2 * unit_part),
            by_part(out_own[:, value_width:], unit_part),
            zeros(down_cols - unit_part),
        ],
        axis=2,
    ).transpose(1, 0, 2)
    small, gains_all, stream, keys_all, rest_all, parts_all = front(
        in_rows(jnp.concatenate([token_ids[0], loss_targets[0]])),
        in_rows(gain_weight.astype(bf16).reshape(-1)),
        table_padded,
        keys_sent,
        rest_sent,
        parts_sent,
        tokens,
        vocab_share,
        1,
    )
    small = small.reshape(nd, -1)
    ids_all = small[:, :tokens]
    slot_targets = small[:, tokens : tokens + slots].reshape(nd // 2, 2, ns // 2, 2, slot_part)
    targets_all = slot_targets.transpose(3, 2, 1, 0, 4).reshape(-1)
    gains_all = gains_all.reshape(nd, -1)[:, : capacity * 4 * block_rows].astype(f32)
    gains_all = gains_all.reshape(nd * capacity, 4, block_rows)
    gains = jnp.where(occupied_all.reshape(-1)[:, None, None], gains_all, 0.0)
    gains = gains.transpose(1, 0, 2).reshape(4, wide)
    index = slot_index(owners, capacity)
    head_gain = lax.dynamic_slice_in_dim(
        gains_all[index][:, 1].reshape(width), me_state * value_width, value_width
    )
    live = (targets_all >= 0).astype(f32)
    count = jnp.sum(live)
    local_ids = ids_all.reshape(-1) - me_state * vocab_share
    hit = jnp.arange(vocab_share)[:, None] == local_ids[None, :]
    stream_mine = lax.dynamic_slice_in_dim(stream, me_state * quarter, quarter, axis=1)

    qcols = heads * KEY_DIM
    keys_all = keys_all.reshape(ns, wide, 2 * key_part)
    w_q = keys_all[:, :, :key_part].transpose(1, 0, 2).reshape(wide, qcols)
    w_f = keys_all[:, :, key_part:].transpose(1, 0, 2).reshape(wide, qcols)
    rest_all = rest_all.reshape(wide, 2 * value_width)
    w_v = rest_all[:, :value_width]
    w_o = rest_all[:, value_width:]
    w_fv = jnp.concatenate([w_f, w_v], axis=1)
    w_qfv = jnp.concatenate([w_q, w_fv], axis=1)
    parts_all = parts_all.reshape(wide, -1)
    w_gu = parts_all[:, :gu_cols]
    w_d = parts_all[:, gu_cols:]
    table_padded, stream = lax.optimization_barrier((table_padded, stream))
    table = swap_dp(spread_columns(table_padded, nd)).reshape(wide, vocab_part)

    positions = loss_positions[0]
    pick_hit = positions[:, None] == jnp.arange(tokens)[None, :]
    pick = pick_hit.astype(f32)
    pick_low = pick_hit.astype(bf16)
    documents = document_ids(doc_starts[0], tokens)
    doc_at = jnp.sum(jnp.where(pick_hit, documents[None, :], 0), axis=1)
    allowed = (positions[:, None] >= jnp.arange(tokens)[None, :]) & (
        doc_at[:, None] == documents[None, :]
    )

    def tall_norm(values, gain):
        mean = jnp.sum(values * values, axis=0, keepdims=True) * (1.0 / width)
        return values * lax.rsqrt(mean + NORM_EPS) * gain[:, None]

    normed_one = tall_norm(stream.astype(f32), gains[0]).astype(bf16)
    normed_at = times_right(pick_low, normed_one).astype(bf16)
    stream_at = times_right(
        lax.dynamic_slice_in_dim(pick_low, me_state * slot_part, slot_part), stream
    )
    forget_value = times_left(normed_one, w_fv)
    query_pre = times_plain(normed_at, w_q)
    query, back_query = jax.vjp(jax.nn.silu, query_pre)
    (key_gate, log_forget), back_gates = jax.vjp(forget_gates, forget_value[:, :qcols])

    def mix(query_in, key_in, forget_in, value_in):
        return slot_mixer(query_in, key_in, forget_in, value_in, pick, allowed, heads, key_part)

    mixed, back_mix = jax.vjp(
        mix,
        query.astype(bf16).astype(f32),
        key_gate.astype(bf16).astype(f32),
        log_forget,
        forget_value[:, qcols:].astype(bf16).astype(f32),
    )

    def head_norm(mixed_in, gain_in):
        return rms_norm(
            mixed_in.reshape(slots, heads, VAL_DIM), gain_in.reshape(heads, VAL_DIM), VAL_DIM
        ).reshape(slots, value_width)

    gated_f, back_head = jax.vjp(head_norm, mixed, head_gain)
    gated = gated_f.astype(bf16)
    stream_one = stream_at + state_sum(times_right(gated, w_o).astype(bf16), 2)

    def wide_norm(values, gain):
        return rms_norm(values, gain, width)

    normed_two = wide_norm(stream_one, gains[2])
    rows_two = gather_all(normed_two.astype(bf16), 3)
    gate_up = times_plain(rows_two, w_gu)
    hidden = swiglu(gate_up, unit_part, down_cols).astype(bf16)
    stream_two = stream_one + scatter_all(times_right(hidden, w_d).astype(bf16), 4)
    normed_three = wide_norm(stream_two, gains[3])
    rows_three = gather_all(normed_three.astype(bf16), 5)

    logits = times_plain(rows_three, table)
    column = jnp.arange(vocab_part)[None, :] + me_dp * vocab_part
    target_hit = (column + me_state * vocab_share == targets_all[:, None]) & (
        column < vocab_share
    )
    logits = jnp.where(column < vocab_share, logits, -1e30)
    top_here = jnp.max(logits, axis=1)
    sum_here = jnp.sum(jnp.exp(logits - top_here[:, None]), axis=1)
    picked_here = jnp.sum(jnp.where(target_hit, logits, 0.0), axis=1)
    shares = small_gather(
        [jnp.stack([top_here, sum_here, picked_here]).reshape(-1, LANES)], True, 6
    )[0].reshape(nd * ns, 3, -1)
    top = jnp.max(shares[:, 0], axis=0)
    lse = top + jnp.log(jnp.sum(shares[:, 1] * jnp.exp(shares[:, 0] - top[None]), axis=0))
    loss_sum = jnp.sum((lse - jnp.sum(shares[:, 2], axis=0)) * live)
    probs = jnp.exp(logits - lse[:, None])
    dlogits = ((probs - target_hit.astype(f32)) * (live / count)[:, None]).astype(bf16)
    grad_table_part = times_left(rows_three, dlogits).astype(bf16)
    grad_one, grad_table_back, grad_ffn, gain_pair = slots_back(
        times_right(dlogits, table).astype(bf16),
        grad_table_part.reshape(nd, own, vocab_part),
        stream_two,
        stream_one,
        gains[2:],
        w_d,
        w_gu,
        gate_up,
        hidden,
        rows_two,
        width,
        unit_part,
        7,
    )
    grad_gain_three, grad_gain_four = gain_pair
    grad_table_own = join_columns(grad_table_back)[:, :vocab_share].astype(f32)
    grad_ffn = swap_dp(grad_ffn.reshape(nd, own, gu_cols + down_cols))

    grad_gated = times_plain(grad_one, w_o)
    grad_o_own = lax.psum_scatter(
        times_left(grad_one, gated).astype(bf16), "dp", scatter_dimension=0, tiled=True
    )
    grad_mixed, grad_gain_two = back_head(grad_gated)
    grad_query, grad_key, grad_forget, grad_value = back_mix(
        grad_mixed.astype(bf16).astype(f32)
    )
    (grad_query_pre,) = back_query(grad_query)
    grad_query_pre = times_left(pick, grad_query_pre)
    (grad_forget_pre,) = back_gates((grad_key, grad_forget))
    grad_qfv = jnp.concatenate([grad_query_pre, grad_forget_pre, grad_value], axis=1).astype(bf16)
    grad_qfv, grad_ffn = lax.optimization_barrier((grad_qfv, grad_ffn))
    pick_mine = lax.dynamic_slice_in_dim(pick_low, me_state * quarter, quarter, axis=1)
    embed, grad_gain_one = rows_back(
        times_right(w_qfv, grad_qfv).astype(bf16),
        stream_mine,
        gains[0][:, None],
        times_left(grad_one, pick_mine),
        width,
        8,
    )
    grad_gain_one = grad_gain_one[:, 0]
    grad_w_qfv = times_plain(normed_one, grad_qfv).astype(bf16)

    def sum_dp(values):
        return lax.psum_scatter(values, "dp", scatter_dimension=0, tiled=True)

    grad_qfv_own = sum_dp(grad_w_qfv)
    grad_lookup = times_right(embed, hit.astype(bf16))
    grad_qfv_own, grad_lookup = lax.optimization_barrier((grad_qfv_own, grad_lookup))
    own_table = grad_table_own + grad_lookup

    grad_keys = grad_qfv_own[:, : 2 * qcols].reshape(own, 2, ns, key_part)
    grad_keys = grad_keys.transpose(2, 0, 1, 3).reshape(ns, own, 2 * key_part)
    grad_keys = lax.all_to_all(grad_keys, "state", split_axis=0, concat_axis=0, tiled=True)
    grad_keys = grad_keys.reshape(ns, own, 2, key_part).transpose(1, 2, 0, 3)
    grad_gate = grad_ffn[:, :, :unit_part]
    grad_up = grad_ffn[:, :, unit_part : 2 * unit_part]
    grad_down = grad_ffn[:, :, gu_cols : gu_cols + unit_part]
    own_in = jnp.concatenate(
        [
            grad_keys.reshape(own, 2 * key_cols),
            grad_qfv_own[:, 2 * qcols :],
            join_columns(grad_gate),
            join_columns(grad_up),
        ],
        axis=1,
    ).astype(f32)
    own_out = jnp.concatenate(
        [grad_o_own, join_columns(grad_down)],
        axis=1,
    ).astype(f32)

    head_full = lax.dynamic_update_slice_in_dim(
        jnp.zeros((width,), f32), grad_gain_two, me_state * value_width, 0
    )
    gain_parts = jnp.concatenate([grad_gain_one, grad_gain_three, grad_gain_four, head_full])
    gain_parts = small_gather([in_rows(gain_parts.astype(bf16))], True, 11)[0]
    gain_sums = jnp.sum(gain_parts.reshape(nd * ns, -1)[:, : 3 * wide + width].astype(f32), axis=0)
    head_slots = (
        jnp.zeros((nd * capacity, block_rows), f32)
        .at[index]
        .set(gain_sums[3 * wide :].reshape(block_count, block_rows))
    )
    gain_slots = gain_sums[: 3 * wide].reshape(3, nd * capacity, block_rows)
    gain_slots = jnp.stack([gain_slots[0], head_slots, gain_slots[1], gain_slots[2]], axis=1)
    own_gain = lax.dynamic_slice_in_dim(gain_slots, me_dp * capacity, capacity)

    squares = jnp.sum(own_in * own_in) + jnp.sum(own_out * own_out) + jnp.sum(own_table * own_table)
    squares = small_gather([jnp.full((8, LANES), squares)], True, 10)[0][:, 0, 0]
    squares_all = jnp.sum(squares) + jnp.sum(gain_sums * gain_sums)
    grad_norm = jnp.sqrt(squares_all)
    scale = jnp.minimum(1.0, CLIP_NORM / (grad_norm + 1e-06))
    occupied = occupied_here.astype(f32)
    new_in = adam_blocks(
        in_weight,
        in_first,
        in_second,
        in_average,
        own_in.reshape(in_weight.shape),
        scale,
        LEARN_RATE,
        WEIGHT_DECAY,
        occupied,
    )
    new_out = adam_blocks(
        out_weight,
        out_first,
        out_second,
        out_average,
        own_out.reshape(out_weight.shape),
        scale,
        LEARN_RATE,
        WEIGHT_DECAY,
        occupied,
    )
    new_table = adam_blocks(
        table_weight,
        table_first,
        table_second,
        table_average,
        own_table.reshape(table_weight.shape),
        scale,
        LEARN_RATE,
        WEIGHT_DECAY,
        occupied,
    )
    new_gain = adam_update(
        gain_weight,
        gain_first,
        gain_second,
        gain_average,
        own_gain,
        scale,
        GAIN_RATE,
        0.0,
        occupied[:, None, None],
    )
    return (
        new_in[0],
        new_out[0],
        new_table[0],
        new_gain[0],
        new_in[1],
        new_out[1],
        new_table[1],
        new_gain[1],
        new_in[2],
        new_out[2],
        new_table[2],
        new_gain[2],
        new_in[3],
        new_out[3],
        new_table[3],
        new_gain[3],
        loss_sum,
        count,
        grad_norm,
    )


def solution(mesh):
    return jax.shard_map(
        on_device,
        mesh=mesh,
        in_specs=(
            P("dp", None),
            P("dp", None),
            P("dp", None),
            P("dp", None),
            P(),
            P("state", "dp", None, None),
            P("state", "dp", None, None),
            P("state", "dp", None, None),
            P("dp", None, None),
            P("state", "dp", None, None),
            P("state", "dp", None, None),
            P("state", "dp", None, None),
            P("dp", None, None),
            P("state", "dp", None, None),
            P("state", "dp", None, None),
            P("state", "dp", None, None),
            P("dp", None, None),
            P("state", "dp", None, None),
            P("state", "dp", None, None),
            P("state", "dp", None, None),
            P("dp", None, None),
        ),
        out_specs=(
            P("state", "dp", None, None),
            P("state", "dp", None, None),
            P("state", "dp", None, None),
            P("dp", None, None),
            P("state", "dp", None, None),
            P("state", "dp", None, None),
            P("state", "dp", None, None),
            P("dp", None, None),
            P("state", "dp", None, None),
            P("state", "dp", None, None),
            P("state", "dp", None, None),
            P("dp", None, None),
            P("state", "dp", None, None),
            P("state", "dp", None, None),
            P("state", "dp", None, None),
            P("dp", None, None),
            P(),
            P(),
            P(),
        ),
        check_vma=False,
    )
```

```python
import functools

import jax
import jax.numpy as jnp
from jax import lax
from jax.experimental import pallas as pl
from jax.experimental.pallas import tpu as pltpu
from jax.sharding import PartitionSpec as P

HEADS = 16
KEY_DIM = 128
GROUP = 128
STEP = 5
VAL_DIM = 128


NORM_EPS = 1e-06
LOWER_BOUND = 0.9
CLIP_NORM = 0.02
BETA_FIRST = 0.5
BETA_SECOND = 0.5
ADAM_EPS = 1e-08
LEARN_RATE = 0.02
GAIN_RATE = 0.2
WEIGHT_DECAY = 0.1
AVERAGE_DECAY = 0.9
FULL_PRECISION = lax.Precision.HIGHEST
LANES = 128
CHUNKS = 5
FEED = ((2, 3, 3), (6, 4), 6, (5, 6, 0))


def rms_norm(values, gain, width):
    mean = jnp.sum(values * values, axis=-1, keepdims=True) * (1.0 / width)
    return values * lax.rsqrt(mean + NORM_EPS) * gain


def forget_gates(forget_pre):
    key_gate = (1.0 - LOWER_BOUND) * jax.nn.sigmoid(-forget_pre)
    log_forget = jnp.log(LOWER_BOUND + (1.0 - LOWER_BOUND) * jax.nn.sigmoid(forget_pre))
    return key_gate, log_forget


def slot_mixer(query, key_gate, log_forget, values, pick, allowed, heads, key_part):
    slots = query.shape[0]
    tokens = key_gate.shape[0]
    blocks = tokens // GROUP
    order = jnp.arange(GROUP)
    lower = (order[:, None] >= order[None, :]).astype(jnp.float32)
    number = jnp.arange(blocks)
    before = (number[:, None] > number[None, :]).astype(jnp.float32)
    inside = jnp.einsum(
        "ts,bsk->btk", lower, log_forget.reshape(blocks, GROUP, -1), precision=FULL_PRECISION
    )
    total = inside[:, -1]
    offset = jnp.dot(before, total, precision=FULL_PRECISION)
    ends = offset + total
    along = (inside + offset[:, None]).reshape(tokens, -1)
    at_slots = jnp.dot(pick, along, precision=FULL_PRECISION)
    key_decay = key_gate * jnp.exp(total[:, None] - inside).reshape(tokens, -1)
    grown = query[None] * jnp.exp(jnp.minimum(at_slots[None] - ends[:, None], 16.0))
    key_decay = key_decay.reshape(blocks, GROUP, heads * KEY_DIM)
    column = jnp.arange(heads * KEY_DIM)
    of_head = (column % key_part) // (key_part // heads) == jnp.arange(heads)[:, None]
    grown = jnp.where(of_head[:, None, None], grown[None], 0.0)
    scores = jnp.einsum("hbnk,bgk->hnbg", grown, key_decay, precision=FULL_PRECISION)
    scores = jnp.where(allowed[None], scores.reshape(heads, slots, tokens), 0.0)
    mixed = jnp.einsum(
        "hns,shv->nhv", scores, values.reshape(tokens, heads, VAL_DIM), precision=FULL_PRECISION
    )
    return mixed.reshape(slots, -1)


def document_ids(starts, length):
    return jnp.sum((jnp.arange(length)[:, None] >= starts[None, :]).astype(jnp.int32), axis=1) - 1


def slot_index(owners, capacity):
    order = jnp.arange(owners.shape[0])
    earlier = (owners[:, None] == owners[None, :]) & (order[None, :] < order[:, None])
    ranks = jnp.sum(earlier.astype(jnp.int32), axis=1)
    return owners * capacity + ranks


def adam_update(weight, first, second, average, grad, scale, rate, decay, occupied):
    clipped = scale * grad
    first_new = BETA_FIRST * first + (1.0 - BETA_FIRST) * clipped
    second_new = BETA_SECOND * second + (1.0 - BETA_SECOND) * clipped * clipped
    first_hat = first_new / (1.0 - BETA_FIRST**STEP)
    second_hat = second_new / (1.0 - BETA_SECOND**STEP)
    weight_new = weight - rate * (first_hat / (jnp.sqrt(second_hat) + ADAM_EPS) + decay * weight)
    average_new = AVERAGE_DECAY * average + (1.0 - AVERAGE_DECAY) * weight_new
    return (
        weight_new * occupied,
        first_new * occupied,
        second_new * occupied,
        average_new * occupied,
    )


def adam_kernel(
    rate, decay, scale_ref, held_ref, weight, first, second, average, grad,
    weight_out, first_out, second_out, average_out
):
    occupied = held_ref[pl.program_id(0)]
    found = adam_update(
        weight[...],
        first[...],
        second[...],
        average[...],
        grad[...].astype(jnp.float32),
        scale_ref[0],
        rate,
        decay,
        occupied,
    )
    for out, value in zip((weight_out, first_out, second_out, average_out), found):
        out[...] = value


def adam_blocks(weight, first, second, average, grad, scale, rate, decay, occupied):
    capacity, block_rows, cols = weight.shape[1:]
    rows = 32
    block = pl.BlockSpec((1, 1, rows, cols), lambda i, j: (0, i, j, 0))
    scalar = pl.BlockSpec(memory_space=pltpu.SMEM)
    return pl.pallas_call(
        functools.partial(adam_kernel, rate, decay),
        grid=(capacity, block_rows // rows),
        out_shape=[jax.ShapeDtypeStruct(weight.shape, weight.dtype)] * 4,
        in_specs=[scalar, scalar] + [block] * 5,
        out_specs=[block] * 4,
        compiler_params=pltpu.CompilerParams(vmem_limit_bytes=48 * 2**20),
    )(scale.reshape(1), occupied, weight, first, second, average, grad)


def times_plain(left, right):
    return jnp.dot(left, right, preferred_element_type=jnp.float32)


def times_right(left, right):
    return lax.dot_general(
        left, right, (((1,), (1,)), ((), ())), preferred_element_type=jnp.float32
    )


def times_left(left, right):
    return lax.dot_general(
        left, right, (((0,), (0,)), ((), ())), preferred_element_type=jnp.float32
    )


def swiglu(joined, units, cols):
    gate = joined[:, :units]
    up = joined[:, units : 2 * units]
    return jnp.pad(jax.nn.silu(gate) * up, ((0, 0), (0, cols - units)))


EVERY = ("dp", "state")


def gather_state(values, axis=0):
    return lax.all_gather(values, "state", axis=axis, tiled=True)


def scatter_state(values, axis=0):
    return lax.psum_scatter(values, "state", scatter_dimension=axis, tiled=True)


def swap_dp(values):
    return lax.all_to_all(values, "dp", split_axis=0, concat_axis=0, tiled=True)


def spread_columns(own, parts):
    return own.reshape(own.shape[0], parts, -1).transpose(1, 0, 2)


def join_columns(split):
    return split.transpose(1, 0, 2).reshape(split.shape[1], -1)


MESH = pl.DeviceIdType.MESH


class Links:
    def __init__(self, sends, recvs):
        self.sends, self.recvs, self.used, self.open = sends, recvs, 0, []

    def copy(self, src, dst, dp, state):
        number = self.used
        self.used += 1
        made = pltpu.make_async_remote_copy(
            src_ref=src,
            dst_ref=dst,
            send_sem=self.sends.at[number],
            recv_sem=self.recvs.at[number],
            device_id=(dp, state),
            device_id_type=MESH,
        )
        made.start()
        self.open.append(made)
        return made

    def settle(self, copies):
        for made in copies:
            made.wait_send()
        self.open = [made for made in self.open if not any(made is one for one in copies)]

    def finish(self):
        for made in self.open:
            made.wait_send()


def nothing(place):
    del place


def greet(peers):
    barrier = pltpu.get_barrier_semaphore()
    for dp, state in peers:
        pl.semaphore_signal(barrier, inc=1, device_id=(dp, state), device_id_type=MESH)
    pl.semaphore_wait(barrier, len(peers))


def places(nd, ns):
    dp, st = lax.axis_index("dp"), lax.axis_index("state")
    return dp, st, lax.div(dp, 2), lax.rem(dp, 2), lax.div(st, 2), lax.rem(st, 2)


def near_peers(nd, ns):
    dp, st, z, y, x, c = places(nd, ns)
    deep, across = nd // 2, ns // 2
    peers = [(lax.rem(z + k, deep) * 2 + y, st) for k in range(1, deep)]
    peers.append((dp + 1 - 2 * y, st))
    peers += [(dp, lax.rem(x + k, across) * 2 + c) for k in range(1, across)]
    peers.append((dp, st + 1 - 2 * c))
    return peers


def add_up(parts):
    found = parts[0]
    for part in parts[1:]:
        found = found + part
    return found


def add_exponentials(parts):
    top = parts[0][0]
    for part in parts[1:]:
        top = jnp.maximum(top, part[0])
    total = add_up([part[1] * jnp.exp(part[0] - top) for part in parts])
    return jnp.stack([top, total, add_up([part[2] for part in parts])])


def combine_kernel(nd, ns, combine, in_ref, out_ref, near, far, sends, recvs):
    dp, st, z, y, x, c = places(nd, ns)
    deep = nd // 2
    plane = []
    for a in range(2):
        for b in range(ns):
            if a or b:
                plane.append((z * 2 + lax.rem(y + a, 2), lax.rem(st + b, ns)))
    line = [(lax.rem(z + k, deep) * 2 + y, st) for k in range(1, deep)]
    greet(plane + line)
    links = Links(sends, recvs)
    me = y * ns + st
    near[me] = in_ref[...]
    made = [links.copy(in_ref, near.at[me], *peer) for peer in plane]
    for copy in made:
        copy.wait_recv()
    far[z] = combine([near[i] for i in range(2 * ns)])
    made = [links.copy(far.at[z], far.at[z], *peer) for peer in line]
    for copy in made:
        copy.wait_recv()
    out_ref[...] = combine([far[i] for i in range(deep)])
    links.finish()


def combine_all(values, combine, number):
    nd, ns = lax.axis_size("dp"), lax.axis_size("state")
    copies = 2 * ns - 1 + nd // 2 - 1
    vmem = pl.BlockSpec(memory_space=pltpu.VMEM)
    return pl.pallas_call(
        functools.partial(combine_kernel, nd, ns, combine),
        out_shape=jax.ShapeDtypeStruct(values.shape, values.dtype),
        in_specs=[vmem],
        out_specs=vmem,
        scratch_shapes=[
            pltpu.VMEM((2 * ns,) + values.shape, values.dtype),
            pltpu.VMEM((nd // 2,) + values.shape, values.dtype),
            pltpu.SemaphoreType.DMA((copies,)),
            pltpu.SemaphoreType.DMA((copies,)),
        ],
        compiler_params=pltpu.CompilerParams(collective_id=number, has_side_effects=True),
    )(values)


def gather_all_kernel(nd, ns, in_ref, out_ref, sends, recvs):
    greet(near_peers(nd, ns))
    links = Links(sends, recvs)
    gather_body(nd, ns, links, in_ref, out_ref)
    links.finish()


def gather_body(nd, ns, links, in_ref, out_ref, meanwhile=nothing):
    dp, st, z, y, x, c = places(nd, ns)
    deep, across = nd // 2, ns // 2
    half = in_ref.shape[1] // 2
    cols = (pl.ds(0, half), pl.ds(half, half))
    to_y = (dp + 1 - 2 * y, st)
    to_core = (dp, st + 1 - 2 * c)
    other_y = 1 - y

    def x_at(k):
        return lax.rem(x + k, across)

    def to_x(k):
        return (dp, x_at(k) * 2 + c)

    def group(xx, yy, part):
        return out_ref.at[c, xx, yy, :, :, cols[part]]

    def send(xx, yy, part, place):
        return links.copy(group(xx, yy, part), group(xx, yy, part), *place)

    out_ref[c, x, y, z] = in_ref[...]
    first = []
    for part in range(2):
        for k in range(1, deep):
            there = (lax.rem(z + k, deep) * 2 + y, st)
            first.append(
                links.copy(
                    in_ref.at[:, cols[part]], out_ref.at[c, x, y, z, :, cols[part]], *there
                )
            )
    for made in first[: deep - 1]:
        made.wait_recv()
    a_y = send(x, y, 0, to_y)
    for made in first[deep - 1 :]:
        made.wait_recv()
    b_x = [send(x, y, 1, to_x(k)) for k in range(1, across)]
    a_x = [send(x, y, 0, to_x(k)) for k in range(1, across)]
    b_y = send(x, y, 1, to_y)
    arriving = [send(x, y, 0, to_core), send(x, y, 1, to_core)]
    meanwhile(0)
    a_y.wait_recv()
    a_xy = [send(x, other_y, 0, to_x(k)) for k in range(1, across)]
    arriving.append(send(x, other_y, 0, to_core))
    b_xy = []
    for k in range(1, across):
        b_x[k - 1].wait_recv()
        from_x = lax.rem(x - k + across, across)
        b_xy.append(send(from_x, y, 1, to_y))
        arriving.append(send(from_x, y, 1, to_core))
    meanwhile(1)
    for k in range(1, across):
        a_x[k - 1].wait_recv()
        arriving.append(send(lax.rem(x - k + across, across), y, 0, to_core))
    b_y.wait_recv()
    arriving.append(send(x, other_y, 1, to_core))
    for k in range(1, across):
        from_x = lax.rem(x - k + across, across)
        a_xy[k - 1].wait_recv()
        arriving.append(send(from_x, other_y, 0, to_core))
        b_xy[k - 1].wait_recv()
        arriving.append(send(from_x, other_y, 1, to_core))
    for made in arriving:
        made.wait_recv()
    links.settle(first + [a_y, b_y] + b_x + a_x + a_xy + b_xy + arriving)


def gather_copies(nd, ns):
    deep, across = nd // 2, ns // 2
    return 2 * (deep - 1) + 2 + 4 * (across - 1) + 4 * across


def gather_all(values, number):
    nd, ns = lax.axis_size("dp"), lax.axis_size("state")
    rows, wide = values.shape
    deep, across = nd // 2, ns // 2
    copies = gather_copies(nd, ns)
    vmem = pl.BlockSpec(memory_space=pltpu.VMEM)
    out = pl.pallas_call(
        functools.partial(gather_all_kernel, nd, ns),
        out_shape=jax.ShapeDtypeStruct((2, across, 2, deep, rows, wide), values.dtype),
        in_specs=[vmem],
        out_specs=vmem,
        scratch_shapes=[pltpu.SemaphoreType.DMA((copies,)), pltpu.SemaphoreType.DMA((copies,))],
        compiler_params=pltpu.CompilerParams(
            collective_id=number, has_side_effects=True, vmem_limit_bytes=40 * 2**20
        ),
    )(values)
    return out.reshape(nd * ns * rows, wide)


def scatter_all_kernel(nd, ns, in_ref, out_ref, *scratch):
    sends, recvs = scratch[-2:]
    greet(near_peers(nd, ns))
    links = Links(sends, recvs)
    scatter_body(nd, ns, links, in_ref, out_ref, scratch[:-2])
    links.finish()


def scatter_body(nd, ns, links, in_ref, out_ref, scratch, meanwhile=nothing):
    rc, acc, rx_a, ry_a, rz_a, ry_b, rx_b, rz_b = scratch
    dp, st, z, y, x, c = places(nd, ns)
    deep, across = nd // 2, ns // 2
    half = in_ref.shape[5] // 2
    cols = (pl.ds(0, half), pl.ds(half, half))
    to_y = (dp + 1 - 2 * y, st)
    to_core = (dp, st + 1 - 2 * c)
    ys = (y, 1 - y)

    def x_at(k):
        return lax.rem(x + k, across)

    def to_x(k):
        return (dp, x_at(k) * 2 + c)

    core = {}
    order = [(k, ky, 0) for k in range(1, across) for ky in (1, 0)]
    order += [(k, 1, 1) for k in range(across)]
    order += [(0, 1, 0)] + [(k, 0, 1) for k in range(1, across)] + [(0, 0, 0), (0, 0, 1)]
    for k, ky, part in order:
        core[k, ky, part] = links.copy(
            in_ref.at[1 - c, x_at(k), ys[ky], :, :, cols[part]],
            rc.at[x_at(k), ys[ky], :, :, cols[part]],
            *to_core,
        )

    def total(k, ky, part, zz, others):
        found = in_ref[c, x_at(k), ys[ky], zz, :, cols[part]].astype(jnp.float32)
        found += rc[x_at(k), ys[ky], zz, :, cols[part]].astype(jnp.float32)
        for other in others:
            found += other[zz].astype(jnp.float32)
        return found

    def add(k, ky, part, others):
        core[k, ky, part].wait_recv()

        @pl.loop(0, deep)
        def _(zz):
            acc[x_at(k), ys[ky], zz, :, cols[part]] = total(k, ky, part, zz, others).astype(
                acc.dtype
            )

        return acc.at[x_at(k), ys[ky], :, :, cols[part]]

    meanwhile(0)
    a_x, b_y = {}, {}
    for k in range(1, across):
        for ky in (1, 0):
            a_x[k, ky] = links.copy(add(k, ky, 0, []), rx_a.at[k - 1, ky], *to_x(k))
    for k in range(across):
        b_y[k] = links.copy(add(k, 1, 1, []), ry_b.at[k], *to_y)
    meanwhile(1)
    for k in range(1, across):
        a_x[k, 1].wait_recv()
    a_y = links.copy(
        add(0, 1, 0, [rx_a.at[k - 1, 1] for k in range(1, across)]), ry_a, *to_y
    )
    b_x = {}
    for k in range(1, across):
        b_y[k].wait_recv()
        b_x[k] = links.copy(add(k, 0, 1, [ry_b.at[k]]), rx_b.at[k - 1], *to_x(k))
    meanwhile(2)
    for k in range(1, across):
        a_x[k, 0].wait_recv()
    a_y.wait_recv()
    left = [rx_a.at[k - 1, 0] for k in range(1, across)] + [ry_a]
    add(0, 0, 0, left)

    def send_z(part, land):
        return [
            links.copy(
                acc.at[x, y, lax.rem(z + k, deep), :, cols[part]],
                land.at[k - 1],
                lax.rem(z + k, deep) * 2 + y,
                st,
            )
            for k in range(1, deep)
        ]

    a_z = send_z(0, rz_a)
    b_y[0].wait_recv()
    for k in range(1, across):
        b_x[k].wait_recv()
    right = [ry_b.at[0]] + [rx_b.at[k - 1] for k in range(1, across)]
    add(0, 0, 1, right)
    b_z = send_z(1, rz_b)
    for part, made, others, land in ((0, a_z, left, rz_a), (1, b_z, right, rz_b)):
        found = total(0, 0, part, z, others)
        for k in range(1, deep):
            made[k - 1].wait_recv()
            found += land[k - 1].astype(jnp.float32)
        out_ref[:, cols[part]] = found
    links.settle(
        list(core.values()) + list(a_x.values()) + list(b_y.values()) + list(b_x.values())
        + [a_y] + a_z + b_z
    )


def scatter_copies(nd, ns):
    deep, across = nd // 2, ns // 2
    return 4 * across + 2 * (across - 1) + across + 1 + (across - 1) + 2 * (deep - 1)


def scatter_scratch(nd, ns, rows, wide, kind):
    deep, across = nd // 2, ns // 2
    half = wide // 2
    return [
        pltpu.VMEM((across, 2, deep, rows, wide), kind),
        pltpu.VMEM((across, 2, deep, rows, wide), kind),
        pltpu.VMEM((across - 1, 2, deep, rows, half), kind),
        pltpu.VMEM((deep, rows, half), kind),
        pltpu.VMEM((deep - 1, rows, half), kind),
        pltpu.VMEM((across, deep, rows, half), kind),
        pltpu.VMEM((across - 1, deep, rows, half), kind),
        pltpu.VMEM((deep - 1, rows, half), kind),
    ]


def scatter_all(values, number):
    nd, ns = lax.axis_size("dp"), lax.axis_size("state")
    deep, across = nd // 2, ns // 2
    rows, wide = values.shape[0] // (nd * ns), values.shape[1]
    copies = scatter_copies(nd, ns)
    vmem = pl.BlockSpec(memory_space=pltpu.VMEM)
    kind = values.dtype
    return pl.pallas_call(
        functools.partial(scatter_all_kernel, nd, ns),
        out_shape=jax.ShapeDtypeStruct((rows, wide), jnp.float32),
        in_specs=[vmem],
        out_specs=vmem,
        scratch_shapes=scatter_scratch(nd, ns, rows, wide, kind)
        + [pltpu.SemaphoreType.DMA((copies,)), pltpu.SemaphoreType.DMA((copies,))],
        compiler_params=pltpu.CompilerParams(
            collective_id=number, has_side_effects=True, vmem_limit_bytes=40 * 2**20
        ),
    )(values.reshape(2, across, 2, deep, rows, wide))


def front_kernel(
    nd,
    ns,
    depth_used,
    small_ref,
    gain_ref,
    table_ref,
    keys_ref,
    rest_ref,
    parts_ref,
    small_out,
    gain_out,
    rows_out,
    keys_out,
    rest_out,
    parts_out,
    looked,
    rc,
    acc,
    rx,
    fin,
    sums,
    sends,
    recvs,
    local,
):
    dp, st, z, y, x, c = places(nd, ns)
    deep, across = nd // 2, ns // 2
    own = table_ref.shape[0]
    tokens = rows_out.shape[1]
    part = tokens // ns
    to_core = (dp, st + 1 - 2 * c)
    to_y = (dp + 1 - 2 * y, st)
    other_y = dp + 1 - 2 * y
    dp_peers = [(lax.rem(dp + k, nd), st) for k in range(1, nd)]
    state_peers = [(dp, lax.rem(st + k, ns)) for k in range(1, ns)]
    greet(dp_peers + state_peers)
    links = Links(sends, recvs)

    ids_made = {}
    small_out[dp] = small_ref[...]
    gain_out[dp] = gain_ref[...]
    for k in range(1, nd):
        ids_made[k] = links.copy(small_ref, small_out.at[dp], *dp_peers[k - 1])
    gain_made = [links.copy(gain_ref, gain_out.at[dp], *peer) for peer in dp_peers]

    here = [
        pltpu.make_async_copy(keys_ref.at[st], keys_out.at[st, dp], local.at[0]),
        pltpu.make_async_copy(rest_ref, rest_out.at[dp], local.at[1]),
        pltpu.make_async_copy(parts_ref.at[dp], parts_out.at[dp], local.at[2]),
    ]
    for made in here:
        made.start()
    key_made = [
        links.copy(keys_ref.at[peer[1]], keys_out.at[st, dp], *peer) for peer in state_peers
    ]

    class Gather:
        def __init__(self, view):
            self.view = view
            self.base = links.used
            links.used += 2 * (deep - 1) + 1 + 2 * (deep - 1)

        def copy(self, number, owner, place):
            return pltpu.make_async_remote_copy(
                src_ref=self.view(owner),
                dst_ref=self.view(owner),
                send_sem=sends.at[self.base + number],
                recv_sem=recvs.at[self.base + number],
                device_id=place,
                device_id_type=MESH,
            )

        def pass_on(self, way, step):
            behind = z - way * step
            ahead = z + way
            number = step if way > 0 else deep - 1 + step

            def go(made):
                @pl.when((behind >= 0) & (behind < deep) & (ahead >= 0) & (ahead < deep))
                def _():
                    made(self.copy(number, behind * 2 + y, (ahead * 2 + y, st)))

            return go

        def begin(self):
            self.copy(2 * (deep - 1), dp, to_y).start()
            for way in (1, -1):
                self.pass_on(way, 0)(lambda made: made.start())

        def arrive(self, way, step):
            began = z - way * (step + 1)
            number = step if way > 0 else deep - 1 + step

            @pl.when((began >= 0) & (began < deep))
            def _():
                self.copy(number, began * 2 + y, to_y).wait_recv()
                self.copy(2 * (deep - 1) + 1 + number, began * 2 + y, to_y).start()

            if step + 1 < deep - 1:
                self.pass_on(way, step + 1)(lambda made: made.start())

        def finish(self):
            self.copy(2 * (deep - 1), other_y, to_y).wait_recv()
            self.copy(2 * (deep - 1), dp, to_y).wait_send()
            for way in (1, -1):
                for step in range(deep - 1):
                    began = z - way * (step + 1)
                    number = step if way > 0 else deep - 1 + step
                    self.pass_on(way, step)(lambda made: made.wait_send())

                    @pl.when((began >= 0) & (began < deep))
                    def _():
                        made = self.copy(2 * (deep - 1) + 1 + number, began * 2 + y, to_y)
                        made.wait_send()
                        made.wait_recv()

    rest = Gather(lambda owner: rest_out.at[owner])
    keys = Gather(lambda owner: keys_out.at[:, owner])
    here[1].wait()
    rest.begin()

    def swap(k):
        there = lax.rem(dp + k, nd)
        return links.copy(parts_ref.at[there], parts_out.at[dp], there, st)

    swapped = [swap(k) for k in range(1, nd // 2)]
    here[0].wait()
    for made in key_made:
        made.wait_recv()
    keys.begin()

    def x_at(k):
        return lax.rem(x + k, across)

    def row_at(k):
        return lax.rem(dp + k, nd)

    def block(k, kx, cc):
        start = (x_at(kx) * 2 + cc) * part
        return looked.at[k, :, pl.ds(pl.multiple_of(start, part), part)]

    def place(owner, share):
        return rows_out.at[
            pl.ds(pl.multiple_of(owner * own, own), own),
            pl.ds(pl.multiple_of(share * part, part), part),
        ]

    def add(sources, target):
        @pl.loop(0, own // 32)
        def _(i):
            rows = pl.ds(pl.multiple_of(i * 32, 32), 32)
            found = sources[0][rows, :].astype(jnp.float32)
            for source in sources[1:]:
                found += source[rows, :].astype(jnp.float32)
            target[rows, :] = found.astype(target.dtype)

    depth = table_ref.shape[1]
    piece = min(1024, depth)
    span = 2 * LANES

    def look(k):
        row = row_at(k)

        @pl.loop(0, tokens // span)
        def _(i):
            ids = jnp.concatenate(
                [small_out[row, pl.ds(2 * i, 1), :], small_out[row, pl.ds(2 * i + 1, 1), :]],
                axis=1,
            )
            ids = ids - st * depth_used
            sums[...] = jnp.zeros_like(sums)

            @pl.loop(0, depth // piece)
            def _(j):
                number = lax.broadcasted_iota(jnp.int32, (piece, span), 0)
                hit = jnp.where(number == ids - j * piece, 1.0, 0.0).astype(jnp.bfloat16)
                cols = pl.ds(pl.multiple_of(j * piece, piece), piece)
                sums[...] += jnp.dot(
                    table_ref[:, cols], hit, preferred_element_type=jnp.float32
                )

            cols = pl.ds(pl.multiple_of(i * span, span), span)
            looked[k, :, cols] = sums[...].astype(looked.dtype)

    turn = list(range(1, nd)) + [0]
    core, across_x, across_dp = {}, {}, {}

    def start_core(k):
        for kx in list(range(1, across)) + [0]:
            core[k, kx] = links.copy(block(k, kx, 1 - c), rc.at[k, kx], *to_core)

    def start_x(k):
        for kx in range(1, across):
            core[k, kx].wait_recv()
            add([block(k, kx, c), rc.at[k, kx]], acc.at[k, kx - 1])
            across_x[k, kx] = links.copy(
                acc.at[k, kx - 1], rx.at[k, kx - 1], dp, x_at(kx) * 2 + c
            )

    def start_dp(k):
        core[k, 0].wait_recv()
        sources = [block(k, 0, c), rc.at[k, 0]]
        for kx in range(1, across):
            across_x[k, kx].wait_recv()
            sources.append(rx.at[k, kx - 1])
        if k:
            add(sources, fin.at[k - 1])
            across_dp[k] = links.copy(fin.at[k - 1], place(dp, st), row_at(k), st)
        else:
            add(sources, place(dp, st))

    chores = []
    for step in range(deep - 1):
        for way in (1, -1):
            chores.append(functools.partial(rest.arrive, way, step))
    for step in range(deep - 1):
        for way in (1, -1):
            chores.append(functools.partial(keys.arrive, way, step))
    each = -(-len(chores) // nd)
    for number, k in enumerate(turn):
        if k:
            ids_made[nd - k].wait_recv()
        look(k)
        start_core(k)
        if number >= 1:
            start_x(turn[number - 1])
        if number >= 2:
            start_dp(turn[number - 2])
        for _ in range(each):
            if number >= 2 and chores:
                chores.pop(0)()
    start_x(turn[-1])
    start_dp(turn[-2])
    start_dp(turn[-1])
    swapped += [swap(k) for k in range(nd // 2, nd)]
    later, last = {}, []
    for number, k in enumerate([0] + list(range(1, nd))):
        owner = lax.rem(dp - k + nd, nd)
        if k:
            across_dp[k].wait_recv()
        for kx in range(1, across):
            later[k, kx] = links.copy(
                place(owner, st), place(owner, st), dp, x_at(kx) * 2 + c
            )
        last.append(links.copy(place(owner, st), place(owner, st), *to_core))
        if chores:
            chores.pop(0)()
    for k in range(nd):
        owner = lax.rem(dp - k + nd, nd)
        for kx in range(1, across):
            later[k, kx].wait_recv()
            share = lax.rem(x - kx + across, across) * 2 + c
            last.append(links.copy(place(owner, share), place(owner, share), *to_core))
    while chores:
        chores.pop(0)()
    for made in last + swapped + gain_made:
        made.wait_recv()
    here[2].wait()
    links.finish()
    rest.finish()
    keys.finish()


def front(small, gain, table, keys, rest, parts, tokens, vocab, number):
    nd, ns = lax.axis_size("dp"), lax.axis_size("state")
    deep, across = nd // 2, ns // 2
    own = table.shape[0]
    part = tokens // ns
    kind = table.dtype
    copies = 2 * (nd - 1) + ns - 1 + 2 * (4 * (deep - 1) + 1) + nd - 1
    copies += nd * across + nd * (across - 1) + nd - 1 + nd * across + nd * (across - 1)
    vmem = pl.BlockSpec(memory_space=pltpu.VMEM)
    hbm = pl.BlockSpec(memory_space=pl.ANY)
    return pl.pallas_call(
        functools.partial(front_kernel, nd, ns, vocab),
        out_shape=[
            jax.ShapeDtypeStruct((nd,) + small.shape, small.dtype),
            jax.ShapeDtypeStruct((nd,) + gain.shape, gain.dtype),
            jax.ShapeDtypeStruct((nd * own, tokens), kind),
            jax.ShapeDtypeStruct((ns, nd) + keys.shape[1:], kind),
            jax.ShapeDtypeStruct((nd,) + rest.shape, kind),
            jax.ShapeDtypeStruct(parts.shape, kind),
        ],
        in_specs=[vmem, vmem, vmem, hbm, hbm, hbm],
        out_specs=[vmem, vmem, vmem, hbm, hbm, hbm],
        scratch_shapes=[
            pltpu.VMEM((nd, own, tokens), kind),
            pltpu.VMEM((nd, across, own, part), kind),
            pltpu.VMEM((nd, across - 1, own, part), kind),
            pltpu.VMEM((nd, across - 1, own, part), kind),
            pltpu.VMEM((nd - 1, own, part), kind),
            pltpu.VMEM((own, 2 * LANES), jnp.float32),
            pltpu.SemaphoreType.DMA((copies,)),
            pltpu.SemaphoreType.DMA((copies,)),
            pltpu.SemaphoreType.DMA((3,)),
        ],
        compiler_params=pltpu.CompilerParams(
            collective_id=number, has_side_effects=True, vmem_limit_bytes=52 * 2**20
        ),
        cost_estimate=pl.CostEstimate(
            flops=2 * table.size * nd * tokens, bytes_accessed=4 * parts.size, transcendentals=0
        ),
    )(small, gain, table, keys, rest, parts)


def slots_back_kernel(
    nd,
    ns,
    width,
    units,
    part_hbm,
    table_ref,
    two_ref,
    one_ref,
    gain_ref,
    wd_ref,
    wgu_ref,
    gu_ref,
    hidden_ref,
    rows_ref,
    one_out,
    table_out,
    ffn_out,
    gains_out,
    part_ref,
    summed,
    low,
    down,
    dgu,
    dffn,
    local,
    *scratch,
):
    sends, recvs = scratch[-2:]
    dp, st, z, y, x, c = places(nd, ns)
    deep, across = nd // 2, ns // 2
    count, wide = two_ref.shape
    every = nd * ns * count
    dp_peers = [(lax.rem(dp + k, nd), st) for k in range(1, nd)]
    state_peers = [(dp, lax.rem(st + k, ns)) for k in range(1, ns)]
    fill = pltpu.make_async_copy(part_hbm, part_ref, local.at[2])
    fill.start()
    greet(dp_peers + state_peers)
    links = Links(sends, recvs)
    own_copy = pltpu.make_async_copy(table_ref.at[dp], table_out.at[dp], local.at[0])
    own_copy.start()
    local_copies = [own_copy]
    own = table_ref.shape[1]
    chunk = own // CHUNKS
    queue = [(peer, i) for i in range(CHUNKS) for peer in dp_peers]
    swapped = []

    def feed(amount):
        for _ in range(min(amount, len(queue))):
            peer, i = queue.pop(0)
            rows = pl.ds(i * chunk, chunk)
            swapped.append(
                links.copy(table_ref.at[peer[0], rows], table_out.at[dp, rows], *peer)
            )

    def feeding(amounts):
        return lambda place: feed(amounts[place])

    def norm_back(grad, values, gain, row):
        mean = jnp.sum(values * values, axis=1, keepdims=True) * (1.0 / width)
        root = lax.rsqrt(mean + NORM_EPS)
        scaled = grad * gain
        inner = jnp.sum(scaled * values, axis=1, keepdims=True) * (1.0 / width)
        gains_out[pl.ds(row, 1), :] = jnp.sum(grad * values * root, axis=0, keepdims=True)
        return scaled * root - values * (root * root * root * inner)

    fill.wait()
    scatter_body(nd, ns, links, part_ref, summed, scratch[:-2], feeding(FEED[0]))
    summed[...] = norm_back(summed[...], two_ref[...], gain_ref[pl.ds(1, 1), :], 1)
    low[...] = summed[...].astype(low.dtype)
    gather_body(nd, ns, links, low, down, feeding(FEED[1]))
    feed(FEED[2])

    inner_cols = gu_ref.shape[1]
    step = deep * count
    flat_down = down

    @pl.loop(0, 2 * across * 2)
    def _(i):
        cc, rest = lax.div(i, 2 * across), lax.rem(i, 2 * across)
        xx, yy = lax.div(rest, 2), lax.rem(rest, 2)
        rows = pl.ds(pl.multiple_of(i * step, step), step)
        grad = jnp.dot(
            flat_down[cc, xx, yy].reshape(step, wide),
            wd_ref[...],
            preferred_element_type=jnp.float32,
        )
        grad = jnp.concatenate(
            [grad, jnp.zeros((step, inner_cols - grad.shape[1]), jnp.float32)], axis=1
        ) if inner_cols > grad.shape[1] else grad[:, :inner_cols]
        gate = gu_ref[rows, :]
        up = pltpu.roll(gate, inner_cols - units, 1)
        gated = 1.0 / (1.0 + jnp.exp(-gate))
        grad_gate = grad * up * (gated * (1.0 + gate * (1.0 - gated)))
        grad_up = pltpu.roll(grad * gate * gated, units, 1)
        lanes = lax.broadcasted_iota(jnp.int32, grad_gate.shape, 1)
        joined = jnp.where(lanes < units, grad_gate, grad_up).astype(dgu.dtype)
        dgu[rows, :] = joined
        part_ref[cc, xx, yy] = (
            lax.dot_general(
                joined, wgu_ref[...], (((1,), (1,)), ((), ())), preferred_element_type=jnp.float32
            )
            .astype(part_ref.dtype)
            .reshape(deep, count, wide)
        )

    def weight_grads(place):
        feed(FEED[3][place])
        if place:
            return
        span = 2 * LANES

        @pl.loop(0, wide // span)
        def _(i):
            cols = pl.ds(pl.multiple_of(i * span, span), span)
            dffn[cols, :inner_cols] = lax.dot_general(
                rows_ref[:, cols], dgu[...], (((0,), (0,)), ((), ())),
                preferred_element_type=jnp.float32,
            ).astype(dgu.dtype)
            dffn[cols, inner_cols:] = lax.dot_general(
                flat_down[:, :, :, :, :, cols].reshape(every, span), hidden_ref[...],
                (((0,), (0,)), ((), ())),
                preferred_element_type=jnp.float32,
            ).astype(dgu.dtype)

        home = pltpu.make_async_copy(dffn, ffn_out, local.at[1])
        home.start()
        local_copies.append(home)

    grad_two = summed[...]
    scatter_body(nd, ns, links, part_ref, summed, scratch[:-2], weight_grads)
    grad_one = grad_two + norm_back(summed[...], one_ref[...], gain_ref[pl.ds(0, 1), :], 0)
    one_out[st] = grad_one.astype(one_out.dtype)
    low[...] = grad_one.astype(low.dtype)
    made = [links.copy(low, one_out.at[st], *peer) for peer in state_peers]
    for copy in made:
        copy.wait_recv()
    feed(len(queue))
    for copy in swapped:
        copy.wait_recv()
    for copy in local_copies:
        copy.wait()
    links.finish()


def slots_back(part, table, two, one, gain, wd, wgu, gu, hidden, rows, width, units, number):
    nd, ns = lax.axis_size("dp"), lax.axis_size("state")
    deep, across = nd // 2, ns // 2
    count, wide = two.shape
    kind = part.dtype
    cols = wgu.shape[1] + wd.shape[1]
    copies = 2 * scatter_copies(nd, ns) + gather_copies(nd, ns) + (nd - 1) * CHUNKS + ns - 1
    vmem = pl.BlockSpec(memory_space=pltpu.VMEM)
    hbm = pl.BlockSpec(memory_space=pl.ANY)
    six = (2, across, 2, deep, count, wide)
    out = pl.pallas_call(
        functools.partial(slots_back_kernel, nd, ns, width, units),
        out_shape=[
            jax.ShapeDtypeStruct((ns, count, wide), kind),
            jax.ShapeDtypeStruct(table.shape, kind),
            jax.ShapeDtypeStruct((wide, cols), kind),
            jax.ShapeDtypeStruct((2, wide), jnp.float32),
        ],
        in_specs=[hbm, hbm] + [vmem] * 8,
        out_specs=[vmem, hbm, hbm, vmem],
        scratch_shapes=[
            pltpu.VMEM(six, kind),
            pltpu.VMEM((count, wide), jnp.float32),
            pltpu.VMEM((count, wide), kind),
            pltpu.VMEM(six, kind),
            pltpu.VMEM((nd * ns * count, wgu.shape[1]), kind),
            pltpu.VMEM((wide, cols), kind),
            pltpu.SemaphoreType.DMA((3,)),
        ]
        + scatter_scratch(nd, ns, count, wide, kind)
        + [pltpu.SemaphoreType.DMA((copies,)), pltpu.SemaphoreType.DMA((copies,))],
        compiler_params=pltpu.CompilerParams(
            collective_id=number, has_side_effects=True, vmem_limit_bytes=58 * 2**20
        ),
        cost_estimate=pl.CostEstimate(
            flops=8 * rows.size * cols, bytes_accessed=100 * part.size, transcendentals=0
        ),
    )(part.reshape(six), table, two, one, gain, wd, wgu, gu, hidden, rows)
    return (out[0].reshape(ns * count, wide),) + tuple(out[1:])


def rows_back_kernel(
    nd, ns, width, in_ref, stream_ref, gain_ref, more_ref, out_ref, gain_out, rc, acc, rx, fin, low,
    sends, recvs
):
    dp, st, z, y, x, c = places(nd, ns)
    across = ns // 2
    tokens = in_ref.shape[1]
    own = in_ref.shape[0] // nd
    part = tokens // ns
    to_core = (dp, st + 1 - 2 * c)
    dp_peers = [(lax.rem(dp + k, nd), st) for k in range(1, nd)]
    peers = dp_peers + [(dp, lax.rem(x + k, across) * 2 + c) for k in range(1, across)]
    greet(peers + [to_core])
    links = Links(sends, recvs)

    def x_at(k):
        return lax.rem(x + k, across)

    def rows_of(owner):
        return pl.ds(pl.multiple_of(owner * own, own), own)

    def block(k, kx, cc):
        start = (x_at(kx) * 2 + cc) * part
        return in_ref.at[pl.ds(k * own, own), pl.ds(pl.multiple_of(start, part), part)]

    def place(row, share):
        return out_ref.at[:, pl.ds(pl.multiple_of(row * tokens + share * part, part), part)]

    def add(sources, target):
        @pl.loop(0, own // 32)
        def _(i):
            rows = pl.ds(pl.multiple_of(i * 32, 32), 32)
            found = sources[0][rows, :].astype(jnp.float32)
            for source in sources[1:]:
                found += source[rows, :].astype(jnp.float32)
            target[rows, :] = found.astype(target.dtype)

    core, across_x = {}, {}
    for kx in list(range(1, across)) + [0]:
        for k in range(nd):
            core[k, kx] = links.copy(block(k, kx, 1 - c), rc.at[k, kx], *to_core)
    for kx in range(1, across):
        for k in range(nd):
            core[k, kx].wait_recv()
            add([block(k, kx, c), rc.at[k, kx]], acc.at[k, kx - 1])
            across_x[k, kx] = links.copy(
                acc.at[k, kx - 1], rx.at[k, kx - 1], dp, x_at(kx) * 2 + c
            )
    for k in range(nd):
        core[k, 0].wait_recv()
        sources = [block(k, 0, c), rc.at[k, 0]]
        for kx in range(1, across):
            across_x[k, kx].wait_recv()
            sources.append(rx.at[k, kx - 1])
        add(sources, fin.at[pl.ds(k * own, own), :])

    step = 32
    pieces = in_ref.shape[0] // step

    def at(i):
        return pl.ds(pl.multiple_of(i * step, step), step)

    def gather_sums(i, carry):
        square, inner = carry
        values = stream_ref[at(i), :].astype(jnp.float32)
        scaled = fin[at(i), :] * gain_ref[at(i), :] * values
        square = square + jnp.sum(values * values, axis=0, keepdims=True)
        return square, inner + jnp.sum(scaled, axis=0, keepdims=True)

    none = jnp.zeros((1, part), jnp.float32)
    square, inner = lax.fori_loop(0, pieces, gather_sums, (none, none))
    root = lax.rsqrt(square * (1.0 / width) + NORM_EPS)
    inner = inner * (1.0 / width) * root * root * root

    @pl.loop(0, pieces)
    def _(i):
        values = stream_ref[at(i), :].astype(jnp.float32)
        grad = fin[at(i), :]
        gain_out[at(i), :] = jnp.sum(grad * values * root, axis=1, keepdims=True)
        found = grad * gain_ref[at(i), :] * root - values * inner + more_ref[at(i), :]
        low[at(i), :] = found.astype(low.dtype)

    swapped = [links.copy(low.at[rows_of(p[0]), :], place(dp, st), *p) for p in dp_peers]
    place(dp, st)[...] = low[rows_of(dp), :]
    later, last = {}, []
    for k in range(nd):
        row = lax.rem(dp - k + nd, nd)
        if k:
            swapped[k - 1].wait_recv()
        for kx in range(1, across):
            later[k, kx] = links.copy(place(row, st), place(row, st), dp, x_at(kx) * 2 + c)
        last.append(links.copy(place(row, st), place(row, st), *to_core))
    for k in range(nd):
        row = lax.rem(dp - k + nd, nd)
        for kx in range(1, across):
            later[k, kx].wait_recv()
            share = lax.rem(x - kx + across, across) * 2 + c
            last.append(links.copy(place(row, share), place(row, share), *to_core))
    for made in last:
        made.wait_recv()
    links.finish()


def rows_back(values, stream, gain, more, width, number):
    nd, ns = lax.axis_size("dp"), lax.axis_size("state")
    across = ns // 2
    wide, tokens = values.shape
    own, part = wide // nd, tokens // ns
    copies = nd * across + nd * (across - 1) + nd - 1 + nd * across + nd * (across - 1)
    vmem = pl.BlockSpec(memory_space=pltpu.VMEM)
    kind = values.dtype
    return pl.pallas_call(
        functools.partial(rows_back_kernel, nd, ns, width),
        out_shape=[
            jax.ShapeDtypeStruct((own, nd * tokens), kind),
            jax.ShapeDtypeStruct((wide, 1), jnp.float32),
        ],
        in_specs=[vmem] * 4,
        out_specs=[vmem] * 2,
        scratch_shapes=[
            pltpu.VMEM((nd, across, own, part), kind),
            pltpu.VMEM((nd, across - 1, own, part), kind),
            pltpu.VMEM((nd, across - 1, own, part), kind),
            pltpu.VMEM((wide, part), jnp.float32),
            pltpu.VMEM((wide, part), kind),
            pltpu.SemaphoreType.DMA((copies,)),
            pltpu.SemaphoreType.DMA((copies,)),
        ],
        compiler_params=pltpu.CompilerParams(
            collective_id=number, has_side_effects=True, vmem_limit_bytes=48 * 2**20
        ),
        cost_estimate=pl.CostEstimate(
            flops=0, bytes_accessed=60 * values.size, transcendentals=0
        ),
    )(values, stream, gain, more)


def state_sum_kernel(nd, ns, in_ref, out_ref, land, sends, recvs):
    dp, st = lax.axis_index("dp"), lax.axis_index("state")
    peers = [(dp, lax.rem(st + k, ns)) for k in range(1, ns)]
    greet(peers)
    links = Links(sends, recvs)
    made = [
        links.copy(in_ref.at[there[1]], land.at[k], *there) for k, there in enumerate(peers)
    ]
    found = in_ref[st].astype(jnp.float32)
    for k in range(ns - 1):
        made[k].wait_recv()
        found += land[k].astype(jnp.float32)
    out_ref[...] = found
    links.finish()


def state_sum(values, number):
    nd, ns = lax.axis_size("dp"), lax.axis_size("state")
    rows, wide = values.shape[0] // ns, values.shape[1]
    vmem = pl.BlockSpec(memory_space=pltpu.VMEM)
    return pl.pallas_call(
        functools.partial(state_sum_kernel, nd, ns),
        out_shape=jax.ShapeDtypeStruct((rows, wide), jnp.float32),
        in_specs=[vmem],
        out_specs=vmem,
        scratch_shapes=[
            pltpu.VMEM((ns - 1, rows, wide), values.dtype),
            pltpu.SemaphoreType.DMA((ns - 1,)),
            pltpu.SemaphoreType.DMA((ns - 1,)),
        ],
        compiler_params=pltpu.CompilerParams(collective_id=number, has_side_effects=True),
    )(values.reshape(ns, rows, wide))


def on_device(
    token_ids,
    doc_starts,
    loss_positions,
    loss_targets,
    owners,
    in_weight,
    out_weight,
    table_weight,
    gain_weight,
    in_first,
    out_first,
    table_first,
    gain_first,
    in_second,
    out_second,
    table_second,
    gain_second,
    in_average,
    out_average,
    table_average,
    gain_average,
):
    f32 = jnp.float32
    bf16 = jnp.bfloat16
    nd = lax.axis_size("dp")
    ns = lax.axis_size("state")
    me_dp = lax.axis_index("dp")
    me_state = lax.axis_index("state")
    tokens = token_ids.shape[1]
    slots = loss_positions.shape[1]
    capacity = in_weight.shape[1]
    block_rows = in_weight.shape[2]
    block_count = owners.shape[0]
    width = block_rows * block_count
    own = capacity * block_rows
    wide = nd * own
    key_share = KEY_DIM // ns
    heads = HEADS // ns
    key_cols = HEADS * key_share
    value_width = heads * VAL_DIM
    mixer_cols = 2 * key_cols + value_width
    units = out_weight.shape[3] - value_width
    unit_part = units // nd
    vocab_share = table_weight.shape[3]
    vocab_part = -(-vocab_share // (nd * LANES)) * LANES
    quarter = tokens // ns
    slot_part = slots // ns

    held_all = jnp.sum((owners[None, :] == jnp.arange(nd)[:, None]).astype(jnp.int32), axis=1)
    occupied_all = jnp.arange(capacity)[None, :] < held_all[:, None]
    held = jnp.sum((owners == me_dp).astype(jnp.int32))
    occupied_here = jnp.arange(capacity) < held
    rows_here = jnp.repeat(occupied_here, block_rows)[:, None]

    def lowered(array):
        return jnp.where(rows_here, array[0].reshape(own, -1), 0.0).astype(bf16)

    in_own = lowered(in_weight)
    out_own = lowered(out_weight)

    def in_rows(flat):
        flat = jnp.pad(flat, (0, -flat.shape[0] % (16 * LANES)))
        return flat.reshape(-1, LANES)

    key_part = heads * key_share
    keys_sent = in_own[:, : 2 * key_cols].reshape(own, 2, ns, key_part)
    keys_sent = keys_sent.transpose(2, 0, 1, 3).reshape(ns, own, 2 * key_part)
    rest_sent = jnp.concatenate(
        [in_own[:, 2 * key_cols : mixer_cols], out_own[:, :value_width]], axis=1
    )
    table_padded = lowered(
        jnp.pad(table_weight, ((0, 0), (0, 0), (0, 0), (0, nd * vocab_part - vocab_share)))
    )

    def by_part(columns, parts):
        return columns.reshape(own, nd, parts)

    def zeros(parts):
        return jnp.zeros((own, nd, parts), bf16)

    gu_cols = -(-2 * unit_part // LANES) * LANES
    down_cols = -(-unit_part // LANES) * LANES
    parts_sent = jnp.concatenate(
        [
            by_part(in_own[:, mixer_cols : mixer_cols + units], unit_part),
            by_part(in_own[:, mixer_cols + units :], unit_part),
            zeros(gu_cols - 2 * unit_part),
            by_part(out_own[:, value_width:], unit_part),
            zeros(down_cols - unit_part),
        ],
        axis=2,
    ).transpose(1, 0, 2)
    small, gains_all, stream, keys_all, rest_all, parts_all = front(
        in_rows(jnp.concatenate([token_ids[0], loss_targets[0]])),
        in_rows(gain_weight.astype(bf16).reshape(-1)),
        table_padded,
        keys_sent,
        rest_sent,
        parts_sent,
        tokens,
        vocab_share,
        1,
    )
    small = small.reshape(nd, -1)
    ids_all = small[:, :tokens]
    slot_targets = small[:, tokens : tokens + slots].reshape(nd // 2, 2, ns // 2, 2, slot_part)
    targets_all = slot_targets.transpose(3, 2, 1, 0, 4).reshape(-1)
    gains_all = gains_all.reshape(nd, -1)[:, : capacity * 4 * block_rows].astype(f32)
    gains_all = gains_all.reshape(nd * capacity, 4, block_rows)
    gains = jnp.where(occupied_all.reshape(-1)[:, None, None], gains_all, 0.0)
    gains = gains.transpose(1, 0, 2).reshape(4, wide)
    index = slot_index(owners, capacity)
    head_gain = lax.dynamic_slice_in_dim(
        gains_all[index][:, 1].reshape(width), me_state * value_width, value_width
    )
    live = (targets_all >= 0).astype(f32)
    count = jnp.sum(live)
    local_ids = ids_all.reshape(-1) - me_state * vocab_share
    hit = jnp.arange(vocab_share)[:, None] == local_ids[None, :]
    stream_mine = lax.dynamic_slice_in_dim(stream, me_state * quarter, quarter, axis=1)

    qcols = heads * KEY_DIM
    keys_all = keys_all.reshape(ns, wide, 2 * key_part)
    w_q = keys_all[:, :, :key_part].transpose(1, 0, 2).reshape(wide, qcols)
    w_f = keys_all[:, :, key_part:].transpose(1, 0, 2).reshape(wide, qcols)
    rest_all = rest_all.reshape(wide, 2 * value_width)
    w_v = rest_all[:, :value_width]
    w_o = rest_all[:, value_width:]
    w_fv = jnp.concatenate([w_f, w_v], axis=1)
    w_qfv = jnp.concatenate([w_q, w_fv], axis=1)
    parts_all = parts_all.reshape(wide, -1)
    w_gu = parts_all[:, :gu_cols]
    w_d = parts_all[:, gu_cols:]
    table_padded, stream = lax.optimization_barrier((table_padded, stream))
    table = swap_dp(spread_columns(table_padded, nd)).reshape(wide, vocab_part)

    positions = loss_positions[0]
    pick_hit = positions[:, None] == jnp.arange(tokens)[None, :]
    pick = pick_hit.astype(f32)
    pick_low = pick_hit.astype(bf16)
    documents = document_ids(doc_starts[0], tokens)
    doc_at = jnp.sum(jnp.where(pick_hit, documents[None, :], 0), axis=1)
    allowed = (positions[:, None] >= jnp.arange(tokens)[None, :]) & (
        doc_at[:, None] == documents[None, :]
    )

    def tall_norm(values, gain):
        mean = jnp.sum(values * values, axis=0, keepdims=True) * (1.0 / width)
        return values * lax.rsqrt(mean + NORM_EPS) * gain[:, None]

    normed_one = tall_norm(stream.astype(f32), gains[0]).astype(bf16)
    normed_at = times_right(pick_low, normed_one).astype(bf16)
    stream_at = times_right(
        lax.dynamic_slice_in_dim(pick_low, me_state * slot_part, slot_part), stream
    )
    forget_value = times_left(normed_one, w_fv)
    query_pre = times_plain(normed_at, w_q)
    query, back_query = jax.vjp(jax.nn.silu, query_pre)
    (key_gate, log_forget), back_gates = jax.vjp(forget_gates, forget_value[:, :qcols])

    def mix(query_in, key_in, forget_in, value_in):
        return slot_mixer(query_in, key_in, forget_in, value_in, pick, allowed, heads, key_part)

    mixed, back_mix = jax.vjp(
        mix,
        query.astype(bf16).astype(f32),
        key_gate.astype(bf16).astype(f32),
        log_forget,
        forget_value[:, qcols:].astype(bf16).astype(f32),
    )

    def head_norm(mixed_in, gain_in):
        return rms_norm(
            mixed_in.reshape(slots, heads, VAL_DIM), gain_in.reshape(heads, VAL_DIM), VAL_DIM
        ).reshape(slots, value_width)

    gated_f, back_head = jax.vjp(head_norm, mixed, head_gain)
    gated = gated_f.astype(bf16)
    stream_one = stream_at + state_sum(times_right(gated, w_o).astype(bf16), 2)

    def wide_norm(values, gain):
        return rms_norm(values, gain, width)

    normed_two = wide_norm(stream_one, gains[2])
    rows_two = gather_all(normed_two.astype(bf16), 3)
    gate_up = times_plain(rows_two, w_gu)
    hidden = swiglu(gate_up, unit_part, down_cols).astype(bf16)
    stream_two = stream_one + scatter_all(times_right(hidden, w_d).astype(bf16), 4)
    normed_three = wide_norm(stream_two, gains[3])
    rows_three = gather_all(normed_three.astype(bf16), 5)

    logits = times_plain(rows_three, table)
    column = jnp.arange(vocab_part)[None, :] + me_dp * vocab_part
    target_hit = (column + me_state * vocab_share == targets_all[:, None]) & (
        column < vocab_share
    )
    logits = jnp.where(column < vocab_share, logits, -1e30)
    top_here = jnp.max(logits, axis=1)
    sum_here = jnp.sum(jnp.exp(logits - top_here[:, None]), axis=1)
    picked_here = jnp.sum(jnp.where(target_hit, logits, 0.0), axis=1)
    shares = combine_all(
        jnp.stack([top_here, sum_here, picked_here]).reshape(3, -1, LANES), add_exponentials, 6
    ).reshape(3, -1)
    lse = shares[0] + jnp.log(shares[1])
    loss_sum = jnp.sum((lse - shares[2]) * live)
    probs = jnp.exp(logits - lse[:, None])
    dlogits = ((probs - target_hit.astype(f32)) * (live / count)[:, None]).astype(bf16)
    grad_table_part = times_left(rows_three, dlogits).astype(bf16)
    grad_one, grad_table_back, grad_ffn, gain_pair = slots_back(
        times_right(dlogits, table).astype(bf16),
        grad_table_part.reshape(nd, own, vocab_part),
        stream_two,
        stream_one,
        gains[2:],
        w_d,
        w_gu,
        gate_up,
        hidden,
        rows_two,
        width,
        unit_part,
        7,
    )
    grad_gain_three, grad_gain_four = gain_pair

    grad_gated = times_plain(grad_one, w_o)
    grad_o_part = times_left(grad_one, gated).astype(bf16)
    grad_gated, grad_o_part = lax.optimization_barrier((grad_gated, grad_o_part))
    grad_mixed, grad_gain_two = back_head(grad_gated)
    grad_query, grad_key, grad_forget, grad_value = back_mix(
        grad_mixed.astype(bf16).astype(f32)
    )
    (grad_query_pre,) = back_query(grad_query)
    grad_query_pre = times_left(pick, grad_query_pre)
    (grad_forget_pre,) = back_gates((grad_key, grad_forget))
    grad_qfv = jnp.concatenate([grad_query_pre, grad_forget_pre, grad_value], axis=1).astype(bf16)
    pick_mine = lax.dynamic_slice_in_dim(pick_low, me_state * quarter, quarter, axis=1)
    grad_rows = times_right(w_qfv, grad_qfv).astype(bf16)
    grad_w_qfv = times_plain(normed_one, grad_qfv).astype(bf16)
    grad_rows, grad_w_qfv = lax.optimization_barrier((grad_rows, grad_w_qfv))
    embed, grad_gain_one = rows_back(
        grad_rows,
        stream_mine,
        gains[0][:, None],
        times_left(grad_one, pick_mine),
        width,
        8,
    )
    embed, grad_ffn, grad_table_back = lax.optimization_barrier(
        (embed, grad_ffn, grad_table_back)
    )
    grad_ffn = swap_dp(grad_ffn.reshape(nd, own, gu_cols + down_cols))
    grad_gain_one = grad_gain_one[:, 0]

    def sum_dp(values):
        return lax.psum_scatter(values, "dp", scatter_dimension=0, tiled=True)

    def square_sum(values):
        values = values.astype(f32)
        return jnp.sum(values * values)

    grad_qfv_own = sum_dp(grad_w_qfv)
    grad_o_own = sum_dp(grad_o_part)
    own_table = times_right(embed, hit.astype(bf16)) + join_columns(grad_table_back)[
        :, :vocab_share
    ].astype(f32)
    squares = square_sum(own_table)
    grad_ffn, squares = lax.optimization_barrier((grad_ffn, squares))
    squares = squares + square_sum(grad_ffn)
    grad_gate = join_columns(grad_ffn[:, :, :unit_part])
    grad_up = join_columns(grad_ffn[:, :, unit_part : 2 * unit_part])
    grad_down = join_columns(grad_ffn[:, :, gu_cols : gu_cols + unit_part])
    grad_qfv_own, grad_o_own, squares, grad_gate, grad_up, grad_down = lax.optimization_barrier(
        (grad_qfv_own, grad_o_own, squares, grad_gate, grad_up, grad_down)
    )
    squares = squares + square_sum(grad_qfv_own) + square_sum(grad_o_own)

    grad_keys = grad_qfv_own[:, : 2 * qcols].reshape(own, 2, ns, key_part)
    grad_keys = grad_keys.transpose(2, 0, 1, 3).reshape(ns, own, 2 * key_part)
    grad_keys = lax.all_to_all(grad_keys, "state", split_axis=0, concat_axis=0, tiled=True)

    head_full = lax.dynamic_update_slice_in_dim(
        jnp.zeros((width,), f32), grad_gain_two, me_state * value_width, 0
    )
    gain_parts = jnp.concatenate([grad_gain_one, grad_gain_three, grad_gain_four, head_full])
    sums = jnp.concatenate([gain_parts, squares[None]])
    sums = jnp.pad(sums, (0, -sums.shape[0] % (8 * LANES))).reshape(-1, LANES)
    sums = combine_all(sums, add_up, 10).reshape(-1)
    gain_sums = sums[: 3 * wide + width]
    head_slots = (
        jnp.zeros((nd * capacity, block_rows), f32)
        .at[index]
        .set(gain_sums[3 * wide :].reshape(block_count, block_rows))
    )
    gain_slots = gain_sums[: 3 * wide].reshape(3, nd * capacity, block_rows)
    gain_slots = jnp.stack([gain_slots[0], head_slots, gain_slots[1], gain_slots[2]], axis=1)
    own_gain = lax.dynamic_slice_in_dim(gain_slots, me_dp * capacity, capacity)

    squares_all = sums[3 * wide + width] + jnp.sum(gain_sums * gain_sums)
    grad_norm = jnp.sqrt(squares_all)
    scale = jnp.minimum(1.0, CLIP_NORM / (grad_norm + 1e-06))
    occupied = occupied_here.astype(f32)
    new_table = adam_blocks(
        table_weight,
        table_first,
        table_second,
        table_average,
        own_table.reshape(table_weight.shape),
        scale,
        LEARN_RATE,
        WEIGHT_DECAY,
        occupied,
    )
    grad_keys, grad_gate, _ = lax.optimization_barrier(
        (grad_keys, grad_gate, new_table[0][0, 0, :8, :LANES])
    )
    grad_keys = grad_keys.reshape(ns, own, 2, key_part).transpose(1, 2, 0, 3)
    own_in = jnp.concatenate(
        [
            grad_keys.reshape(own, 2 * key_cols),
            grad_qfv_own[:, 2 * qcols :],
            grad_gate,
            grad_up,
        ],
        axis=1,
    )
    own_out = jnp.concatenate([grad_o_own, grad_down], axis=1)

    new_in = adam_blocks(
        in_weight,
        in_first,
        in_second,
        in_average,
        own_in.reshape(in_weight.shape),
        scale,
        LEARN_RATE,
        WEIGHT_DECAY,
        occupied,
    )
    new_out = adam_blocks(
        out_weight,
        out_first,
        out_second,
        out_average,
        own_out.reshape(out_weight.shape),
        scale,
        LEARN_RATE,
        WEIGHT_DECAY,
        occupied,
    )
    new_gain = adam_update(
        gain_weight,
        gain_first,
        gain_second,
        gain_average,
        own_gain,
        scale,
        GAIN_RATE,
        0.0,
        occupied[:, None, None],
    )
    return (
        new_in[0],
        new_out[0],
        new_table[0],
        new_gain[0],
        new_in[1],
        new_out[1],
        new_table[1],
        new_gain[1],
        new_in[2],
        new_out[2],
        new_table[2],
        new_gain[2],
        new_in[3],
        new_out[3],
        new_table[3],
        new_gain[3],
        loss_sum,
        count,
        grad_norm,
    )


def solution(mesh):
    return jax.shard_map(
        on_device,
        mesh=mesh,
        in_specs=(
            P("dp", None),
            P("dp", None),
            P("dp", None),
            P("dp", None),
            P(),
            P("state", "dp", None, None),
            P("state", "dp", None, None),
            P("state", "dp", None, None),
            P("dp", None, None),
            P("state", "dp", None, None),
            P("state", "dp", None, None),
            P("state", "dp", None, None),
            P("dp", None, None),
            P("state", "dp", None, None),
            P("state", "dp", None, None),
            P("state", "dp", None, None),
            P("dp", None, None),
            P("state", "dp", None, None),
            P("state", "dp", None, None),
            P("state", "dp", None, None),
            P("dp", None, None),
        ),
        out_specs=(
            P("state", "dp", None, None),
            P("state", "dp", None, None),
            P("state", "dp", None, None),
            P("dp", None, None),
            P("state", "dp", None, None),
            P("state", "dp", None, None),
            P("state", "dp", None, None),
            P("dp", None, None),
            P("state", "dp", None, None),
            P("state", "dp", None, None),
            P("state", "dp", None, None),
            P("dp", None, None),
            P("state", "dp", None, None),
            P("state", "dp", None, None),
            P("state", "dp", None, None),
            P("dp", None, None),
            P(),
            P(),
            P(),
        ),
        check_vma=False,
    )
```

```python
import functools

import jax
import jax.numpy as jnp
from jax import lax
from jax.experimental import pallas as pl
from jax.experimental.pallas import tpu as pltpu
from jax.sharding import PartitionSpec as P

HEADS = 16
KEY_DIM = 128
GROUP = 128
STEP = 5
VAL_DIM = 128


NORM_EPS = 1e-06
LOWER_BOUND = 0.9
CLIP_NORM = 0.02
BETA_FIRST = 0.5
BETA_SECOND = 0.5
ADAM_EPS = 1e-08
LEARN_RATE = 0.02
GAIN_RATE = 0.2
WEIGHT_DECAY = 0.1
AVERAGE_DECAY = 0.9
FULL_PRECISION = lax.Precision.HIGHEST
LANES = 128
CHUNKS = 5
FEED = ((2, 3, 3), (6, 4), 6, (5, 6, 0))


def rms_norm(values, gain, width):
    mean = jnp.sum(values * values, axis=-1, keepdims=True) * (1.0 / width)
    return values * lax.rsqrt(mean + NORM_EPS) * gain


def forget_gates(forget_pre):
    key_gate = (1.0 - LOWER_BOUND) * jax.nn.sigmoid(-forget_pre)
    log_forget = jnp.log(LOWER_BOUND + (1.0 - LOWER_BOUND) * jax.nn.sigmoid(forget_pre))
    return key_gate, log_forget


def slot_mixer(query, key_gate, log_forget, values, pick, allowed, heads, key_part):
    slots = query.shape[0]
    tokens = key_gate.shape[0]
    blocks = tokens // GROUP
    order = jnp.arange(GROUP)
    lower = (order[:, None] >= order[None, :]).astype(jnp.float32)
    number = jnp.arange(blocks)
    before = (number[:, None] > number[None, :]).astype(jnp.float32)
    inside = jnp.einsum(
        "ts,bsk->btk", lower, log_forget.reshape(blocks, GROUP, -1), precision=FULL_PRECISION
    )
    total = inside[:, -1]
    offset = jnp.dot(before, total, precision=FULL_PRECISION)
    ends = offset + total
    along = (inside + offset[:, None]).reshape(tokens, -1)
    at_slots = jnp.dot(pick, along, precision=FULL_PRECISION)
    key_decay = key_gate * jnp.exp(total[:, None] - inside).reshape(tokens, -1)
    grown = query[None] * jnp.exp(jnp.minimum(at_slots[None] - ends[:, None], 16.0))
    key_decay = key_decay.reshape(blocks, GROUP, heads * KEY_DIM)
    column = jnp.arange(heads * KEY_DIM)
    of_head = (column % key_part) // (key_part // heads) == jnp.arange(heads)[:, None]
    grown = jnp.where(of_head[:, None, None], grown[None], 0.0)
    scores = jnp.einsum("hbnk,bgk->hnbg", grown, key_decay, precision=FULL_PRECISION)
    scores = jnp.where(allowed[None], scores.reshape(heads, slots, tokens), 0.0)
    mixed = jnp.einsum(
        "hns,shv->nhv", scores, values.reshape(tokens, heads, VAL_DIM), precision=FULL_PRECISION
    )
    return mixed.reshape(slots, -1)


def document_ids(starts, length):
    return jnp.sum((jnp.arange(length)[:, None] >= starts[None, :]).astype(jnp.int32), axis=1) - 1


def slot_index(owners, capacity):
    order = jnp.arange(owners.shape[0])
    earlier = (owners[:, None] == owners[None, :]) & (order[None, :] < order[:, None])
    ranks = jnp.sum(earlier.astype(jnp.int32), axis=1)
    return owners * capacity + ranks


def adam_update(weight, first, second, average, grad, scale, rate, decay, occupied):
    clipped = scale * grad
    first_new = BETA_FIRST * first + (1.0 - BETA_FIRST) * clipped
    second_new = BETA_SECOND * second + (1.0 - BETA_SECOND) * clipped * clipped
    first_hat = first_new / (1.0 - BETA_FIRST**STEP)
    second_hat = second_new / (1.0 - BETA_SECOND**STEP)
    weight_new = weight - rate * (first_hat / (jnp.sqrt(second_hat) + ADAM_EPS) + decay * weight)
    average_new = AVERAGE_DECAY * average + (1.0 - AVERAGE_DECAY) * weight_new
    return (
        weight_new * occupied,
        first_new * occupied,
        second_new * occupied,
        average_new * occupied,
    )


def adam_kernel(
    rate, decay, scale_ref, held_ref, weight, first, second, average, grad,
    weight_out, first_out, second_out, average_out
):
    occupied = held_ref[pl.program_id(0)]
    found = adam_update(
        weight[...],
        first[...],
        second[...],
        average[...],
        grad[...].astype(jnp.float32),
        scale_ref[0],
        rate,
        decay,
        occupied,
    )
    for out, value in zip((weight_out, first_out, second_out, average_out), found):
        out[...] = value


def adam_blocks(weight, first, second, average, grad, scale, rate, decay, occupied):
    capacity, block_rows, cols = weight.shape[1:]
    rows = 32
    block = pl.BlockSpec((1, 1, rows, cols), lambda i, j: (0, i, j, 0))
    scalar = pl.BlockSpec(memory_space=pltpu.SMEM)
    return pl.pallas_call(
        functools.partial(adam_kernel, rate, decay),
        grid=(capacity, block_rows // rows),
        out_shape=[jax.ShapeDtypeStruct(weight.shape, weight.dtype)] * 4,
        in_specs=[scalar, scalar] + [block] * 5,
        out_specs=[block] * 4,
        compiler_params=pltpu.CompilerParams(vmem_limit_bytes=48 * 2**20),
    )(scale.reshape(1), occupied, weight, first, second, average, grad)


def times_plain(left, right):
    return jnp.dot(left, right, preferred_element_type=jnp.float32)


def times_right(left, right):
    return lax.dot_general(
        left, right, (((1,), (1,)), ((), ())), preferred_element_type=jnp.float32
    )


def times_left(left, right):
    return lax.dot_general(
        left, right, (((0,), (0,)), ((), ())), preferred_element_type=jnp.float32
    )


def swiglu(joined, units, cols):
    gate = joined[:, :units]
    up = joined[:, units : 2 * units]
    return jnp.pad(jax.nn.silu(gate) * up, ((0, 0), (0, cols - units)))


EVERY = ("dp", "state")


def gather_state(values, axis=0):
    return lax.all_gather(values, "state", axis=axis, tiled=True)


def scatter_state(values, axis=0):
    return lax.psum_scatter(values, "state", scatter_dimension=axis, tiled=True)


def swap_dp(values):
    return lax.all_to_all(values, "dp", split_axis=0, concat_axis=0, tiled=True)


def spread_columns(own, parts):
    return own.reshape(own.shape[0], parts, -1).transpose(1, 0, 2)


def join_columns(split):
    return split.transpose(1, 0, 2).reshape(split.shape[1], -1)


MESH = pl.DeviceIdType.MESH


class Links:
    def __init__(self, sends, recvs):
        self.sends, self.recvs, self.used, self.open = sends, recvs, 0, []

    def copy(self, src, dst, dp, state):
        number = self.used
        self.used += 1
        made = pltpu.make_async_remote_copy(
            src_ref=src,
            dst_ref=dst,
            send_sem=self.sends.at[number],
            recv_sem=self.recvs.at[number],
            device_id=(dp, state),
            device_id_type=MESH,
        )
        made.start()
        self.open.append(made)
        return made

    def settle(self, copies):
        for made in copies:
            made.wait_send()
        self.open = [made for made in self.open if not any(made is one for one in copies)]

    def finish(self):
        for made in self.open:
            made.wait_send()


def nothing(place):
    del place


def greet(peers):
    barrier = pltpu.get_barrier_semaphore()
    for dp, state in peers:
        pl.semaphore_signal(barrier, inc=1, device_id=(dp, state), device_id_type=MESH)
    pl.semaphore_wait(barrier, len(peers))


def places(nd, ns):
    dp, st = lax.axis_index("dp"), lax.axis_index("state")
    return dp, st, lax.div(dp, 2), lax.rem(dp, 2), lax.div(st, 2), lax.rem(st, 2)


def near_peers(nd, ns):
    dp, st, z, y, x, c = places(nd, ns)
    deep, across = nd // 2, ns // 2
    peers = [(lax.rem(z + k, deep) * 2 + y, st) for k in range(1, deep)]
    peers.append((dp + 1 - 2 * y, st))
    peers += [(dp, lax.rem(x + k, across) * 2 + c) for k in range(1, across)]
    peers.append((dp, st + 1 - 2 * c))
    return peers


def add_up(parts):
    found = parts[0]
    for part in parts[1:]:
        found = found + part
    return found


def add_exponentials(parts):
    top = parts[0][0]
    for part in parts[1:]:
        top = jnp.maximum(top, part[0])
    total = add_up([part[1] * jnp.exp(part[0] - top) for part in parts])
    return jnp.stack([top, total, add_up([part[2] for part in parts])])


def combine_kernel(nd, ns, combine, in_ref, out_ref, near, far, sends, recvs):
    dp, st, z, y, x, c = places(nd, ns)
    deep = nd // 2
    plane = []
    for a in range(2):
        for b in range(ns):
            if a or b:
                plane.append((z * 2 + lax.rem(y + a, 2), lax.rem(st + b, ns)))
    line = [(lax.rem(z + k, deep) * 2 + y, st) for k in range(1, deep)]
    greet(plane + line)
    links = Links(sends, recvs)
    me = y * ns + st
    near[me] = in_ref[...]
    made = [links.copy(in_ref, near.at[me], *peer) for peer in plane]
    for copy in made:
        copy.wait_recv()
    far[z] = combine([near[i] for i in range(2 * ns)])
    made = [links.copy(far.at[z], far.at[z], *peer) for peer in line]
    for copy in made:
        copy.wait_recv()
    out_ref[...] = combine([far[i] for i in range(deep)])
    links.finish()


def combine_all(values, combine, number):
    nd, ns = lax.axis_size("dp"), lax.axis_size("state")
    copies = 2 * ns - 1 + nd // 2 - 1
    vmem = pl.BlockSpec(memory_space=pltpu.VMEM)
    return pl.pallas_call(
        functools.partial(combine_kernel, nd, ns, combine),
        out_shape=jax.ShapeDtypeStruct(values.shape, values.dtype),
        in_specs=[vmem],
        out_specs=vmem,
        scratch_shapes=[
            pltpu.VMEM((2 * ns,) + values.shape, values.dtype),
            pltpu.VMEM((nd // 2,) + values.shape, values.dtype),
            pltpu.SemaphoreType.DMA((copies,)),
            pltpu.SemaphoreType.DMA((copies,)),
        ],
        compiler_params=pltpu.CompilerParams(collective_id=number, has_side_effects=True),
    )(values)


def gather_all_kernel(nd, ns, in_ref, out_ref, sends, recvs):
    greet(near_peers(nd, ns))
    links = Links(sends, recvs)
    gather_body(nd, ns, links, in_ref, out_ref)
    links.finish()


def gather_body(nd, ns, links, in_ref, out_ref, meanwhile=nothing):
    dp, st, z, y, x, c = places(nd, ns)
    deep, across = nd // 2, ns // 2
    half = in_ref.shape[1] // 2
    cols = (pl.ds(0, half), pl.ds(half, half))
    to_y = (dp + 1 - 2 * y, st)
    to_core = (dp, st + 1 - 2 * c)
    other_y = 1 - y

    def x_at(k):
        return lax.rem(x + k, across)

    def to_x(k):
        return (dp, x_at(k) * 2 + c)

    def group(xx, yy, part):
        return out_ref.at[c, xx, yy, :, :, cols[part]]

    def send(xx, yy, part, place):
        return links.copy(group(xx, yy, part), group(xx, yy, part), *place)

    out_ref[c, x, y, z] = in_ref[...]
    first = []
    for part in range(2):
        for k in range(1, deep):
            there = (lax.rem(z + k, deep) * 2 + y, st)
            first.append(
                links.copy(
                    in_ref.at[:, cols[part]], out_ref.at[c, x, y, z, :, cols[part]], *there
                )
            )
    for made in first[: deep - 1]:
        made.wait_recv()
    a_y = send(x, y, 0, to_y)
    for made in first[deep - 1 :]:
        made.wait_recv()
    b_x = [send(x, y, 1, to_x(k)) for k in range(1, across)]
    a_x = [send(x, y, 0, to_x(k)) for k in range(1, across)]
    b_y = send(x, y, 1, to_y)
    arriving = [send(x, y, 0, to_core), send(x, y, 1, to_core)]
    meanwhile(0)
    a_y.wait_recv()
    a_xy = [send(x, other_y, 0, to_x(k)) for k in range(1, across)]
    arriving.append(send(x, other_y, 0, to_core))
    b_xy = []
    for k in range(1, across):
        b_x[k - 1].wait_recv()
        from_x = lax.rem(x - k + across, across)
        b_xy.append(send(from_x, y, 1, to_y))
        arriving.append(send(from_x, y, 1, to_core))
    meanwhile(1)
    for k in range(1, across):
        a_x[k - 1].wait_recv()
        arriving.append(send(lax.rem(x - k + across, across), y, 0, to_core))
    b_y.wait_recv()
    arriving.append(send(x, other_y, 1, to_core))
    for k in range(1, across):
        from_x = lax.rem(x - k + across, across)
        a_xy[k - 1].wait_recv()
        arriving.append(send(from_x, other_y, 0, to_core))
        b_xy[k - 1].wait_recv()
        arriving.append(send(from_x, other_y, 1, to_core))
    for made in arriving:
        made.wait_recv()
    links.settle(first + [a_y, b_y] + b_x + a_x + a_xy + b_xy + arriving)


def gather_copies(nd, ns):
    deep, across = nd // 2, ns // 2
    return 2 * (deep - 1) + 2 + 4 * (across - 1) + 4 * across


def gather_all(values, number):
    nd, ns = lax.axis_size("dp"), lax.axis_size("state")
    rows, wide = values.shape
    deep, across = nd // 2, ns // 2
    copies = gather_copies(nd, ns)
    vmem = pl.BlockSpec(memory_space=pltpu.VMEM)
    out = pl.pallas_call(
        functools.partial(gather_all_kernel, nd, ns),
        out_shape=jax.ShapeDtypeStruct((2, across, 2, deep, rows, wide), values.dtype),
        in_specs=[vmem],
        out_specs=vmem,
        scratch_shapes=[pltpu.SemaphoreType.DMA((copies,)), pltpu.SemaphoreType.DMA((copies,))],
        compiler_params=pltpu.CompilerParams(
            collective_id=number, has_side_effects=True, vmem_limit_bytes=40 * 2**20
        ),
    )(values)
    return out.reshape(nd * ns * rows, wide)


def scatter_all_kernel(nd, ns, in_ref, cargo_ref, out_ref, cargo_out, local, *scratch):
    sends, recvs = scratch[-2:]
    dp, st, z, y, x, c = places(nd, ns)
    dp_peers = [(lax.rem(dp + k, nd), st) for k in range(1, nd)]
    x_peers = [(dp, lax.rem(x + k, ns // 2) * 2 + c) for k in range(1, ns // 2)]
    greet(dp_peers + x_peers + [(dp, st + 1 - 2 * c)])
    links = Links(sends, recvs)
    own_copy = pltpu.make_async_copy(cargo_ref.at[dp], cargo_out.at[dp], local.at[0])
    own_copy.start()
    chunk = cargo_ref.shape[1] // CHUNKS
    queue = [(peer, i) for i in range(CHUNKS) for peer in dp_peers]
    third = -(-len(queue) // 3)
    pieces = []

    def feed(place):
        for peer, i in queue[place * third : (place + 1) * third]:
            rows = pl.ds(i * chunk, chunk)
            pieces.append(links.copy(cargo_ref.at[peer[0], rows], cargo_out.at[dp, rows], *peer))

    scatter_body(nd, ns, links, in_ref, out_ref, scratch[:-2], feed)
    for made in pieces:
        made.wait_recv()
    own_copy.wait()
    links.finish()


def scatter_body(nd, ns, links, in_ref, out_ref, scratch, meanwhile=nothing):
    rc, acc, rx_a, ry_a, rz_a, ry_b, rx_b, rz_b = scratch
    dp, st, z, y, x, c = places(nd, ns)
    deep, across = nd // 2, ns // 2
    half = in_ref.shape[5] // 2
    cols = (pl.ds(0, half), pl.ds(half, half))
    to_y = (dp + 1 - 2 * y, st)
    to_core = (dp, st + 1 - 2 * c)
    ys = (y, 1 - y)

    def x_at(k):
        return lax.rem(x + k, across)

    def to_x(k):
        return (dp, x_at(k) * 2 + c)

    core = {}
    order = [(k, ky, 0) for k in range(1, across) for ky in (1, 0)]
    order += [(k, 1, 1) for k in range(across)]
    order += [(0, 1, 0)] + [(k, 0, 1) for k in range(1, across)] + [(0, 0, 0), (0, 0, 1)]
    for k, ky, part in order:
        core[k, ky, part] = links.copy(
            in_ref.at[1 - c, x_at(k), ys[ky], :, :, cols[part]],
            rc.at[x_at(k), ys[ky], :, :, cols[part]],
            *to_core,
        )

    def total(k, ky, part, zz, others):
        found = in_ref[c, x_at(k), ys[ky], zz, :, cols[part]].astype(jnp.float32)
        found += rc[x_at(k), ys[ky], zz, :, cols[part]].astype(jnp.float32)
        for other in others:
            found += other[zz].astype(jnp.float32)
        return found

    def add(k, ky, part, others):
        core[k, ky, part].wait_recv()

        @pl.loop(0, deep)
        def _(zz):
            acc[x_at(k), ys[ky], zz, :, cols[part]] = total(k, ky, part, zz, others).astype(
                acc.dtype
            )

        return acc.at[x_at(k), ys[ky], :, :, cols[part]]

    meanwhile(0)
    a_x, b_y = {}, {}
    for k in range(1, across):
        for ky in (1, 0):
            a_x[k, ky] = links.copy(add(k, ky, 0, []), rx_a.at[k - 1, ky], *to_x(k))
    for k in range(across):
        b_y[k] = links.copy(add(k, 1, 1, []), ry_b.at[k], *to_y)
    meanwhile(1)
    for k in range(1, across):
        a_x[k, 1].wait_recv()
    a_y = links.copy(
        add(0, 1, 0, [rx_a.at[k - 1, 1] for k in range(1, across)]), ry_a, *to_y
    )
    b_x = {}
    for k in range(1, across):
        b_y[k].wait_recv()
        b_x[k] = links.copy(add(k, 0, 1, [ry_b.at[k]]), rx_b.at[k - 1], *to_x(k))
    meanwhile(2)
    for k in range(1, across):
        a_x[k, 0].wait_recv()
    a_y.wait_recv()
    left = [rx_a.at[k - 1, 0] for k in range(1, across)] + [ry_a]
    add(0, 0, 0, left)

    def send_z(part, land):
        return [
            links.copy(
                acc.at[x, y, lax.rem(z + k, deep), :, cols[part]],
                land.at[k - 1],
                lax.rem(z + k, deep) * 2 + y,
                st,
            )
            for k in range(1, deep)
        ]

    a_z = send_z(0, rz_a)
    b_y[0].wait_recv()
    for k in range(1, across):
        b_x[k].wait_recv()
    right = [ry_b.at[0]] + [rx_b.at[k - 1] for k in range(1, across)]
    add(0, 0, 1, right)
    b_z = send_z(1, rz_b)
    for part, made, others, land in ((0, a_z, left, rz_a), (1, b_z, right, rz_b)):
        found = total(0, 0, part, z, others)
        for k in range(1, deep):
            made[k - 1].wait_recv()
            found += land[k - 1].astype(jnp.float32)
        out_ref[:, cols[part]] = found
    links.settle(
        list(core.values()) + list(a_x.values()) + list(b_y.values()) + list(b_x.values())
        + [a_y] + a_z + b_z
    )


def scatter_copies(nd, ns):
    deep, across = nd // 2, ns // 2
    return 4 * across + 2 * (across - 1) + across + 1 + (across - 1) + 2 * (deep - 1)


def scatter_scratch(nd, ns, rows, wide, kind):
    deep, across = nd // 2, ns // 2
    half = wide // 2
    return [
        pltpu.VMEM((across, 2, deep, rows, wide), kind),
        pltpu.VMEM((across, 2, deep, rows, wide), kind),
        pltpu.VMEM((across - 1, 2, deep, rows, half), kind),
        pltpu.VMEM((deep, rows, half), kind),
        pltpu.VMEM((deep - 1, rows, half), kind),
        pltpu.VMEM((across, deep, rows, half), kind),
        pltpu.VMEM((across - 1, deep, rows, half), kind),
        pltpu.VMEM((deep - 1, rows, half), kind),
    ]


def scatter_all(values, cargo, number):
    nd, ns = lax.axis_size("dp"), lax.axis_size("state")
    deep, across = nd // 2, ns // 2
    rows, wide = values.shape[0] // (nd * ns), values.shape[1]
    copies = scatter_copies(nd, ns) + (nd - 1) * CHUNKS
    vmem = pl.BlockSpec(memory_space=pltpu.VMEM)
    hbm = pl.BlockSpec(memory_space=pl.ANY)
    kind = values.dtype
    return pl.pallas_call(
        functools.partial(scatter_all_kernel, nd, ns),
        out_shape=[
            jax.ShapeDtypeStruct((rows, wide), jnp.float32),
            jax.ShapeDtypeStruct(cargo.shape, cargo.dtype),
        ],
        in_specs=[vmem, hbm],
        out_specs=[vmem, hbm],
        scratch_shapes=[pltpu.SemaphoreType.DMA((1,))]
        + scatter_scratch(nd, ns, rows, wide, kind)
        + [pltpu.SemaphoreType.DMA((copies,)), pltpu.SemaphoreType.DMA((copies,))],
        compiler_params=pltpu.CompilerParams(
            collective_id=number, has_side_effects=True, vmem_limit_bytes=40 * 2**20
        ),
    )(values.reshape(2, across, 2, deep, rows, wide), cargo)


def front_kernel(
    nd,
    ns,
    depth_used,
    small_ref,
    gain_ref,
    table_ref,
    keys_ref,
    rest_ref,
    parts_ref,
    small_out,
    gain_out,
    rows_out,
    keys_out,
    rest_out,
    parts_out,
    looked,
    rc,
    acc,
    rx,
    fin,
    sums,
    sends,
    recvs,
    local,
):
    dp, st, z, y, x, c = places(nd, ns)
    deep, across = nd // 2, ns // 2
    own = table_ref.shape[0]
    tokens = rows_out.shape[1]
    part = tokens // ns
    to_core = (dp, st + 1 - 2 * c)
    to_y = (dp + 1 - 2 * y, st)
    other_y = dp + 1 - 2 * y
    dp_peers = [(lax.rem(dp + k, nd), st) for k in range(1, nd)]
    state_peers = [(dp, lax.rem(st + k, ns)) for k in range(1, ns)]
    greet(dp_peers + state_peers)
    links = Links(sends, recvs)

    ids_made = {}
    small_out[dp] = small_ref[...]
    gain_out[dp] = gain_ref[...]
    for k in range(1, nd):
        ids_made[k] = links.copy(small_ref, small_out.at[dp], *dp_peers[k - 1])
    gain_made = [links.copy(gain_ref, gain_out.at[dp], *peer) for peer in dp_peers]

    here = [
        pltpu.make_async_copy(keys_ref.at[st], keys_out.at[st, dp], local.at[0]),
        pltpu.make_async_copy(rest_ref, rest_out.at[dp], local.at[1]),
        pltpu.make_async_copy(parts_ref.at[dp], parts_out.at[dp], local.at[2]),
    ]
    for made in here:
        made.start()
    key_made = [
        links.copy(keys_ref.at[peer[1]], keys_out.at[st, dp], *peer) for peer in state_peers
    ]

    class Gather:
        def __init__(self, view):
            self.view = view
            self.base = links.used
            links.used += 2 * (deep - 1) + 1 + 2 * (deep - 1)

        def copy(self, number, owner, place):
            return pltpu.make_async_remote_copy(
                src_ref=self.view(owner),
                dst_ref=self.view(owner),
                send_sem=sends.at[self.base + number],
                recv_sem=recvs.at[self.base + number],
                device_id=place,
                device_id_type=MESH,
            )

        def pass_on(self, way, step):
            behind = z - way * step
            ahead = z + way
            number = step if way > 0 else deep - 1 + step

            def go(made):
                @pl.when((behind >= 0) & (behind < deep) & (ahead >= 0) & (ahead < deep))
                def _():
                    made(self.copy(number, behind * 2 + y, (ahead * 2 + y, st)))

            return go

        def begin(self):
            self.copy(2 * (deep - 1), dp, to_y).start()
            for way in (1, -1):
                self.pass_on(way, 0)(lambda made: made.start())

        def arrive(self, way, step):
            began = z - way * (step + 1)
            number = step if way > 0 else deep - 1 + step

            @pl.when((began >= 0) & (began < deep))
            def _():
                self.copy(number, began * 2 + y, to_y).wait_recv()
                self.copy(2 * (deep - 1) + 1 + number, began * 2 + y, to_y).start()

            if step + 1 < deep - 1:
                self.pass_on(way, step + 1)(lambda made: made.start())

        def finish(self):
            self.copy(2 * (deep - 1), other_y, to_y).wait_recv()
            self.copy(2 * (deep - 1), dp, to_y).wait_send()
            for way in (1, -1):
                for step in range(deep - 1):
                    began = z - way * (step + 1)
                    number = step if way > 0 else deep - 1 + step
                    self.pass_on(way, step)(lambda made: made.wait_send())

                    @pl.when((began >= 0) & (began < deep))
                    def _():
                        made = self.copy(2 * (deep - 1) + 1 + number, began * 2 + y, to_y)
                        made.wait_send()
                        made.wait_recv()

    rest = Gather(lambda owner: rest_out.at[owner])
    keys = Gather(lambda owner: keys_out.at[:, owner])
    here[1].wait()
    rest.begin()

    def swap(k):
        there = lax.rem(dp + k, nd)
        return links.copy(parts_ref.at[there], parts_out.at[dp], there, st)

    swapped = [swap(k) for k in range(1, nd // 2)]
    here[0].wait()
    for made in key_made:
        made.wait_recv()
    keys.begin()

    def x_at(k):
        return lax.rem(x + k, across)

    def row_at(k):
        return lax.rem(dp + k, nd)

    def block(k, kx, cc):
        start = (x_at(kx) * 2 + cc) * part
        return looked.at[k, :, pl.ds(pl.multiple_of(start, part), part)]

    def place(owner, share):
        return rows_out.at[
            pl.ds(pl.multiple_of(owner * own, own), own),
            pl.ds(pl.multiple_of(share * part, part), part),
        ]

    def add(sources, target):
        @pl.loop(0, own // 32)
        def _(i):
            rows = pl.ds(pl.multiple_of(i * 32, 32), 32)
            found = sources[0][rows, :].astype(jnp.float32)
            for source in sources[1:]:
                found += source[rows, :].astype(jnp.float32)
            target[rows, :] = found.astype(target.dtype)

    depth = table_ref.shape[1]
    piece = min(1024, depth)
    span = 2 * LANES

    def look(k):
        row = row_at(k)

        @pl.loop(0, tokens // span)
        def _(i):
            ids = jnp.concatenate(
                [small_out[row, pl.ds(2 * i, 1), :], small_out[row, pl.ds(2 * i + 1, 1), :]],
                axis=1,
            )
            ids = ids - st * depth_used
            sums[...] = jnp.zeros_like(sums)

            @pl.loop(0, depth // piece)
            def _(j):
                number = lax.broadcasted_iota(jnp.int32, (piece, span), 0)
                hit = jnp.where(number == ids - j * piece, 1.0, 0.0).astype(jnp.bfloat16)
                cols = pl.ds(pl.multiple_of(j * piece, piece), piece)
                sums[...] += jnp.dot(
                    table_ref[:, cols], hit, preferred_element_type=jnp.float32
                )

            cols = pl.ds(pl.multiple_of(i * span, span), span)
            looked[k, :, cols] = sums[...].astype(looked.dtype)

    turn = list(range(1, nd)) + [0]
    core, across_x, across_dp = {}, {}, {}

    def start_core(k):
        for kx in list(range(1, across)) + [0]:
            core[k, kx] = links.copy(block(k, kx, 1 - c), rc.at[k, kx], *to_core)

    def start_x(k):
        for kx in range(1, across):
            core[k, kx].wait_recv()
            add([block(k, kx, c), rc.at[k, kx]], acc.at[k, kx - 1])
            across_x[k, kx] = links.copy(
                acc.at[k, kx - 1], rx.at[k, kx - 1], dp, x_at(kx) * 2 + c
            )

    def start_dp(k):
        core[k, 0].wait_recv()
        sources = [block(k, 0, c), rc.at[k, 0]]
        for kx in range(1, across):
            across_x[k, kx].wait_recv()
            sources.append(rx.at[k, kx - 1])
        if k:
            add(sources, fin.at[k - 1])
            across_dp[k] = links.copy(fin.at[k - 1], place(dp, st), row_at(k), st)
        else:
            add(sources, place(dp, st))

    chores = []
    for step in range(deep - 1):
        for way in (1, -1):
            chores.append(functools.partial(rest.arrive, way, step))
    for step in range(deep - 1):
        for way in (1, -1):
            chores.append(functools.partial(keys.arrive, way, step))
    each = -(-len(chores) // nd)
    for number, k in enumerate(turn):
        if k:
            ids_made[nd - k].wait_recv()
        look(k)
        start_core(k)
        if number >= 1:
            start_x(turn[number - 1])
        if number >= 2:
            start_dp(turn[number - 2])
        for _ in range(each):
            if number >= 2 and chores:
                chores.pop(0)()
    start_x(turn[-1])
    start_dp(turn[-2])
    start_dp(turn[-1])
    swapped += [swap(k) for k in range(nd // 2, nd)]
    later, last = {}, []
    for number, k in enumerate([0] + list(range(1, nd))):
        owner = lax.rem(dp - k + nd, nd)
        if k:
            across_dp[k].wait_recv()
        for kx in range(1, across):
            later[k, kx] = links.copy(
                place(owner, st), place(owner, st), dp, x_at(kx) * 2 + c
            )
        last.append(links.copy(place(owner, st), place(owner, st), *to_core))
        if chores:
            chores.pop(0)()
    for k in range(nd):
        owner = lax.rem(dp - k + nd, nd)
        for kx in range(1, across):
            later[k, kx].wait_recv()
            share = lax.rem(x - kx + across, across) * 2 + c
            last.append(links.copy(place(owner, share), place(owner, share), *to_core))
    while chores:
        chores.pop(0)()
    for made in last + swapped + gain_made:
        made.wait_recv()
    here[2].wait()
    links.finish()
    rest.finish()
    keys.finish()


def front(small, gain, table, keys, rest, parts, tokens, vocab, number):
    nd, ns = lax.axis_size("dp"), lax.axis_size("state")
    deep, across = nd // 2, ns // 2
    own = table.shape[0]
    part = tokens // ns
    kind = table.dtype
    copies = 2 * (nd - 1) + ns - 1 + 2 * (4 * (deep - 1) + 1) + nd - 1
    copies += nd * across + nd * (across - 1) + nd - 1 + nd * across + nd * (across - 1)
    vmem = pl.BlockSpec(memory_space=pltpu.VMEM)
    hbm = pl.BlockSpec(memory_space=pl.ANY)
    return pl.pallas_call(
        functools.partial(front_kernel, nd, ns, vocab),
        out_shape=[
            jax.ShapeDtypeStruct((nd,) + small.shape, small.dtype),
            jax.ShapeDtypeStruct((nd,) + gain.shape, gain.dtype),
            jax.ShapeDtypeStruct((nd * own, tokens), kind),
            jax.ShapeDtypeStruct((ns, nd) + keys.shape[1:], kind),
            jax.ShapeDtypeStruct((nd,) + rest.shape, kind),
            jax.ShapeDtypeStruct(parts.shape, kind),
        ],
        in_specs=[vmem, vmem, vmem, hbm, hbm, hbm],
        out_specs=[vmem, vmem, vmem, hbm, hbm, hbm],
        scratch_shapes=[
            pltpu.VMEM((nd, own, tokens), kind),
            pltpu.VMEM((nd, across, own, part), kind),
            pltpu.VMEM((nd, across - 1, own, part), kind),
            pltpu.VMEM((nd, across - 1, own, part), kind),
            pltpu.VMEM((nd - 1, own, part), kind),
            pltpu.VMEM((own, 2 * LANES), jnp.float32),
            pltpu.SemaphoreType.DMA((copies,)),
            pltpu.SemaphoreType.DMA((copies,)),
            pltpu.SemaphoreType.DMA((3,)),
        ],
        compiler_params=pltpu.CompilerParams(
            collective_id=number, has_side_effects=True, vmem_limit_bytes=52 * 2**20
        ),
        cost_estimate=pl.CostEstimate(
            flops=2 * table.size * nd * tokens, bytes_accessed=4 * parts.size, transcendentals=0
        ),
    )(small, gain, table, keys, rest, parts)


def slots_back_kernel(
    nd,
    ns,
    width,
    units,
    part_hbm,
    table_ref,
    two_ref,
    one_ref,
    gain_ref,
    wd_ref,
    wgu_ref,
    gu_ref,
    hidden_ref,
    rows_ref,
    one_out,
    table_out,
    ffn_out,
    gains_out,
    part_ref,
    summed,
    low,
    down,
    dgu,
    dffn,
    local,
    *scratch,
):
    sends, recvs = scratch[-2:]
    dp, st, z, y, x, c = places(nd, ns)
    deep, across = nd // 2, ns // 2
    count, wide = two_ref.shape
    every = nd * ns * count
    dp_peers = [(lax.rem(dp + k, nd), st) for k in range(1, nd)]
    state_peers = [(dp, lax.rem(st + k, ns)) for k in range(1, ns)]
    fill = pltpu.make_async_copy(part_hbm, part_ref, local.at[2])
    fill.start()
    greet(dp_peers + state_peers)
    links = Links(sends, recvs)
    own_copy = pltpu.make_async_copy(table_ref.at[dp], table_out.at[dp], local.at[0])
    own_copy.start()
    local_copies = [own_copy]
    own = table_ref.shape[1]
    chunk = own // CHUNKS
    queue = [(peer, i) for i in range(CHUNKS) for peer in dp_peers]
    swapped = []

    def feed(amount):
        for _ in range(min(amount, len(queue))):
            peer, i = queue.pop(0)
            rows = pl.ds(i * chunk, chunk)
            swapped.append(
                links.copy(table_ref.at[peer[0], rows], table_out.at[dp, rows], *peer)
            )

    def feeding(amounts):
        return lambda place: feed(amounts[place])

    def norm_back(grad, values, gain, row):
        mean = jnp.sum(values * values, axis=1, keepdims=True) * (1.0 / width)
        root = lax.rsqrt(mean + NORM_EPS)
        scaled = grad * gain
        inner = jnp.sum(scaled * values, axis=1, keepdims=True) * (1.0 / width)
        gains_out[pl.ds(row, 1), :] = jnp.sum(grad * values * root, axis=0, keepdims=True)
        return scaled * root - values * (root * root * root * inner)

    fill.wait()
    scatter_body(nd, ns, links, part_ref, summed, scratch[:-2], feeding(FEED[0]))
    summed[...] = norm_back(summed[...], two_ref[...], gain_ref[pl.ds(1, 1), :], 1)
    low[...] = summed[...].astype(low.dtype)
    gather_body(nd, ns, links, low, down, feeding(FEED[1]))
    feed(FEED[2])

    inner_cols = gu_ref.shape[1]
    step = deep * count
    flat_down = down

    @pl.loop(0, 2 * across * 2)
    def _(i):
        cc, rest = lax.div(i, 2 * across), lax.rem(i, 2 * across)
        xx, yy = lax.div(rest, 2), lax.rem(rest, 2)
        rows = pl.ds(pl.multiple_of(i * step, step), step)
        grad = jnp.dot(
            flat_down[cc, xx, yy].reshape(step, wide),
            wd_ref[...],
            preferred_element_type=jnp.float32,
        )
        grad = jnp.concatenate(
            [grad, jnp.zeros((step, inner_cols - grad.shape[1]), jnp.float32)], axis=1
        ) if inner_cols > grad.shape[1] else grad[:, :inner_cols]
        gate = gu_ref[rows, :]
        up = pltpu.roll(gate, inner_cols - units, 1)
        gated = 1.0 / (1.0 + jnp.exp(-gate))
        grad_gate = grad * up * (gated * (1.0 + gate * (1.0 - gated)))
        grad_up = pltpu.roll(grad * gate * gated, units, 1)
        lanes = lax.broadcasted_iota(jnp.int32, grad_gate.shape, 1)
        joined = jnp.where(lanes < units, grad_gate, grad_up).astype(dgu.dtype)
        dgu[rows, :] = joined
        part_ref[cc, xx, yy] = (
            lax.dot_general(
                joined, wgu_ref[...], (((1,), (1,)), ((), ())), preferred_element_type=jnp.float32
            )
            .astype(part_ref.dtype)
            .reshape(deep, count, wide)
        )

    def weight_grads(place):
        feed(FEED[3][place])
        if place:
            return
        span = 2 * LANES

        @pl.loop(0, wide // span)
        def _(i):
            cols = pl.ds(pl.multiple_of(i * span, span), span)
            dffn[cols, :inner_cols] = lax.dot_general(
                rows_ref[:, cols], dgu[...], (((0,), (0,)), ((), ())),
                preferred_element_type=jnp.float32,
            ).astype(dgu.dtype)
            dffn[cols, inner_cols:] = lax.dot_general(
                flat_down[:, :, :, :, :, cols].reshape(every, span), hidden_ref[...],
                (((0,), (0,)), ((), ())),
                preferred_element_type=jnp.float32,
            ).astype(dgu.dtype)

        home = pltpu.make_async_copy(dffn, ffn_out, local.at[1])
        home.start()
        local_copies.append(home)

    grad_two = summed[...]
    scatter_body(nd, ns, links, part_ref, summed, scratch[:-2], weight_grads)
    grad_one = grad_two + norm_back(summed[...], one_ref[...], gain_ref[pl.ds(0, 1), :], 0)
    one_out[st] = grad_one.astype(one_out.dtype)
    low[...] = grad_one.astype(low.dtype)
    made = [links.copy(low, one_out.at[st], *peer) for peer in state_peers]
    for copy in made:
        copy.wait_recv()
    feed(len(queue))
    for copy in swapped:
        copy.wait_recv()
    for copy in local_copies:
        copy.wait()
    links.finish()


def slots_back(part, table, two, one, gain, wd, wgu, gu, hidden, rows, width, units, number):
    nd, ns = lax.axis_size("dp"), lax.axis_size("state")
    deep, across = nd // 2, ns // 2
    count, wide = two.shape
    kind = part.dtype
    cols = wgu.shape[1] + wd.shape[1]
    copies = 2 * scatter_copies(nd, ns) + gather_copies(nd, ns) + (nd - 1) * CHUNKS + ns - 1
    vmem = pl.BlockSpec(memory_space=pltpu.VMEM)
    hbm = pl.BlockSpec(memory_space=pl.ANY)
    six = (2, across, 2, deep, count, wide)
    out = pl.pallas_call(
        functools.partial(slots_back_kernel, nd, ns, width, units),
        out_shape=[
            jax.ShapeDtypeStruct((ns, count, wide), kind),
            jax.ShapeDtypeStruct(table.shape, kind),
            jax.ShapeDtypeStruct((wide, cols), kind),
            jax.ShapeDtypeStruct((2, wide), jnp.float32),
        ],
        in_specs=[hbm, hbm] + [vmem] * 8,
        out_specs=[vmem, hbm, hbm, vmem],
        scratch_shapes=[
            pltpu.VMEM(six, kind),
            pltpu.VMEM((count, wide), jnp.float32),
            pltpu.VMEM((count, wide), kind),
            pltpu.VMEM(six, kind),
            pltpu.VMEM((nd * ns * count, wgu.shape[1]), kind),
            pltpu.VMEM((wide, cols), kind),
            pltpu.SemaphoreType.DMA((3,)),
        ]
        + scatter_scratch(nd, ns, count, wide, kind)
        + [pltpu.SemaphoreType.DMA((copies,)), pltpu.SemaphoreType.DMA((copies,))],
        compiler_params=pltpu.CompilerParams(
            collective_id=number, has_side_effects=True, vmem_limit_bytes=58 * 2**20
        ),
        cost_estimate=pl.CostEstimate(
            flops=8 * rows.size * cols, bytes_accessed=100 * part.size, transcendentals=0
        ),
    )(part.reshape(six), table, two, one, gain, wd, wgu, gu, hidden, rows)
    return (out[0].reshape(ns * count, wide),) + tuple(out[1:])


def rows_back_kernel(
    nd, ns, width, in_ref, stream_ref, gain_ref, more_ref, out_ref, gain_out, rc, acc, rx, fin, low,
    sends, recvs
):
    dp, st, z, y, x, c = places(nd, ns)
    across = ns // 2
    tokens = in_ref.shape[1]
    own = in_ref.shape[0] // nd
    part = tokens // ns
    to_core = (dp, st + 1 - 2 * c)
    dp_peers = [(lax.rem(dp + k, nd), st) for k in range(1, nd)]
    peers = dp_peers + [(dp, lax.rem(x + k, across) * 2 + c) for k in range(1, across)]
    greet(peers + [to_core])
    links = Links(sends, recvs)

    def x_at(k):
        return lax.rem(x + k, across)

    def rows_of(owner):
        return pl.ds(pl.multiple_of(owner * own, own), own)

    def block(k, kx, cc):
        start = (x_at(kx) * 2 + cc) * part
        return in_ref.at[pl.ds(k * own, own), pl.ds(pl.multiple_of(start, part), part)]

    def place(row, share):
        return out_ref.at[:, pl.ds(pl.multiple_of(row * tokens + share * part, part), part)]

    def add(sources, target):
        @pl.loop(0, own // 32)
        def _(i):
            rows = pl.ds(pl.multiple_of(i * 32, 32), 32)
            found = sources[0][rows, :].astype(jnp.float32)
            for source in sources[1:]:
                found += source[rows, :].astype(jnp.float32)
            target[rows, :] = found.astype(target.dtype)

    core, across_x = {}, {}
    for kx in list(range(1, across)) + [0]:
        for k in range(nd):
            core[k, kx] = links.copy(block(k, kx, 1 - c), rc.at[k, kx], *to_core)
    for kx in range(1, across):
        for k in range(nd):
            core[k, kx].wait_recv()
            add([block(k, kx, c), rc.at[k, kx]], acc.at[k, kx - 1])
            across_x[k, kx] = links.copy(
                acc.at[k, kx - 1], rx.at[k, kx - 1], dp, x_at(kx) * 2 + c
            )
    for k in range(nd):
        core[k, 0].wait_recv()
        sources = [block(k, 0, c), rc.at[k, 0]]
        for kx in range(1, across):
            across_x[k, kx].wait_recv()
            sources.append(rx.at[k, kx - 1])
        add(sources, fin.at[pl.ds(k * own, own), :])

    step = 32
    pieces = in_ref.shape[0] // step

    def at(i):
        return pl.ds(pl.multiple_of(i * step, step), step)

    def gather_sums(i, carry):
        square, inner = carry
        values = stream_ref[at(i), :].astype(jnp.float32)
        scaled = fin[at(i), :] * gain_ref[at(i), :] * values
        square = square + jnp.sum(values * values, axis=0, keepdims=True)
        return square, inner + jnp.sum(scaled, axis=0, keepdims=True)

    none = jnp.zeros((1, part), jnp.float32)
    square, inner = lax.fori_loop(0, pieces, gather_sums, (none, none))
    root = lax.rsqrt(square * (1.0 / width) + NORM_EPS)
    inner = inner * (1.0 / width) * root * root * root

    @pl.loop(0, pieces)
    def _(i):
        values = stream_ref[at(i), :].astype(jnp.float32)
        grad = fin[at(i), :]
        gain_out[at(i), :] = jnp.sum(grad * values * root, axis=1, keepdims=True)
        found = grad * gain_ref[at(i), :] * root - values * inner + more_ref[at(i), :]
        low[at(i), :] = found.astype(low.dtype)

    swapped = [links.copy(low.at[rows_of(p[0]), :], place(dp, st), *p) for p in dp_peers]
    place(dp, st)[...] = low[rows_of(dp), :]
    later, last = {}, []
    for k in range(nd):
        row = lax.rem(dp - k + nd, nd)
        if k:
            swapped[k - 1].wait_recv()
        for kx in range(1, across):
            later[k, kx] = links.copy(place(row, st), place(row, st), dp, x_at(kx) * 2 + c)
        last.append(links.copy(place(row, st), place(row, st), *to_core))
    for k in range(nd):
        row = lax.rem(dp - k + nd, nd)
        for kx in range(1, across):
            later[k, kx].wait_recv()
            share = lax.rem(x - kx + across, across) * 2 + c
            last.append(links.copy(place(row, share), place(row, share), *to_core))
    for made in last:
        made.wait_recv()
    links.finish()


def rows_back(values, stream, gain, more, width, number):
    nd, ns = lax.axis_size("dp"), lax.axis_size("state")
    across = ns // 2
    wide, tokens = values.shape
    own, part = wide // nd, tokens // ns
    copies = nd * across + nd * (across - 1) + nd - 1 + nd * across + nd * (across - 1)
    vmem = pl.BlockSpec(memory_space=pltpu.VMEM)
    kind = values.dtype
    return pl.pallas_call(
        functools.partial(rows_back_kernel, nd, ns, width),
        out_shape=[
            jax.ShapeDtypeStruct((own, nd * tokens), kind),
            jax.ShapeDtypeStruct((wide, 1), jnp.float32),
        ],
        in_specs=[vmem] * 4,
        out_specs=[vmem] * 2,
        scratch_shapes=[
            pltpu.VMEM((nd, across, own, part), kind),
            pltpu.VMEM((nd, across - 1, own, part), kind),
            pltpu.VMEM((nd, across - 1, own, part), kind),
            pltpu.VMEM((wide, part), jnp.float32),
            pltpu.VMEM((wide, part), kind),
            pltpu.SemaphoreType.DMA((copies,)),
            pltpu.SemaphoreType.DMA((copies,)),
        ],
        compiler_params=pltpu.CompilerParams(
            collective_id=number, has_side_effects=True, vmem_limit_bytes=48 * 2**20
        ),
        cost_estimate=pl.CostEstimate(
            flops=0, bytes_accessed=60 * values.size, transcendentals=0
        ),
    )(values, stream, gain, more)


def state_sum_kernel(nd, ns, in_ref, out_ref, land, sends, recvs):
    dp, st = lax.axis_index("dp"), lax.axis_index("state")
    peers = [(dp, lax.rem(st + k, ns)) for k in range(1, ns)]
    greet(peers)
    links = Links(sends, recvs)
    made = [
        links.copy(in_ref.at[there[1]], land.at[k], *there) for k, there in enumerate(peers)
    ]
    found = in_ref[st].astype(jnp.float32)
    for k in range(ns - 1):
        made[k].wait_recv()
        found += land[k].astype(jnp.float32)
    out_ref[...] = found
    links.finish()


def state_sum(values, number):
    nd, ns = lax.axis_size("dp"), lax.axis_size("state")
    rows, wide = values.shape[0] // ns, values.shape[1]
    vmem = pl.BlockSpec(memory_space=pltpu.VMEM)
    return pl.pallas_call(
        functools.partial(state_sum_kernel, nd, ns),
        out_shape=jax.ShapeDtypeStruct((rows, wide), jnp.float32),
        in_specs=[vmem],
        out_specs=vmem,
        scratch_shapes=[
            pltpu.VMEM((ns - 1, rows, wide), values.dtype),
            pltpu.SemaphoreType.DMA((ns - 1,)),
            pltpu.SemaphoreType.DMA((ns - 1,)),
        ],
        compiler_params=pltpu.CompilerParams(collective_id=number, has_side_effects=True),
    )(values.reshape(ns, rows, wide))


def on_device(
    token_ids,
    doc_starts,
    loss_positions,
    loss_targets,
    owners,
    in_weight,
    out_weight,
    table_weight,
    gain_weight,
    in_first,
    out_first,
    table_first,
    gain_first,
    in_second,
    out_second,
    table_second,
    gain_second,
    in_average,
    out_average,
    table_average,
    gain_average,
):
    f32 = jnp.float32
    bf16 = jnp.bfloat16
    nd = lax.axis_size("dp")
    ns = lax.axis_size("state")
    me_dp = lax.axis_index("dp")
    me_state = lax.axis_index("state")
    tokens = token_ids.shape[1]
    slots = loss_positions.shape[1]
    capacity = in_weight.shape[1]
    block_rows = in_weight.shape[2]
    block_count = owners.shape[0]
    width = block_rows * block_count
    own = capacity * block_rows
    wide = nd * own
    key_share = KEY_DIM // ns
    heads = HEADS // ns
    key_cols = HEADS * key_share
    value_width = heads * VAL_DIM
    mixer_cols = 2 * key_cols + value_width
    units = out_weight.shape[3] - value_width
    unit_part = units // nd
    vocab_share = table_weight.shape[3]
    vocab_part = -(-vocab_share // (nd * LANES)) * LANES
    quarter = tokens // ns
    slot_part = slots // ns

    held_all = jnp.sum((owners[None, :] == jnp.arange(nd)[:, None]).astype(jnp.int32), axis=1)
    occupied_all = jnp.arange(capacity)[None, :] < held_all[:, None]
    held = jnp.sum((owners == me_dp).astype(jnp.int32))
    occupied_here = jnp.arange(capacity) < held
    rows_here = jnp.repeat(occupied_here, block_rows)[:, None]

    def lowered(array):
        return jnp.where(rows_here, array[0].reshape(own, -1), 0.0).astype(bf16)

    in_own = lowered(in_weight)
    out_own = lowered(out_weight)

    def in_rows(flat):
        flat = jnp.pad(flat, (0, -flat.shape[0] % (16 * LANES)))
        return flat.reshape(-1, LANES)

    key_part = heads * key_share
    keys_sent = in_own[:, : 2 * key_cols].reshape(own, 2, ns, key_part)
    keys_sent = keys_sent.transpose(2, 0, 1, 3).reshape(ns, own, 2 * key_part)
    rest_sent = jnp.concatenate(
        [in_own[:, 2 * key_cols : mixer_cols], out_own[:, :value_width]], axis=1
    )
    table_padded = lowered(
        jnp.pad(table_weight, ((0, 0), (0, 0), (0, 0), (0, nd * vocab_part - vocab_share)))
    )

    def by_part(columns, parts):
        return columns.reshape(own, nd, parts)

    def zeros(parts):
        return jnp.zeros((own, nd, parts), bf16)

    gu_cols = -(-2 * unit_part // LANES) * LANES
    down_cols = -(-unit_part // LANES) * LANES
    parts_sent = jnp.concatenate(
        [
            by_part(in_own[:, mixer_cols : mixer_cols + units], unit_part),
            by_part(in_own[:, mixer_cols + units :], unit_part),
            zeros(gu_cols - 2 * unit_part),
            by_part(out_own[:, value_width:], unit_part),
            zeros(down_cols - unit_part),
        ],
        axis=2,
    ).transpose(1, 0, 2)
    small, gains_all, stream, keys_all, rest_all, parts_all = front(
        in_rows(jnp.concatenate([token_ids[0], loss_targets[0]])),
        in_rows(gain_weight.astype(bf16).reshape(-1)),
        table_padded,
        keys_sent,
        rest_sent,
        parts_sent,
        tokens,
        vocab_share,
        1,
    )
    small = small.reshape(nd, -1)
    ids_all = small[:, :tokens]
    slot_targets = small[:, tokens : tokens + slots].reshape(nd // 2, 2, ns // 2, 2, slot_part)
    targets_all = slot_targets.transpose(3, 2, 1, 0, 4).reshape(-1)
    gains_all = gains_all.reshape(nd, -1)[:, : capacity * 4 * block_rows].astype(f32)
    gains_all = gains_all.reshape(nd * capacity, 4, block_rows)
    gains = jnp.where(occupied_all.reshape(-1)[:, None, None], gains_all, 0.0)
    gains = gains.transpose(1, 0, 2).reshape(4, wide)
    index = slot_index(owners, capacity)
    head_gain = lax.dynamic_slice_in_dim(
        gains_all[index][:, 1].reshape(width), me_state * value_width, value_width
    )
    live = (targets_all >= 0).astype(f32)
    count = jnp.sum(live)
    local_ids = ids_all.reshape(-1) - me_state * vocab_share
    hit = jnp.arange(vocab_share)[:, None] == local_ids[None, :]
    stream_mine = lax.dynamic_slice_in_dim(stream, me_state * quarter, quarter, axis=1)

    qcols = heads * KEY_DIM
    keys_all = keys_all.reshape(ns, wide, 2 * key_part)
    w_q = keys_all[:, :, :key_part].transpose(1, 0, 2).reshape(wide, qcols)
    w_f = keys_all[:, :, key_part:].transpose(1, 0, 2).reshape(wide, qcols)
    rest_all = rest_all.reshape(wide, 2 * value_width)
    w_v = rest_all[:, :value_width]
    w_o = rest_all[:, value_width:]
    w_fv = jnp.concatenate([w_f, w_v], axis=1)
    w_qfv = jnp.concatenate([w_q, w_fv], axis=1)
    parts_all = parts_all.reshape(wide, -1)
    w_gu = parts_all[:, :gu_cols]
    w_d = parts_all[:, gu_cols:]
    table_padded, stream = lax.optimization_barrier((table_padded, stream))
    table_parts = spread_columns(table_padded, nd)
    late_cols = max(LANES, vocab_part // (4 * LANES) * LANES)
    early_cols = vocab_part - late_cols
    table_early = swap_dp(table_parts[:, :, :early_cols])

    positions = loss_positions[0]
    pick_hit = positions[:, None] == jnp.arange(tokens)[None, :]
    pick = pick_hit.astype(f32)
    pick_low = pick_hit.astype(bf16)
    documents = document_ids(doc_starts[0], tokens)
    doc_at = jnp.sum(jnp.where(pick_hit, documents[None, :], 0), axis=1)
    allowed = (positions[:, None] >= jnp.arange(tokens)[None, :]) & (
        doc_at[:, None] == documents[None, :]
    )

    def tall_norm(values, gain):
        mean = jnp.sum(values * values, axis=0, keepdims=True) * (1.0 / width)
        return values * lax.rsqrt(mean + NORM_EPS) * gain[:, None]

    normed_one = tall_norm(stream.astype(f32), gains[0]).astype(bf16)
    normed_at = times_right(pick_low, normed_one).astype(bf16)
    stream_at = times_right(
        lax.dynamic_slice_in_dim(pick_low, me_state * slot_part, slot_part), stream
    )
    forget_value = times_left(normed_one, w_fv)
    query_pre = times_plain(normed_at, w_q)
    query, back_query = jax.vjp(jax.nn.silu, query_pre)
    (key_gate, log_forget), back_gates = jax.vjp(forget_gates, forget_value[:, :qcols])

    def mix(query_in, key_in, forget_in, value_in):
        return slot_mixer(query_in, key_in, forget_in, value_in, pick, allowed, heads, key_part)

    mixed, back_mix = jax.vjp(
        mix,
        query.astype(bf16).astype(f32),
        key_gate.astype(bf16).astype(f32),
        log_forget,
        forget_value[:, qcols:].astype(bf16).astype(f32),
    )

    def head_norm(mixed_in, gain_in):
        return rms_norm(
            mixed_in.reshape(slots, heads, VAL_DIM), gain_in.reshape(heads, VAL_DIM), VAL_DIM
        ).reshape(slots, value_width)

    gated_f, back_head = jax.vjp(head_norm, mixed, head_gain)
    gated = gated_f.astype(bf16)
    stream_one = stream_at + state_sum(times_right(gated, w_o).astype(bf16), 2)

    def wide_norm(values, gain):
        return rms_norm(values, gain, width)

    normed_two = wide_norm(stream_one, gains[2])
    rows_two = gather_all(normed_two.astype(bf16), 3)
    gate_up = times_plain(rows_two, w_gu)
    hidden = swiglu(gate_up, unit_part, down_cols).astype(bf16)
    ffn_sum, table_late = scatter_all(
        times_right(hidden, w_d).astype(bf16), table_parts[:, :, early_cols:], 4
    )
    stream_two = stream_one + ffn_sum
    table = jnp.concatenate([table_early, table_late], axis=2).reshape(wide, vocab_part)
    normed_three = wide_norm(stream_two, gains[3])
    rows_three = gather_all(normed_three.astype(bf16), 5)

    logits = times_plain(rows_three, table)
    column = jnp.arange(vocab_part)[None, :] + me_dp * vocab_part
    target_hit = (column + me_state * vocab_share == targets_all[:, None]) & (
        column < vocab_share
    )
    logits = jnp.where(column < vocab_share, logits, -1e30)
    top_here = jnp.max(logits, axis=1)
    sum_here = jnp.sum(jnp.exp(logits - top_here[:, None]), axis=1)
    picked_here = jnp.sum(jnp.where(target_hit, logits, 0.0), axis=1)
    shares = combine_all(
        jnp.stack([top_here, sum_here, picked_here]).reshape(3, -1, LANES), add_exponentials, 6
    ).reshape(3, -1)
    lse = shares[0] + jnp.log(shares[1])
    loss_sum = jnp.sum((lse - shares[2]) * live)
    probs = jnp.exp(logits - lse[:, None])
    dlogits = ((probs - target_hit.astype(f32)) * (live / count)[:, None]).astype(bf16)
    grad_table_part = times_left(rows_three, dlogits).astype(bf16)
    grad_one, grad_table_back, grad_ffn, gain_pair = slots_back(
        times_right(dlogits, table).astype(bf16),
        grad_table_part.reshape(nd, own, vocab_part),
        stream_two,
        stream_one,
        gains[2:],
        w_d,
        w_gu,
        gate_up,
        hidden,
        rows_two,
        width,
        unit_part,
        7,
    )
    grad_gain_three, grad_gain_four = gain_pair

    grad_gated = times_plain(grad_one, w_o)
    grad_o_part = times_left(grad_one, gated).astype(bf16)
    grad_gated, grad_o_part = lax.optimization_barrier((grad_gated, grad_o_part))
    grad_mixed, grad_gain_two = back_head(grad_gated)
    grad_query, grad_key, grad_forget, grad_value = back_mix(
        grad_mixed.astype(bf16).astype(f32)
    )
    (grad_query_pre,) = back_query(grad_query)
    grad_query_pre = times_left(pick, grad_query_pre)
    (grad_forget_pre,) = back_gates((grad_key, grad_forget))
    grad_qfv = jnp.concatenate([grad_query_pre, grad_forget_pre, grad_value], axis=1).astype(bf16)
    pick_mine = lax.dynamic_slice_in_dim(pick_low, me_state * quarter, quarter, axis=1)
    grad_rows = times_right(w_qfv, grad_qfv).astype(bf16)
    grad_w_qfv = times_plain(normed_one, grad_qfv).astype(bf16)
    grad_rows, grad_w_qfv = lax.optimization_barrier((grad_rows, grad_w_qfv))
    embed, grad_gain_one = rows_back(
        grad_rows,
        stream_mine,
        gains[0][:, None],
        times_left(grad_one, pick_mine),
        width,
        8,
    )
    embed, grad_ffn, grad_table_back = lax.optimization_barrier(
        (embed, grad_ffn, grad_table_back)
    )
    grad_ffn = swap_dp(grad_ffn.reshape(nd, own, gu_cols + down_cols))
    grad_gain_one = grad_gain_one[:, 0]

    def sum_dp(values):
        return lax.psum_scatter(values, "dp", scatter_dimension=0, tiled=True)

    def square_sum(values):
        values = values.astype(f32)
        return jnp.sum(values * values)

    grad_qfv_own = sum_dp(grad_w_qfv)
    grad_o_own = sum_dp(grad_o_part)
    own_table = times_right(embed, hit.astype(bf16)) + join_columns(grad_table_back)[
        :, :vocab_share
    ].astype(f32)
    squares = square_sum(own_table)
    grad_ffn, squares = lax.optimization_barrier((grad_ffn, squares))
    squares = squares + square_sum(grad_ffn)
    grad_gate = join_columns(grad_ffn[:, :, :unit_part])
    grad_up = join_columns(grad_ffn[:, :, unit_part : 2 * unit_part])
    grad_down = join_columns(grad_ffn[:, :, gu_cols : gu_cols + unit_part])
    grad_qfv_own, grad_o_own, squares, grad_gate, grad_up, grad_down = lax.optimization_barrier(
        (grad_qfv_own, grad_o_own, squares, grad_gate, grad_up, grad_down)
    )
    squares = squares + square_sum(grad_qfv_own) + square_sum(grad_o_own)

    grad_keys = grad_qfv_own[:, : 2 * qcols].reshape(own, 2, ns, key_part)
    grad_keys = grad_keys.transpose(2, 0, 1, 3).reshape(ns, own, 2 * key_part)
    grad_keys = lax.all_to_all(grad_keys, "state", split_axis=0, concat_axis=0, tiled=True)

    head_full = lax.dynamic_update_slice_in_dim(
        jnp.zeros((width,), f32), grad_gain_two, me_state * value_width, 0
    )
    gain_parts = jnp.concatenate([grad_gain_one, grad_gain_three, grad_gain_four, head_full])
    sums = jnp.concatenate([gain_parts, squares[None]])
    sums = jnp.pad(sums, (0, -sums.shape[0] % (8 * LANES))).reshape(-1, LANES)
    sums = combine_all(sums, add_up, 10).reshape(-1)
    gain_sums = sums[: 3 * wide + width]
    head_slots = (
        jnp.zeros((nd * capacity, block_rows), f32)
        .at[index]
        .set(gain_sums[3 * wide :].reshape(block_count, block_rows))
    )
    gain_slots = gain_sums[: 3 * wide].reshape(3, nd * capacity, block_rows)
    gain_slots = jnp.stack([gain_slots[0], head_slots, gain_slots[1], gain_slots[2]], axis=1)
    own_gain = lax.dynamic_slice_in_dim(gain_slots, me_dp * capacity, capacity)

    squares_all = sums[3 * wide + width] + jnp.sum(gain_sums * gain_sums)
    grad_norm = jnp.sqrt(squares_all)
    scale = jnp.minimum(1.0, CLIP_NORM / (grad_norm + 1e-06))
    occupied = occupied_here.astype(f32)
    new_table = adam_blocks(
        table_weight,
        table_first,
        table_second,
        table_average,
        own_table.reshape(table_weight.shape),
        scale,
        LEARN_RATE,
        WEIGHT_DECAY,
        occupied,
    )
    grad_keys, grad_gate, _ = lax.optimization_barrier(
        (grad_keys, grad_gate, new_table[0][0, 0, :8, :LANES])
    )
    grad_keys = grad_keys.reshape(ns, own, 2, key_part).transpose(1, 2, 0, 3)
    own_in = jnp.concatenate(
        [
            grad_keys.reshape(own, 2 * key_cols),
            grad_qfv_own[:, 2 * qcols :],
            grad_gate,
            grad_up,
        ],
        axis=1,
    )
    own_out = jnp.concatenate([grad_o_own, grad_down], axis=1)

    new_in = adam_blocks(
        in_weight,
        in_first,
        in_second,
        in_average,
        own_in.reshape(in_weight.shape),
        scale,
        LEARN_RATE,
        WEIGHT_DECAY,
        occupied,
    )
    new_out = adam_blocks(
        out_weight,
        out_first,
        out_second,
        out_average,
        own_out.reshape(out_weight.shape),
        scale,
        LEARN_RATE,
        WEIGHT_DECAY,
        occupied,
    )
    new_gain = adam_update(
        gain_weight,
        gain_first,
        gain_second,
        gain_average,
        own_gain,
        scale,
        GAIN_RATE,
        0.0,
        occupied[:, None, None],
    )
    return (
        new_in[0],
        new_out[0],
        new_table[0],
        new_gain[0],
        new_in[1],
        new_out[1],
        new_table[1],
        new_gain[1],
        new_in[2],
        new_out[2],
        new_table[2],
        new_gain[2],
        new_in[3],
        new_out[3],
        new_table[3],
        new_gain[3],
        loss_sum,
        count,
        grad_norm,
    )


def solution(mesh):
    return jax.shard_map(
        on_device,
        mesh=mesh,
        in_specs=(
            P("dp", None),
            P("dp", None),
            P("dp", None),
            P("dp", None),
            P(),
            P("state", "dp", None, None),
            P("state", "dp", None, None),
            P("state", "dp", None, None),
            P("dp", None, None),
            P("state", "dp", None, None),
            P("state", "dp", None, None),
            P("state", "dp", None, None),
            P("dp", None, None),
            P("state", "dp", None, None),
            P("state", "dp", None, None),
            P("state", "dp", None, None),
            P("dp", None, None),
            P("state", "dp", None, None),
            P("state", "dp", None, None),
            P("state", "dp", None, None),
            P("dp", None, None),
        ),
        out_specs=(
            P("state", "dp", None, None),
            P("state", "dp", None, None),
            P("state", "dp", None, None),
            P("dp", None, None),
            P("state", "dp", None, None),
            P("state", "dp", None, None),
            P("state", "dp", None, None),
            P("dp", None, None),
            P("state", "dp", None, None),
            P("state", "dp", None, None),
            P("state", "dp", None, None),
            P("dp", None, None),
            P("state", "dp", None, None),
            P("state", "dp", None, None),
            P("state", "dp", None, None),
            P("dp", None, None),
            P(),
            P(),
            P(),
        ),
        check_vma=False,
    )
```

```python
import functools

import jax
import jax.numpy as jnp
from jax import lax
from jax.experimental import pallas as pl
from jax.experimental.pallas import tpu as pltpu
from jax.sharding import PartitionSpec as P

HEADS = 16
KEY_DIM = 128
GROUP = 128
STEP = 5
VAL_DIM = 128


NORM_EPS = 1e-06
LOWER_BOUND = 0.9
CLIP_NORM = 0.02
BETA_FIRST = 0.5
BETA_SECOND = 0.5
ADAM_EPS = 1e-08
LEARN_RATE = 0.02
GAIN_RATE = 0.2
WEIGHT_DECAY = 0.1
AVERAGE_DECAY = 0.9
FULL_PRECISION = lax.Precision.HIGHEST
LANES = 128
CHUNKS = 5
FEED = ((2, 3, 3), (6, 4), 6, (5, 6, 0))


def rms_norm(values, gain, width):
    mean = jnp.sum(values * values, axis=-1, keepdims=True) * (1.0 / width)
    return values * lax.rsqrt(mean + NORM_EPS) * gain


def forget_gates(forget_pre):
    key_gate = (1.0 - LOWER_BOUND) * jax.nn.sigmoid(-forget_pre)
    log_forget = jnp.log(LOWER_BOUND + (1.0 - LOWER_BOUND) * jax.nn.sigmoid(forget_pre))
    return key_gate, log_forget


def slot_mixer(query, key_gate, log_forget, values, pick, allowed, heads, key_part):
    slots = query.shape[0]
    tokens = key_gate.shape[0]
    blocks = tokens // GROUP
    order = jnp.arange(GROUP)
    lower = (order[:, None] >= order[None, :]).astype(jnp.float32)
    number = jnp.arange(blocks)
    before = (number[:, None] > number[None, :]).astype(jnp.float32)
    inside = jnp.einsum(
        "ts,bsk->btk", lower, log_forget.reshape(blocks, GROUP, -1), precision=FULL_PRECISION
    )
    total = inside[:, -1]
    offset = jnp.dot(before, total, precision=FULL_PRECISION)
    ends = offset + total
    along = (inside + offset[:, None]).reshape(tokens, -1)
    at_slots = jnp.dot(pick, along, precision=FULL_PRECISION)
    key_decay = key_gate * jnp.exp(total[:, None] - inside).reshape(tokens, -1)
    grown = query[None] * jnp.exp(jnp.minimum(at_slots[None] - ends[:, None], 16.0))
    key_decay = key_decay.reshape(blocks, GROUP, heads * KEY_DIM)
    column = jnp.arange(heads * KEY_DIM)
    of_head = (column % key_part) // (key_part // heads) == jnp.arange(heads)[:, None]
    grown = jnp.where(of_head[:, None, None], grown[None], 0.0)
    scores = jnp.einsum("hbnk,bgk->hnbg", grown, key_decay, precision=lax.Precision.HIGH)
    scores = jnp.where(allowed[None], scores.reshape(heads, slots, tokens), 0.0)
    mixed = jnp.einsum(
        "hns,shv->nhv", scores, values.reshape(tokens, heads, VAL_DIM), precision=lax.Precision.HIGH
    )
    return mixed.reshape(slots, -1)


def document_ids(starts, length):
    return jnp.sum((jnp.arange(length)[:, None] >= starts[None, :]).astype(jnp.int32), axis=1) - 1


def slot_index(owners, capacity):
    order = jnp.arange(owners.shape[0])
    earlier = (owners[:, None] == owners[None, :]) & (order[None, :] < order[:, None])
    ranks = jnp.sum(earlier.astype(jnp.int32), axis=1)
    return owners * capacity + ranks


def adam_update(weight, first, second, average, grad, scale, rate, decay, occupied):
    clipped = scale * grad
    first_new = BETA_FIRST * first + (1.0 - BETA_FIRST) * clipped
    second_new = BETA_SECOND * second + (1.0 - BETA_SECOND) * clipped * clipped
    first_hat = first_new / (1.0 - BETA_FIRST**STEP)
    second_hat = second_new / (1.0 - BETA_SECOND**STEP)
    weight_new = weight - rate * (first_hat / (jnp.sqrt(second_hat) + ADAM_EPS) + decay * weight)
    average_new = AVERAGE_DECAY * average + (1.0 - AVERAGE_DECAY) * weight_new
    return (
        weight_new * occupied,
        first_new * occupied,
        second_new * occupied,
        average_new * occupied,
    )


def adam_kernel(
    rate, decay, scale_ref, held_ref, weight, first, second, average, grad,
    weight_out, first_out, second_out, average_out
):
    occupied = held_ref[pl.program_id(0)]
    found = adam_update(
        weight[...],
        first[...],
        second[...],
        average[...],
        grad[...].astype(jnp.float32),
        scale_ref[0],
        rate,
        decay,
        occupied,
    )
    for out, value in zip((weight_out, first_out, second_out, average_out), found):
        out[...] = value


def adam_blocks(weight, first, second, average, grad, scale, rate, decay, occupied):
    capacity, block_rows, cols = weight.shape[1:]
    rows = 32
    block = pl.BlockSpec((1, 1, rows, cols), lambda i, j: (0, i, j, 0))
    scalar = pl.BlockSpec(memory_space=pltpu.SMEM)
    return pl.pallas_call(
        functools.partial(adam_kernel, rate, decay),
        grid=(capacity, block_rows // rows),
        out_shape=[jax.ShapeDtypeStruct(weight.shape, weight.dtype)] * 4,
        in_specs=[scalar, scalar] + [block] * 5,
        out_specs=[block] * 4,
        compiler_params=pltpu.CompilerParams(vmem_limit_bytes=48 * 2**20),
    )(scale.reshape(1), occupied, weight, first, second, average, grad)


def times_plain(left, right):
    return jnp.dot(left, right, preferred_element_type=jnp.float32)


def times_right(left, right):
    return lax.dot_general(
        left, right, (((1,), (1,)), ((), ())), preferred_element_type=jnp.float32
    )


def times_left(left, right):
    return lax.dot_general(
        left, right, (((0,), (0,)), ((), ())), preferred_element_type=jnp.float32
    )


def swiglu(joined, units, cols):
    gate = joined[:, :units]
    up = joined[:, units : 2 * units]
    return jnp.pad(jax.nn.silu(gate) * up, ((0, 0), (0, cols - units)))


EVERY = ("dp", "state")


def gather_state(values, axis=0):
    return lax.all_gather(values, "state", axis=axis, tiled=True)


def scatter_state(values, axis=0):
    return lax.psum_scatter(values, "state", scatter_dimension=axis, tiled=True)


def swap_dp(values):
    return lax.all_to_all(values, "dp", split_axis=0, concat_axis=0, tiled=True)


def spread_columns(own, parts):
    return own.reshape(own.shape[0], parts, -1).transpose(1, 0, 2)


def join_columns(split):
    return split.transpose(1, 0, 2).reshape(split.shape[1], -1)


MESH = pl.DeviceIdType.MESH


class Links:
    def __init__(self, sends, recvs):
        self.sends, self.recvs, self.used, self.open = sends, recvs, 0, []

    def copy(self, src, dst, dp, state):
        number = self.used
        self.used += 1
        made = pltpu.make_async_remote_copy(
            src_ref=src,
            dst_ref=dst,
            send_sem=self.sends.at[number],
            recv_sem=self.recvs.at[number],
            device_id=(dp, state),
            device_id_type=MESH,
        )
        made.start()
        self.open.append(made)
        return made

    def settle(self, copies):
        for made in copies:
            made.wait_send()
        self.open = [made for made in self.open if not any(made is one for one in copies)]

    def finish(self):
        for made in self.open:
            made.wait_send()


def nothing(place):
    del place


def greet(peers):
    barrier = pltpu.get_barrier_semaphore()
    for dp, state in peers:
        pl.semaphore_signal(barrier, inc=1, device_id=(dp, state), device_id_type=MESH)
    pl.semaphore_wait(barrier, len(peers))


def places(nd, ns):
    dp, st = lax.axis_index("dp"), lax.axis_index("state")
    return dp, st, lax.div(dp, 2), lax.rem(dp, 2), lax.div(st, 2), lax.rem(st, 2)


def near_peers(nd, ns):
    dp, st, z, y, x, c = places(nd, ns)
    deep, across = nd // 2, ns // 2
    peers = [(lax.rem(z + k, deep) * 2 + y, st) for k in range(1, deep)]
    peers.append((dp + 1 - 2 * y, st))
    peers += [(dp, lax.rem(x + k, across) * 2 + c) for k in range(1, across)]
    peers.append((dp, st + 1 - 2 * c))
    return peers


def add_up(parts):
    found = parts[0]
    for part in parts[1:]:
        found = found + part
    return found


def add_exponentials(parts):
    top = parts[0][0]
    for part in parts[1:]:
        top = jnp.maximum(top, part[0])
    total = add_up([part[1] * jnp.exp(part[0] - top) for part in parts])
    return jnp.stack([top, total, add_up([part[2] for part in parts])])


def combine_kernel(nd, ns, combine, in_ref, out_ref, near, far, sends, recvs):
    dp, st, z, y, x, c = places(nd, ns)
    deep = nd // 2
    plane = []
    for a in range(2):
        for b in range(ns):
            if a or b:
                plane.append((z * 2 + lax.rem(y + a, 2), lax.rem(st + b, ns)))
    line = [(lax.rem(z + k, deep) * 2 + y, st) for k in range(1, deep)]
    greet(plane + line)
    links = Links(sends, recvs)
    me = y * ns + st
    near[me] = in_ref[...]
    made = [links.copy(in_ref, near.at[me], *peer) for peer in plane]
    for copy in made:
        copy.wait_recv()
    far[z] = combine([near[i] for i in range(2 * ns)])
    made = [links.copy(far.at[z], far.at[z], *peer) for peer in line]
    for copy in made:
        copy.wait_recv()
    out_ref[...] = combine([far[i] for i in range(deep)])
    links.finish()


def combine_all(values, combine, number):
    nd, ns = lax.axis_size("dp"), lax.axis_size("state")
    copies = 2 * ns - 1 + nd // 2 - 1
    vmem = pl.BlockSpec(memory_space=pltpu.VMEM)
    return pl.pallas_call(
        functools.partial(combine_kernel, nd, ns, combine),
        out_shape=jax.ShapeDtypeStruct(values.shape, values.dtype),
        in_specs=[vmem],
        out_specs=vmem,
        scratch_shapes=[
            pltpu.VMEM((2 * ns,) + values.shape, values.dtype),
            pltpu.VMEM((nd // 2,) + values.shape, values.dtype),
            pltpu.SemaphoreType.DMA((copies,)),
            pltpu.SemaphoreType.DMA((copies,)),
        ],
        compiler_params=pltpu.CompilerParams(collective_id=number, has_side_effects=True),
    )(values)


def gather_all_kernel(nd, ns, in_ref, out_ref, sends, recvs):
    greet(near_peers(nd, ns))
    links = Links(sends, recvs)
    gather_body(nd, ns, links, in_ref, out_ref)
    links.finish()


def gather_body(nd, ns, links, in_ref, out_ref, meanwhile=nothing):
    dp, st, z, y, x, c = places(nd, ns)
    deep, across = nd // 2, ns // 2
    half = in_ref.shape[1] // 2
    cols = (pl.ds(0, half), pl.ds(half, half))
    to_y = (dp + 1 - 2 * y, st)
    to_core = (dp, st + 1 - 2 * c)
    other_y = 1 - y

    def x_at(k):
        return lax.rem(x + k, across)

    def to_x(k):
        return (dp, x_at(k) * 2 + c)

    def group(xx, yy, part):
        return out_ref.at[c, xx, yy, :, :, cols[part]]

    def send(xx, yy, part, place):
        return links.copy(group(xx, yy, part), group(xx, yy, part), *place)

    out_ref[c, x, y, z] = in_ref[...]
    first = []
    for part in range(2):
        for k in range(1, deep):
            there = (lax.rem(z + k, deep) * 2 + y, st)
            first.append(
                links.copy(
                    in_ref.at[:, cols[part]], out_ref.at[c, x, y, z, :, cols[part]], *there
                )
            )
    for made in first[: deep - 1]:
        made.wait_recv()
    a_y = send(x, y, 0, to_y)
    for made in first[deep - 1 :]:
        made.wait_recv()
    b_x = [send(x, y, 1, to_x(k)) for k in range(1, across)]
    a_x = [send(x, y, 0, to_x(k)) for k in range(1, across)]
    b_y = send(x, y, 1, to_y)
    arriving = [send(x, y, 0, to_core), send(x, y, 1, to_core)]
    meanwhile(0)
    a_y.wait_recv()
    a_xy = [send(x, other_y, 0, to_x(k)) for k in range(1, across)]
    arriving.append(send(x, other_y, 0, to_core))
    b_xy = []
    for k in range(1, across):
        b_x[k - 1].wait_recv()
        from_x = lax.rem(x - k + across, across)
        b_xy.append(send(from_x, y, 1, to_y))
        arriving.append(send(from_x, y, 1, to_core))
    meanwhile(1)
    for k in range(1, across):
        a_x[k - 1].wait_recv()
        arriving.append(send(lax.rem(x - k + across, across), y, 0, to_core))
    b_y.wait_recv()
    arriving.append(send(x, other_y, 1, to_core))
    for k in range(1, across):
        from_x = lax.rem(x - k + across, across)
        a_xy[k - 1].wait_recv()
        arriving.append(send(from_x, other_y, 0, to_core))
        b_xy[k - 1].wait_recv()
        arriving.append(send(from_x, other_y, 1, to_core))
    for made in arriving:
        made.wait_recv()
    links.settle(first + [a_y, b_y] + b_x + a_x + a_xy + b_xy + arriving)


def gather_copies(nd, ns):
    deep, across = nd // 2, ns // 2
    return 2 * (deep - 1) + 2 + 4 * (across - 1) + 4 * across


def gather_all(values, number):
    nd, ns = lax.axis_size("dp"), lax.axis_size("state")
    rows, wide = values.shape
    deep, across = nd // 2, ns // 2
    copies = gather_copies(nd, ns)
    vmem = pl.BlockSpec(memory_space=pltpu.VMEM)
    out = pl.pallas_call(
        functools.partial(gather_all_kernel, nd, ns),
        out_shape=jax.ShapeDtypeStruct((2, across, 2, deep, rows, wide), values.dtype),
        in_specs=[vmem],
        out_specs=vmem,
        scratch_shapes=[pltpu.SemaphoreType.DMA((copies,)), pltpu.SemaphoreType.DMA((copies,))],
        compiler_params=pltpu.CompilerParams(
            collective_id=number, has_side_effects=True, vmem_limit_bytes=40 * 2**20
        ),
    )(values)
    return out.reshape(nd * ns * rows, wide)


def scatter_all_kernel(nd, ns, in_ref, cargo_ref, out_ref, cargo_out, local, *scratch):
    sends, recvs = scratch[-2:]
    dp, st, z, y, x, c = places(nd, ns)
    dp_peers = [(lax.rem(dp + k, nd), st) for k in range(1, nd)]
    x_peers = [(dp, lax.rem(x + k, ns // 2) * 2 + c) for k in range(1, ns // 2)]
    greet(dp_peers + x_peers + [(dp, st + 1 - 2 * c)])
    links = Links(sends, recvs)
    own_copy = pltpu.make_async_copy(cargo_ref.at[dp], cargo_out.at[dp], local.at[0])
    own_copy.start()
    chunk = cargo_ref.shape[1] // CHUNKS
    queue = [(peer, i) for i in range(CHUNKS) for peer in dp_peers]
    third = -(-len(queue) // 3)
    pieces = []

    def feed(place):
        for peer, i in queue[place * third : (place + 1) * third]:
            rows = pl.ds(i * chunk, chunk)
            pieces.append(links.copy(cargo_ref.at[peer[0], rows], cargo_out.at[dp, rows], *peer))

    scatter_body(nd, ns, links, in_ref, out_ref, scratch[:-2], feed)
    for made in pieces:
        made.wait_recv()
    own_copy.wait()
    links.finish()


def scatter_body(nd, ns, links, in_ref, out_ref, scratch, meanwhile=nothing):
    rc, acc, rx_a, ry_a, rz_a, ry_b, rx_b, rz_b = scratch
    dp, st, z, y, x, c = places(nd, ns)
    deep, across = nd // 2, ns // 2
    half = in_ref.shape[5] // 2
    cols = (pl.ds(0, half), pl.ds(half, half))
    to_y = (dp + 1 - 2 * y, st)
    to_core = (dp, st + 1 - 2 * c)
    ys = (y, 1 - y)

    def x_at(k):
        return lax.rem(x + k, across)

    def to_x(k):
        return (dp, x_at(k) * 2 + c)

    core = {}
    order = [(k, ky, 0) for k in range(1, across) for ky in (1, 0)]
    order += [(k, 1, 1) for k in range(across)]
    order += [(0, 1, 0)] + [(k, 0, 1) for k in range(1, across)] + [(0, 0, 0), (0, 0, 1)]
    for k, ky, part in order:
        core[k, ky, part] = links.copy(
            in_ref.at[1 - c, x_at(k), ys[ky], :, :, cols[part]],
            rc.at[x_at(k), ys[ky], :, :, cols[part]],
            *to_core,
        )

    def total(k, ky, part, zz, others):
        found = in_ref[c, x_at(k), ys[ky], zz, :, cols[part]].astype(jnp.float32)
        found += rc[x_at(k), ys[ky], zz, :, cols[part]].astype(jnp.float32)
        for other in others:
            found += other[zz].astype(jnp.float32)
        return found

    def add(k, ky, part, others):
        core[k, ky, part].wait_recv()

        @pl.loop(0, deep)
        def _(zz):
            acc[x_at(k), ys[ky], zz, :, cols[part]] = total(k, ky, part, zz, others).astype(
                acc.dtype
            )

        return acc.at[x_at(k), ys[ky], :, :, cols[part]]

    meanwhile(0)
    a_x, b_y = {}, {}
    for k in range(1, across):
        for ky in (1, 0):
            a_x[k, ky] = links.copy(add(k, ky, 0, []), rx_a.at[k - 1, ky], *to_x(k))
    for k in range(across):
        b_y[k] = links.copy(add(k, 1, 1, []), ry_b.at[k], *to_y)
    meanwhile(1)
    for k in range(1, across):
        a_x[k, 1].wait_recv()
    a_y = links.copy(
        add(0, 1, 0, [rx_a.at[k - 1, 1] for k in range(1, across)]), ry_a, *to_y
    )
    b_x = {}
    for k in range(1, across):
        b_y[k].wait_recv()
        b_x[k] = links.copy(add(k, 0, 1, [ry_b.at[k]]), rx_b.at[k - 1], *to_x(k))
    meanwhile(2)
    for k in range(1, across):
        a_x[k, 0].wait_recv()
    a_y.wait_recv()
    left = [rx_a.at[k - 1, 0] for k in range(1, across)] + [ry_a]
    add(0, 0, 0, left)

    def send_z(part, land):
        return [
            links.copy(
                acc.at[x, y, lax.rem(z + k, deep), :, cols[part]],
                land.at[k - 1],
                lax.rem(z + k, deep) * 2 + y,
                st,
            )
            for k in range(1, deep)
        ]

    a_z = send_z(0, rz_a)
    b_y[0].wait_recv()
    for k in range(1, across):
        b_x[k].wait_recv()
    right = [ry_b.at[0]] + [rx_b.at[k - 1] for k in range(1, across)]
    add(0, 0, 1, right)
    b_z = send_z(1, rz_b)
    for part, made, others, land in ((0, a_z, left, rz_a), (1, b_z, right, rz_b)):
        found = total(0, 0, part, z, others)
        for k in range(1, deep):
            made[k - 1].wait_recv()
            found += land[k - 1].astype(jnp.float32)
        out_ref[:, cols[part]] = found
    links.settle(
        list(core.values()) + list(a_x.values()) + list(b_y.values()) + list(b_x.values())
        + [a_y] + a_z + b_z
    )


def scatter_copies(nd, ns):
    deep, across = nd // 2, ns // 2
    return 4 * across + 2 * (across - 1) + across + 1 + (across - 1) + 2 * (deep - 1)


def scatter_scratch(nd, ns, rows, wide, kind):
    deep, across = nd // 2, ns // 2
    half = wide // 2
    return [
        pltpu.VMEM((across, 2, deep, rows, wide), kind),
        pltpu.VMEM((across, 2, deep, rows, wide), kind),
        pltpu.VMEM((across - 1, 2, deep, rows, half), kind),
        pltpu.VMEM((deep, rows, half), kind),
        pltpu.VMEM((deep - 1, rows, half), kind),
        pltpu.VMEM((across, deep, rows, half), kind),
        pltpu.VMEM((across - 1, deep, rows, half), kind),
        pltpu.VMEM((deep - 1, rows, half), kind),
    ]


def scatter_all(values, cargo, number):
    nd, ns = lax.axis_size("dp"), lax.axis_size("state")
    deep, across = nd // 2, ns // 2
    rows, wide = values.shape[0] // (nd * ns), values.shape[1]
    copies = scatter_copies(nd, ns) + (nd - 1) * CHUNKS
    vmem = pl.BlockSpec(memory_space=pltpu.VMEM)
    hbm = pl.BlockSpec(memory_space=pl.ANY)
    kind = values.dtype
    return pl.pallas_call(
        functools.partial(scatter_all_kernel, nd, ns),
        out_shape=[
            jax.ShapeDtypeStruct((rows, wide), jnp.float32),
            jax.ShapeDtypeStruct(cargo.shape, cargo.dtype),
        ],
        in_specs=[vmem, hbm],
        out_specs=[vmem, hbm],
        scratch_shapes=[pltpu.SemaphoreType.DMA((1,))]
        + scatter_scratch(nd, ns, rows, wide, kind)
        + [pltpu.SemaphoreType.DMA((copies,)), pltpu.SemaphoreType.DMA((copies,))],
        compiler_params=pltpu.CompilerParams(
            collective_id=number, has_side_effects=True, vmem_limit_bytes=40 * 2**20
        ),
    )(values.reshape(2, across, 2, deep, rows, wide), cargo)


def front_kernel(
    nd,
    ns,
    depth_used,
    small_ref,
    gain_ref,
    table_ref,
    keys_ref,
    rest_ref,
    parts_ref,
    small_out,
    gain_out,
    rows_out,
    keys_out,
    rest_out,
    parts_out,
    looked,
    rc,
    acc,
    rx,
    fin,
    sums,
    sends,
    recvs,
    local,
):
    dp, st, z, y, x, c = places(nd, ns)
    deep, across = nd // 2, ns // 2
    own = table_ref.shape[0]
    tokens = rows_out.shape[1]
    part = tokens // ns
    to_core = (dp, st + 1 - 2 * c)
    to_y = (dp + 1 - 2 * y, st)
    other_y = dp + 1 - 2 * y
    dp_peers = [(lax.rem(dp + k, nd), st) for k in range(1, nd)]
    state_peers = [(dp, lax.rem(st + k, ns)) for k in range(1, ns)]
    greet(dp_peers + state_peers)
    links = Links(sends, recvs)

    ids_made = {}
    small_out[dp] = small_ref[...]
    gain_out[dp] = gain_ref[...]
    for k in range(1, nd):
        ids_made[k] = links.copy(small_ref, small_out.at[dp], *dp_peers[k - 1])
    gain_made = [links.copy(gain_ref, gain_out.at[dp], *peer) for peer in dp_peers]

    here = [
        pltpu.make_async_copy(keys_ref.at[st], keys_out.at[st, dp], local.at[0]),
        pltpu.make_async_copy(rest_ref, rest_out.at[dp], local.at[1]),
        pltpu.make_async_copy(parts_ref.at[dp], parts_out.at[dp], local.at[2]),
    ]
    for made in here:
        made.start()
    key_made = [
        links.copy(keys_ref.at[peer[1]], keys_out.at[st, dp], *peer) for peer in state_peers
    ]

    class Gather:
        def __init__(self, view):
            self.view = view
            self.base = links.used
            links.used += 2 * (deep - 1) + 1 + 2 * (deep - 1)

        def copy(self, number, owner, place):
            return pltpu.make_async_remote_copy(
                src_ref=self.view(owner),
                dst_ref=self.view(owner),
                send_sem=sends.at[self.base + number],
                recv_sem=recvs.at[self.base + number],
                device_id=place,
                device_id_type=MESH,
            )

        def pass_on(self, way, step):
            behind = z - way * step
            ahead = z + way
            number = step if way > 0 else deep - 1 + step

            def go(made):
                @pl.when((behind >= 0) & (behind < deep) & (ahead >= 0) & (ahead < deep))
                def _():
                    made(self.copy(number, behind * 2 + y, (ahead * 2 + y, st)))

            return go

        def begin(self):
            self.copy(2 * (deep - 1), dp, to_y).start()
            for way in (1, -1):
                self.pass_on(way, 0)(lambda made: made.start())

        def arrive(self, way, step):
            began = z - way * (step + 1)
            number = step if way > 0 else deep - 1 + step

            @pl.when((began >= 0) & (began < deep))
            def _():
                self.copy(number, began * 2 + y, to_y).wait_recv()
                self.copy(2 * (deep - 1) + 1 + number, began * 2 + y, to_y).start()

            if step + 1 < deep - 1:
                self.pass_on(way, step + 1)(lambda made: made.start())

        def finish(self):
            self.copy(2 * (deep - 1), other_y, to_y).wait_recv()
            self.copy(2 * (deep - 1), dp, to_y).wait_send()
            for way in (1, -1):
                for step in range(deep - 1):
                    began = z - way * (step + 1)
                    number = step if way > 0 else deep - 1 + step
                    self.pass_on(way, step)(lambda made: made.wait_send())

                    @pl.when((began >= 0) & (began < deep))
                    def _():
                        made = self.copy(2 * (deep - 1) + 1 + number, began * 2 + y, to_y)
                        made.wait_send()
                        made.wait_recv()

    rest = Gather(lambda owner: rest_out.at[owner])
    keys = Gather(lambda owner: keys_out.at[:, owner])
    here[1].wait()
    rest.begin()

    def swap(k):
        there = lax.rem(dp + k, nd)
        return links.copy(parts_ref.at[there], parts_out.at[dp], there, st)

    swapped = [swap(k) for k in range(1, nd // 2)]
    here[0].wait()
    for made in key_made:
        made.wait_recv()
    keys.begin()

    def x_at(k):
        return lax.rem(x + k, across)

    def row_at(k):
        return lax.rem(dp + k, nd)

    def block(k, kx, cc):
        start = (x_at(kx) * 2 + cc) * part
        return looked.at[k, :, pl.ds(pl.multiple_of(start, part), part)]

    def place(owner, share):
        return rows_out.at[
            pl.ds(pl.multiple_of(owner * own, own), own),
            pl.ds(pl.multiple_of(share * part, part), part),
        ]

    def add(sources, target):
        @pl.loop(0, own // 32)
        def _(i):
            rows = pl.ds(pl.multiple_of(i * 32, 32), 32)
            found = sources[0][rows, :].astype(jnp.float32)
            for source in sources[1:]:
                found += source[rows, :].astype(jnp.float32)
            target[rows, :] = found.astype(target.dtype)

    depth = table_ref.shape[1]
    piece = min(1024, depth)
    span = 2 * LANES

    def look(k):
        row = row_at(k)

        @pl.loop(0, tokens // span)
        def _(i):
            ids = jnp.concatenate(
                [small_out[row, pl.ds(2 * i, 1), :], small_out[row, pl.ds(2 * i + 1, 1), :]],
                axis=1,
            )
            ids = ids - st * depth_used
            sums[...] = jnp.zeros_like(sums)

            @pl.loop(0, depth // piece)
            def _(j):
                number = lax.broadcasted_iota(jnp.int32, (piece, span), 0)
                hit = jnp.where(number == ids - j * piece, 1.0, 0.0).astype(jnp.bfloat16)
                cols = pl.ds(pl.multiple_of(j * piece, piece), piece)
                sums[...] += jnp.dot(
                    table_ref[:, cols], hit, preferred_element_type=jnp.float32
                )

            cols = pl.ds(pl.multiple_of(i * span, span), span)
            looked[k, :, cols] = sums[...].astype(looked.dtype)

    turn = list(range(1, nd)) + [0]
    core, across_x, across_dp = {}, {}, {}

    def start_core(k):
        for kx in list(range(1, across)) + [0]:
            core[k, kx] = links.copy(block(k, kx, 1 - c), rc.at[k, kx], *to_core)

    def start_x(k):
        for kx in range(1, across):
            core[k, kx].wait_recv()
            add([block(k, kx, c), rc.at[k, kx]], acc.at[k, kx - 1])
            across_x[k, kx] = links.copy(
                acc.at[k, kx - 1], rx.at[k, kx - 1], dp, x_at(kx) * 2 + c
            )

    def start_dp(k):
        core[k, 0].wait_recv()
        sources = [block(k, 0, c), rc.at[k, 0]]
        for kx in range(1, across):
            across_x[k, kx].wait_recv()
            sources.append(rx.at[k, kx - 1])
        if k:
            add(sources, fin.at[k - 1])
            across_dp[k] = links.copy(fin.at[k - 1], place(dp, st), row_at(k), st)
        else:
            add(sources, place(dp, st))

    chores = []
    for step in range(deep - 1):
        for way in (1, -1):
            chores.append(functools.partial(rest.arrive, way, step))
    for step in range(deep - 1):
        for way in (1, -1):
            chores.append(functools.partial(keys.arrive, way, step))
    each = -(-len(chores) // nd)
    for number, k in enumerate(turn):
        if k:
            ids_made[nd - k].wait_recv()
        look(k)
        start_core(k)
        if number >= 1:
            start_x(turn[number - 1])
        if number >= 2:
            start_dp(turn[number - 2])
        for _ in range(each):
            if number >= 2 and chores:
                chores.pop(0)()
    start_x(turn[-1])
    start_dp(turn[-2])
    start_dp(turn[-1])
    swapped += [swap(k) for k in range(nd // 2, nd)]
    later, last = {}, []
    for number, k in enumerate([0] + list(range(1, nd))):
        owner = lax.rem(dp - k + nd, nd)
        if k:
            across_dp[k].wait_recv()
        for kx in range(1, across):
            later[k, kx] = links.copy(
                place(owner, st), place(owner, st), dp, x_at(kx) * 2 + c
            )
        last.append(links.copy(place(owner, st), place(owner, st), *to_core))
        if chores:
            chores.pop(0)()
    for k in range(nd):
        owner = lax.rem(dp - k + nd, nd)
        for kx in range(1, across):
            later[k, kx].wait_recv()
            share = lax.rem(x - kx + across, across) * 2 + c
            last.append(links.copy(place(owner, share), place(owner, share), *to_core))
    while chores:
        chores.pop(0)()
    for made in last + swapped + gain_made:
        made.wait_recv()
    here[2].wait()
    links.finish()
    rest.finish()
    keys.finish()


def front(small, gain, table, keys, rest, parts, tokens, vocab, number):
    nd, ns = lax.axis_size("dp"), lax.axis_size("state")
    deep, across = nd // 2, ns // 2
    own = table.shape[0]
    part = tokens // ns
    kind = table.dtype
    copies = 2 * (nd - 1) + ns - 1 + 2 * (4 * (deep - 1) + 1) + nd - 1
    copies += nd * across + nd * (across - 1) + nd - 1 + nd * across + nd * (across - 1)
    vmem = pl.BlockSpec(memory_space=pltpu.VMEM)
    hbm = pl.BlockSpec(memory_space=pl.ANY)
    return pl.pallas_call(
        functools.partial(front_kernel, nd, ns, vocab),
        out_shape=[
            jax.ShapeDtypeStruct((nd,) + small.shape, small.dtype),
            jax.ShapeDtypeStruct((nd,) + gain.shape, gain.dtype),
            jax.ShapeDtypeStruct((nd * own, tokens), kind),
            jax.ShapeDtypeStruct((ns, nd) + keys.shape[1:], kind),
            jax.ShapeDtypeStruct((nd,) + rest.shape, kind),
            jax.ShapeDtypeStruct(parts.shape, kind),
        ],
        in_specs=[vmem, vmem, vmem, hbm, hbm, hbm],
        out_specs=[vmem, vmem, vmem, hbm, hbm, hbm],
        scratch_shapes=[
            pltpu.VMEM((nd, own, tokens), kind),
            pltpu.VMEM((nd, across, own, part), kind),
            pltpu.VMEM((nd, across - 1, own, part), kind),
            pltpu.VMEM((nd, across - 1, own, part), kind),
            pltpu.VMEM((nd - 1, own, part), kind),
            pltpu.VMEM((own, 2 * LANES), jnp.float32),
            pltpu.SemaphoreType.DMA((copies,)),
            pltpu.SemaphoreType.DMA((copies,)),
            pltpu.SemaphoreType.DMA((3,)),
        ],
        compiler_params=pltpu.CompilerParams(
            collective_id=number, has_side_effects=True, vmem_limit_bytes=52 * 2**20
        ),
        cost_estimate=pl.CostEstimate(
            flops=2 * table.size * nd * tokens, bytes_accessed=4 * parts.size, transcendentals=0
        ),
    )(small, gain, table, keys, rest, parts)


def slots_back_kernel(
    nd,
    ns,
    width,
    units,
    part_hbm,
    table_ref,
    two_ref,
    one_ref,
    gain_ref,
    wd_ref,
    wgu_ref,
    gu_ref,
    hidden_ref,
    rows_ref,
    one_out,
    table_out,
    ffn_out,
    gains_out,
    part_ref,
    summed,
    low,
    down,
    dgu,
    dffn,
    local,
    *scratch,
):
    sends, recvs = scratch[-2:]
    dp, st, z, y, x, c = places(nd, ns)
    deep, across = nd // 2, ns // 2
    count, wide = two_ref.shape
    every = nd * ns * count
    dp_peers = [(lax.rem(dp + k, nd), st) for k in range(1, nd)]
    state_peers = [(dp, lax.rem(st + k, ns)) for k in range(1, ns)]
    fill = pltpu.make_async_copy(part_hbm, part_ref, local.at[2])
    fill.start()
    greet(dp_peers + state_peers)
    links = Links(sends, recvs)
    own_copy = pltpu.make_async_copy(table_ref.at[dp], table_out.at[dp], local.at[0])
    own_copy.start()
    local_copies = [own_copy]
    own = table_ref.shape[1]
    chunk = own // CHUNKS
    queue = [(peer, i) for i in range(CHUNKS) for peer in dp_peers]
    swapped = []

    def feed(amount):
        for _ in range(min(amount, len(queue))):
            peer, i = queue.pop(0)
            rows = pl.ds(i * chunk, chunk)
            swapped.append(
                links.copy(table_ref.at[peer[0], rows], table_out.at[dp, rows], *peer)
            )

    def feeding(amounts):
        return lambda place: feed(amounts[place])

    def norm_back(grad, values, gain, row):
        mean = jnp.sum(values * values, axis=1, keepdims=True) * (1.0 / width)
        root = lax.rsqrt(mean + NORM_EPS)
        scaled = grad * gain
        inner = jnp.sum(scaled * values, axis=1, keepdims=True) * (1.0 / width)
        gains_out[pl.ds(row, 1), :] = jnp.sum(grad * values * root, axis=0, keepdims=True)
        return scaled * root - values * (root * root * root * inner)

    fill.wait()
    scatter_body(nd, ns, links, part_ref, summed, scratch[:-2], feeding(FEED[0]))
    summed[...] = norm_back(summed[...], two_ref[...], gain_ref[pl.ds(1, 1), :], 1)
    low[...] = summed[...].astype(low.dtype)
    gather_body(nd, ns, links, low, down, feeding(FEED[1]))
    feed(FEED[2])

    inner_cols = gu_ref.shape[1]
    step = deep * count
    flat_down = down

    @pl.loop(0, 2 * across * 2)
    def _(i):
        cc, rest = lax.div(i, 2 * across), lax.rem(i, 2 * across)
        xx, yy = lax.div(rest, 2), lax.rem(rest, 2)
        rows = pl.ds(pl.multiple_of(i * step, step), step)
        grad = jnp.dot(
            flat_down[cc, xx, yy].reshape(step, wide),
            wd_ref[...],
            preferred_element_type=jnp.float32,
        )
        grad = jnp.concatenate(
            [grad, jnp.zeros((step, inner_cols - grad.shape[1]), jnp.float32)], axis=1
        ) if inner_cols > grad.shape[1] else grad[:, :inner_cols]
        gate = gu_ref[rows, :]
        up = pltpu.roll(gate, inner_cols - units, 1)
        gated = 1.0 / (1.0 + jnp.exp(-gate))
        grad_gate = grad * up * (gated * (1.0 + gate * (1.0 - gated)))
        grad_up = pltpu.roll(grad * gate * gated, units, 1)
        lanes = lax.broadcasted_iota(jnp.int32, grad_gate.shape, 1)
        joined = jnp.where(lanes < units, grad_gate, grad_up).astype(dgu.dtype)
        dgu[rows, :] = joined
        part_ref[cc, xx, yy] = (
            lax.dot_general(
                joined, wgu_ref[...], (((1,), (1,)), ((), ())), preferred_element_type=jnp.float32
            )
            .astype(part_ref.dtype)
            .reshape(deep, count, wide)
        )

    def weight_grads(place):
        feed(FEED[3][place])
        if place:
            return
        span = 2 * LANES

        @pl.loop(0, wide // span)
        def _(i):
            cols = pl.ds(pl.multiple_of(i * span, span), span)
            dffn[cols, :inner_cols] = lax.dot_general(
                rows_ref[:, cols], dgu[...], (((0,), (0,)), ((), ())),
                preferred_element_type=jnp.float32,
            ).astype(dgu.dtype)
            dffn[cols, inner_cols:] = lax.dot_general(
                flat_down[:, :, :, :, :, cols].reshape(every, span), hidden_ref[...],
                (((0,), (0,)), ((), ())),
                preferred_element_type=jnp.float32,
            ).astype(dgu.dtype)

        home = pltpu.make_async_copy(dffn, ffn_out, local.at[1])
        home.start()
        local_copies.append(home)

    grad_two = summed[...]
    scatter_body(nd, ns, links, part_ref, summed, scratch[:-2], weight_grads)
    grad_one = grad_two + norm_back(summed[...], one_ref[...], gain_ref[pl.ds(0, 1), :], 0)
    one_out[st] = grad_one.astype(one_out.dtype)
    low[...] = grad_one.astype(low.dtype)
    made = [links.copy(low, one_out.at[st], *peer) for peer in state_peers]
    for copy in made:
        copy.wait_recv()
    feed(len(queue))
    for copy in swapped:
        copy.wait_recv()
    for copy in local_copies:
        copy.wait()
    links.finish()


def slots_back(part, table, two, one, gain, wd, wgu, gu, hidden, rows, width, units, number):
    nd, ns = lax.axis_size("dp"), lax.axis_size("state")
    deep, across = nd // 2, ns // 2
    count, wide = two.shape
    kind = part.dtype
    cols = wgu.shape[1] + wd.shape[1]
    copies = 2 * scatter_copies(nd, ns) + gather_copies(nd, ns) + (nd - 1) * CHUNKS + ns - 1
    vmem = pl.BlockSpec(memory_space=pltpu.VMEM)
    hbm = pl.BlockSpec(memory_space=pl.ANY)
    six = (2, across, 2, deep, count, wide)
    out = pl.pallas_call(
        functools.partial(slots_back_kernel, nd, ns, width, units),
        out_shape=[
            jax.ShapeDtypeStruct((ns, count, wide), kind),
            jax.ShapeDtypeStruct(table.shape, kind),
            jax.ShapeDtypeStruct((wide, cols), kind),
            jax.ShapeDtypeStruct((2, wide), jnp.float32),
        ],
        in_specs=[hbm, hbm] + [vmem] * 8,
        out_specs=[vmem, hbm, hbm, vmem],
        scratch_shapes=[
            pltpu.VMEM(six, kind),
            pltpu.VMEM((count, wide), jnp.float32),
            pltpu.VMEM((count, wide), kind),
            pltpu.VMEM(six, kind),
            pltpu.VMEM((nd * ns * count, wgu.shape[1]), kind),
            pltpu.VMEM((wide, cols), kind),
            pltpu.SemaphoreType.DMA((3,)),
        ]
        + scatter_scratch(nd, ns, count, wide, kind)
        + [pltpu.SemaphoreType.DMA((copies,)), pltpu.SemaphoreType.DMA((copies,))],
        compiler_params=pltpu.CompilerParams(
            collective_id=number, has_side_effects=True, vmem_limit_bytes=58 * 2**20
        ),
        cost_estimate=pl.CostEstimate(
            flops=8 * rows.size * cols, bytes_accessed=100 * part.size, transcendentals=0
        ),
    )(part.reshape(six), table, two, one, gain, wd, wgu, gu, hidden, rows)
    return (out[0].reshape(ns * count, wide),) + tuple(out[1:])


def rows_back_kernel(
    nd, ns, width, in_ref, stream_ref, gain_ref, more_ref, out_ref, gain_out, rc, acc, rx, fin, low,
    sends, recvs
):
    dp, st, z, y, x, c = places(nd, ns)
    across = ns // 2
    tokens = in_ref.shape[1]
    own = in_ref.shape[0] // nd
    part = tokens // ns
    to_core = (dp, st + 1 - 2 * c)
    dp_peers = [(lax.rem(dp + k, nd), st) for k in range(1, nd)]
    peers = dp_peers + [(dp, lax.rem(x + k, across) * 2 + c) for k in range(1, across)]
    greet(peers + [to_core])
    links = Links(sends, recvs)

    def x_at(k):
        return lax.rem(x + k, across)

    def rows_of(owner):
        return pl.ds(pl.multiple_of(owner * own, own), own)

    def block(k, kx, cc):
        start = (x_at(kx) * 2 + cc) * part
        return in_ref.at[pl.ds(k * own, own), pl.ds(pl.multiple_of(start, part), part)]

    def place(row, share):
        return out_ref.at[:, pl.ds(pl.multiple_of(row * tokens + share * part, part), part)]

    def add(sources, target):
        @pl.loop(0, own // 32)
        def _(i):
            rows = pl.ds(pl.multiple_of(i * 32, 32), 32)
            found = sources[0][rows, :].astype(jnp.float32)
            for source in sources[1:]:
                found += source[rows, :].astype(jnp.float32)
            target[rows, :] = found.astype(target.dtype)

    core, across_x = {}, {}
    for kx in list(range(1, across)) + [0]:
        for k in range(nd):
            core[k, kx] = links.copy(block(k, kx, 1 - c), rc.at[k, kx], *to_core)
    for kx in range(1, across):
        for k in range(nd):
            core[k, kx].wait_recv()
            add([block(k, kx, c), rc.at[k, kx]], acc.at[k, kx - 1])
            across_x[k, kx] = links.copy(
                acc.at[k, kx - 1], rx.at[k, kx - 1], dp, x_at(kx) * 2 + c
            )
    for k in range(nd):
        core[k, 0].wait_recv()
        sources = [block(k, 0, c), rc.at[k, 0]]
        for kx in range(1, across):
            across_x[k, kx].wait_recv()
            sources.append(rx.at[k, kx - 1])
        add(sources, fin.at[pl.ds(k * own, own), :])

    step = 32
    pieces = in_ref.shape[0] // step

    def at(i):
        return pl.ds(pl.multiple_of(i * step, step), step)

    def gather_sums(i, carry):
        square, inner = carry
        values = stream_ref[at(i), :].astype(jnp.float32)
        scaled = fin[at(i), :] * gain_ref[at(i), :] * values
        square = square + jnp.sum(values * values, axis=0, keepdims=True)
        return square, inner + jnp.sum(scaled, axis=0, keepdims=True)

    none = jnp.zeros((1, part), jnp.float32)
    square, inner = lax.fori_loop(0, pieces, gather_sums, (none, none))
    root = lax.rsqrt(square * (1.0 / width) + NORM_EPS)
    inner = inner * (1.0 / width) * root * root * root

    @pl.loop(0, pieces)
    def _(i):
        values = stream_ref[at(i), :].astype(jnp.float32)
        grad = fin[at(i), :]
        gain_out[at(i), :] = jnp.sum(grad * values * root, axis=1, keepdims=True)
        found = grad * gain_ref[at(i), :] * root - values * inner + more_ref[at(i), :]
        low[at(i), :] = found.astype(low.dtype)

    swapped = [links.copy(low.at[rows_of(p[0]), :], place(dp, st), *p) for p in dp_peers]
    place(dp, st)[...] = low[rows_of(dp), :]
    later, last = {}, []
    for k in range(nd):
        row = lax.rem(dp - k + nd, nd)
        if k:
            swapped[k - 1].wait_recv()
        for kx in range(1, across):
            later[k, kx] = links.copy(place(row, st), place(row, st), dp, x_at(kx) * 2 + c)
        last.append(links.copy(place(row, st), place(row, st), *to_core))
    for k in range(nd):
        row = lax.rem(dp - k + nd, nd)
        for kx in range(1, across):
            later[k, kx].wait_recv()
            share = lax.rem(x - kx + across, across) * 2 + c
            last.append(links.copy(place(row, share), place(row, share), *to_core))
    for made in last:
        made.wait_recv()
    links.finish()


def rows_back(values, stream, gain, more, width, number):
    nd, ns = lax.axis_size("dp"), lax.axis_size("state")
    across = ns // 2
    wide, tokens = values.shape
    own, part = wide // nd, tokens // ns
    copies = nd * across + nd * (across - 1) + nd - 1 + nd * across + nd * (across - 1)
    vmem = pl.BlockSpec(memory_space=pltpu.VMEM)
    kind = values.dtype
    return pl.pallas_call(
        functools.partial(rows_back_kernel, nd, ns, width),
        out_shape=[
            jax.ShapeDtypeStruct((own, nd * tokens), kind),
            jax.ShapeDtypeStruct((wide, 1), jnp.float32),
        ],
        in_specs=[vmem] * 4,
        out_specs=[vmem] * 2,
        scratch_shapes=[
            pltpu.VMEM((nd, across, own, part), kind),
            pltpu.VMEM((nd, across - 1, own, part), kind),
            pltpu.VMEM((nd, across - 1, own, part), kind),
            pltpu.VMEM((wide, part), jnp.float32),
            pltpu.VMEM((wide, part), kind),
            pltpu.SemaphoreType.DMA((copies,)),
            pltpu.SemaphoreType.DMA((copies,)),
        ],
        compiler_params=pltpu.CompilerParams(
            collective_id=number, has_side_effects=True, vmem_limit_bytes=48 * 2**20
        ),
        cost_estimate=pl.CostEstimate(
            flops=0, bytes_accessed=60 * values.size, transcendentals=0
        ),
    )(values, stream, gain, more)


def state_sum_kernel(nd, ns, in_ref, out_ref, land, sends, recvs):
    dp, st = lax.axis_index("dp"), lax.axis_index("state")
    peers = [(dp, lax.rem(st + k, ns)) for k in range(1, ns)]
    greet(peers)
    links = Links(sends, recvs)
    made = [
        links.copy(in_ref.at[there[1]], land.at[k], *there) for k, there in enumerate(peers)
    ]
    found = in_ref[st].astype(jnp.float32)
    for k in range(ns - 1):
        made[k].wait_recv()
        found += land[k].astype(jnp.float32)
    out_ref[...] = found
    links.finish()


def state_sum(values, number):
    nd, ns = lax.axis_size("dp"), lax.axis_size("state")
    rows, wide = values.shape[0] // ns, values.shape[1]
    vmem = pl.BlockSpec(memory_space=pltpu.VMEM)
    return pl.pallas_call(
        functools.partial(state_sum_kernel, nd, ns),
        out_shape=jax.ShapeDtypeStruct((rows, wide), jnp.float32),
        in_specs=[vmem],
        out_specs=vmem,
        scratch_shapes=[
            pltpu.VMEM((ns - 1, rows, wide), values.dtype),
            pltpu.SemaphoreType.DMA((ns - 1,)),
            pltpu.SemaphoreType.DMA((ns - 1,)),
        ],
        compiler_params=pltpu.CompilerParams(collective_id=number, has_side_effects=True),
    )(values.reshape(ns, rows, wide))


def on_device(
    token_ids,
    doc_starts,
    loss_positions,
    loss_targets,
    owners,
    in_weight,
    out_weight,
    table_weight,
    gain_weight,
    in_first,
    out_first,
    table_first,
    gain_first,
    in_second,
    out_second,
    table_second,
    gain_second,
    in_average,
    out_average,
    table_average,
    gain_average,
):
    f32 = jnp.float32
    bf16 = jnp.bfloat16
    nd = lax.axis_size("dp")
    ns = lax.axis_size("state")
    me_dp = lax.axis_index("dp")
    me_state = lax.axis_index("state")
    tokens = token_ids.shape[1]
    slots = loss_positions.shape[1]
    capacity = in_weight.shape[1]
    block_rows = in_weight.shape[2]
    block_count = owners.shape[0]
    width = block_rows * block_count
    own = capacity * block_rows
    wide = nd * own
    key_share = KEY_DIM // ns
    heads = HEADS // ns
    key_cols = HEADS * key_share
    value_width = heads * VAL_DIM
    mixer_cols = 2 * key_cols + value_width
    units = out_weight.shape[3] - value_width
    unit_part = units // nd
    vocab_share = table_weight.shape[3]
    vocab_part = -(-vocab_share // (nd * LANES)) * LANES
    quarter = tokens // ns
    slot_part = slots // ns

    held_all = jnp.sum((owners[None, :] == jnp.arange(nd)[:, None]).astype(jnp.int32), axis=1)
    occupied_all = jnp.arange(capacity)[None, :] < held_all[:, None]
    held = jnp.sum((owners == me_dp).astype(jnp.int32))
    occupied_here = jnp.arange(capacity) < held
    rows_here = jnp.repeat(occupied_here, block_rows)[:, None]

    def lowered(array):
        return jnp.where(rows_here, array[0].reshape(own, -1), 0.0).astype(bf16)

    in_own = lowered(in_weight)
    out_own = lowered(out_weight)

    def in_rows(flat):
        flat = jnp.pad(flat, (0, -flat.shape[0] % (16 * LANES)))
        return flat.reshape(-1, LANES)

    key_part = heads * key_share
    keys_sent = in_own[:, : 2 * key_cols].reshape(own, 2, ns, key_part)
    keys_sent = keys_sent.transpose(2, 0, 1, 3).reshape(ns, own, 2 * key_part)
    rest_sent = jnp.concatenate(
        [in_own[:, 2 * key_cols : mixer_cols], out_own[:, :value_width]], axis=1
    )
    table_padded = lowered(
        jnp.pad(table_weight, ((0, 0), (0, 0), (0, 0), (0, nd * vocab_part - vocab_share)))
    )

    def by_part(columns, parts):
        return columns.reshape(own, nd, parts)

    def zeros(parts):
        return jnp.zeros((own, nd, parts), bf16)

    gu_cols = -(-2 * unit_part // LANES) * LANES
    down_cols = -(-unit_part // LANES) * LANES
    parts_sent = jnp.concatenate(
        [
            by_part(in_own[:, mixer_cols : mixer_cols + units], unit_part),
            by_part(in_own[:, mixer_cols + units :], unit_part),
            zeros(gu_cols - 2 * unit_part),
            by_part(out_own[:, value_width:], unit_part),
            zeros(down_cols - unit_part),
        ],
        axis=2,
    ).transpose(1, 0, 2)
    small, gains_all, stream, keys_all, rest_all, parts_all = front(
        in_rows(jnp.concatenate([token_ids[0], loss_targets[0]])),
        in_rows(gain_weight.astype(bf16).reshape(-1)),
        table_padded,
        keys_sent,
        rest_sent,
        parts_sent,
        tokens,
        vocab_share,
        1,
    )
    small = small.reshape(nd, -1)
    ids_all = small[:, :tokens]
    slot_targets = small[:, tokens : tokens + slots].reshape(nd // 2, 2, ns // 2, 2, slot_part)
    targets_all = slot_targets.transpose(3, 2, 1, 0, 4).reshape(-1)
    gains_all = gains_all.reshape(nd, -1)[:, : capacity * 4 * block_rows].astype(f32)
    gains_all = gains_all.reshape(nd * capacity, 4, block_rows)
    gains = jnp.where(occupied_all.reshape(-1)[:, None, None], gains_all, 0.0)
    gains = gains.transpose(1, 0, 2).reshape(4, wide)
    index = slot_index(owners, capacity)
    head_gain = lax.dynamic_slice_in_dim(
        gains_all[index][:, 1].reshape(width), me_state * value_width, value_width
    )
    live = (targets_all >= 0).astype(f32)
    count = jnp.sum(live)
    local_ids = ids_all.reshape(-1) - me_state * vocab_share
    hit = jnp.arange(vocab_share)[:, None] == local_ids[None, :]
    stream_mine = lax.dynamic_slice_in_dim(stream, me_state * quarter, quarter, axis=1)

    qcols = heads * KEY_DIM
    keys_all = keys_all.reshape(ns, wide, 2 * key_part)
    w_q = keys_all[:, :, :key_part].transpose(1, 0, 2).reshape(wide, qcols)
    w_f = keys_all[:, :, key_part:].transpose(1, 0, 2).reshape(wide, qcols)
    rest_all = rest_all.reshape(wide, 2 * value_width)
    w_v = rest_all[:, :value_width]
    w_o = rest_all[:, value_width:]
    w_fv = jnp.concatenate([w_f, w_v], axis=1)
    w_qfv = jnp.concatenate([w_q, w_fv], axis=1)
    parts_all = parts_all.reshape(wide, -1)
    w_gu = parts_all[:, :gu_cols]
    w_d = parts_all[:, gu_cols:]
    table_padded, stream = lax.optimization_barrier((table_padded, stream))
    table_parts = spread_columns(table_padded, nd)
    late_cols = max(LANES, vocab_part // (4 * LANES) * LANES)
    early_cols = vocab_part - late_cols
    table_early = swap_dp(table_parts[:, :, :early_cols])

    positions = loss_positions[0]
    pick_hit = positions[:, None] == jnp.arange(tokens)[None, :]
    pick = pick_hit.astype(f32)
    pick_low = pick_hit.astype(bf16)
    documents = document_ids(doc_starts[0], tokens)
    doc_at = jnp.sum(jnp.where(pick_hit, documents[None, :], 0), axis=1)
    allowed = (positions[:, None] >= jnp.arange(tokens)[None, :]) & (
        doc_at[:, None] == documents[None, :]
    )

    def tall_norm(values, gain):
        mean = jnp.sum(values * values, axis=0, keepdims=True) * (1.0 / width)
        return values * lax.rsqrt(mean + NORM_EPS) * gain[:, None]

    normed_one = tall_norm(stream.astype(f32), gains[0]).astype(bf16)
    normed_at = times_right(pick_low, normed_one).astype(bf16)
    stream_at = times_right(
        lax.dynamic_slice_in_dim(pick_low, me_state * slot_part, slot_part), stream
    )
    forget_value = times_left(normed_one, w_fv)
    query_pre = times_plain(normed_at, w_q)
    query, back_query = jax.vjp(jax.nn.silu, query_pre)
    (key_gate, log_forget), back_gates = jax.vjp(forget_gates, forget_value[:, :qcols])

    def mix(query_in, key_in, forget_in, value_in):
        return slot_mixer(query_in, key_in, forget_in, value_in, pick, allowed, heads, key_part)

    mixed, back_mix = jax.vjp(
        mix,
        query.astype(bf16).astype(f32),
        key_gate.astype(bf16).astype(f32),
        log_forget,
        forget_value[:, qcols:].astype(bf16).astype(f32),
    )

    def head_norm(mixed_in, gain_in):
        return rms_norm(
            mixed_in.reshape(slots, heads, VAL_DIM), gain_in.reshape(heads, VAL_DIM), VAL_DIM
        ).reshape(slots, value_width)

    gated_f, back_head = jax.vjp(head_norm, mixed, head_gain)
    gated = gated_f.astype(bf16)
    stream_one = stream_at + state_sum(times_right(gated, w_o).astype(bf16), 2)

    def wide_norm(values, gain):
        return rms_norm(values, gain, width)

    normed_two = wide_norm(stream_one, gains[2])
    rows_two = gather_all(normed_two.astype(bf16), 3)
    gate_up = times_plain(rows_two, w_gu)
    hidden = swiglu(gate_up, unit_part, down_cols).astype(bf16)
    ffn_sum, table_late = scatter_all(
        times_right(hidden, w_d).astype(bf16), table_parts[:, :, early_cols:], 4
    )
    stream_two = stream_one + ffn_sum
    table = jnp.concatenate([table_early, table_late], axis=2).reshape(wide, vocab_part)
    normed_three = wide_norm(stream_two, gains[3])
    rows_three = gather_all(normed_three.astype(bf16), 5)

    logits = times_plain(rows_three, table)
    column = jnp.arange(vocab_part)[None, :] + me_dp * vocab_part
    target_hit = (column + me_state * vocab_share == targets_all[:, None]) & (
        column < vocab_share
    )
    logits = jnp.where(column < vocab_share, logits, -1e30)
    top_here = jnp.max(logits, axis=1)
    sum_here = jnp.sum(jnp.exp(logits - top_here[:, None]), axis=1)
    picked_here = jnp.sum(jnp.where(target_hit, logits, 0.0), axis=1)
    shares = combine_all(
        jnp.stack([top_here, sum_here, picked_here]).reshape(3, -1, LANES), add_exponentials, 6
    ).reshape(3, -1)
    lse = shares[0] + jnp.log(shares[1])
    loss_sum = jnp.sum((lse - shares[2]) * live)
    probs = jnp.exp(logits - lse[:, None])
    dlogits = ((probs - target_hit.astype(f32)) * (live / count)[:, None]).astype(bf16)
    grad_table_part = times_left(rows_three, dlogits).astype(bf16)
    grad_one, grad_table_back, grad_ffn, gain_pair = slots_back(
        times_right(dlogits, table).astype(bf16),
        grad_table_part.reshape(nd, own, vocab_part),
        stream_two,
        stream_one,
        gains[2:],
        w_d,
        w_gu,
        gate_up,
        hidden,
        rows_two,
        width,
        unit_part,
        7,
    )
    grad_gain_three, grad_gain_four = gain_pair

    grad_gated = times_plain(grad_one, w_o)
    grad_o_part = times_left(grad_one, gated).astype(bf16)
    grad_gated, grad_o_part = lax.optimization_barrier((grad_gated, grad_o_part))
    grad_mixed, grad_gain_two = back_head(grad_gated)
    grad_query, grad_key, grad_forget, grad_value = back_mix(
        grad_mixed.astype(bf16).astype(f32)
    )
    (grad_query_pre,) = back_query(grad_query)
    grad_query_pre = times_left(pick, grad_query_pre)
    (grad_forget_pre,) = back_gates((grad_key, grad_forget))
    grad_qfv = jnp.concatenate([grad_query_pre, grad_forget_pre, grad_value], axis=1).astype(bf16)
    pick_mine = lax.dynamic_slice_in_dim(pick_low, me_state * quarter, quarter, axis=1)
    grad_rows = times_right(w_qfv, grad_qfv).astype(bf16)
    grad_w_qfv = times_plain(normed_one, grad_qfv).astype(bf16)
    grad_rows, grad_w_qfv = lax.optimization_barrier((grad_rows, grad_w_qfv))
    embed, grad_gain_one = rows_back(
        grad_rows,
        stream_mine,
        gains[0][:, None],
        times_left(grad_one, pick_mine),
        width,
        8,
    )
    embed, grad_ffn, grad_table_back = lax.optimization_barrier(
        (embed, grad_ffn, grad_table_back)
    )
    grad_ffn = swap_dp(grad_ffn.reshape(nd, own, gu_cols + down_cols))
    grad_gain_one = grad_gain_one[:, 0]

    def sum_dp(values):
        return lax.psum_scatter(values, "dp", scatter_dimension=0, tiled=True)

    def square_sum(values):
        values = values.astype(f32)
        return jnp.sum(values * values)

    grad_qfv_own = sum_dp(grad_w_qfv)
    grad_o_own = sum_dp(grad_o_part)
    own_table = times_right(embed, hit.astype(bf16)) + join_columns(grad_table_back)[
        :, :vocab_share
    ].astype(f32)
    squares = square_sum(own_table)
    grad_ffn, squares = lax.optimization_barrier((grad_ffn, squares))
    squares = squares + square_sum(grad_ffn)
    grad_gate = join_columns(grad_ffn[:, :, :unit_part])
    grad_up = join_columns(grad_ffn[:, :, unit_part : 2 * unit_part])
    grad_down = join_columns(grad_ffn[:, :, gu_cols : gu_cols + unit_part])
    grad_qfv_own, grad_o_own, squares, grad_gate, grad_up, grad_down = lax.optimization_barrier(
        (grad_qfv_own, grad_o_own, squares, grad_gate, grad_up, grad_down)
    )
    squares = squares + square_sum(grad_qfv_own) + square_sum(grad_o_own)

    grad_keys = grad_qfv_own[:, : 2 * qcols].reshape(own, 2, ns, key_part)
    grad_keys = grad_keys.transpose(2, 0, 1, 3).reshape(ns, own, 2 * key_part)
    grad_keys = lax.all_to_all(grad_keys, "state", split_axis=0, concat_axis=0, tiled=True)

    head_full = lax.dynamic_update_slice_in_dim(
        jnp.zeros((width,), f32), grad_gain_two, me_state * value_width, 0
    )
    gain_parts = jnp.concatenate([grad_gain_one, grad_gain_three, grad_gain_four, head_full])
    sums = jnp.concatenate([gain_parts, squares[None]])
    sums = jnp.pad(sums, (0, -sums.shape[0] % (8 * LANES))).reshape(-1, LANES)
    sums = combine_all(sums, add_up, 10).reshape(-1)
    gain_sums = sums[: 3 * wide + width]
    head_slots = (
        jnp.zeros((nd * capacity, block_rows), f32)
        .at[index]
        .set(gain_sums[3 * wide :].reshape(block_count, block_rows))
    )
    gain_slots = gain_sums[: 3 * wide].reshape(3, nd * capacity, block_rows)
    gain_slots = jnp.stack([gain_slots[0], head_slots, gain_slots[1], gain_slots[2]], axis=1)
    own_gain = lax.dynamic_slice_in_dim(gain_slots, me_dp * capacity, capacity)

    squares_all = sums[3 * wide + width] + jnp.sum(gain_sums * gain_sums)
    grad_norm = jnp.sqrt(squares_all)
    scale = jnp.minimum(1.0, CLIP_NORM / (grad_norm + 1e-06))
    occupied = occupied_here.astype(f32)
    new_table = adam_blocks(
        table_weight,
        table_first,
        table_second,
        table_average,
        own_table.reshape(table_weight.shape),
        scale,
        LEARN_RATE,
        WEIGHT_DECAY,
        occupied,
    )
    grad_keys, grad_gate, _ = lax.optimization_barrier(
        (grad_keys, grad_gate, new_table[0][0, 0, :8, :LANES])
    )
    grad_keys = grad_keys.reshape(ns, own, 2, key_part).transpose(1, 2, 0, 3)
    own_in = jnp.concatenate(
        [
            grad_keys.reshape(own, 2 * key_cols),
            grad_qfv_own[:, 2 * qcols :],
            grad_gate,
            grad_up,
        ],
        axis=1,
    )
    own_out = jnp.concatenate([grad_o_own, grad_down], axis=1)

    new_in = adam_blocks(
        in_weight,
        in_first,
        in_second,
        in_average,
        own_in.reshape(in_weight.shape),
        scale,
        LEARN_RATE,
        WEIGHT_DECAY,
        occupied,
    )
    new_out = adam_blocks(
        out_weight,
        out_first,
        out_second,
        out_average,
        own_out.reshape(out_weight.shape),
        scale,
        LEARN_RATE,
        WEIGHT_DECAY,
        occupied,
    )
    new_gain = adam_update(
        gain_weight,
        gain_first,
        gain_second,
        gain_average,
        own_gain,
        scale,
        GAIN_RATE,
        0.0,
        occupied[:, None, None],
    )
    return (
        new_in[0],
        new_out[0],
        new_table[0],
        new_gain[0],
        new_in[1],
        new_out[1],
        new_table[1],
        new_gain[1],
        new_in[2],
        new_out[2],
        new_table[2],
        new_gain[2],
        new_in[3],
        new_out[3],
        new_table[3],
        new_gain[3],
        loss_sum,
        count,
        grad_norm,
    )


def solution(mesh):
    return jax.shard_map(
        on_device,
        mesh=mesh,
        in_specs=(
            P("dp", None),
            P("dp", None),
            P("dp", None),
            P("dp", None),
            P(),
            P("state", "dp", None, None),
            P("state", "dp", None, None),
            P("state", "dp", None, None),
            P("dp", None, None),
            P("state", "dp", None, None),
            P("state", "dp", None, None),
            P("state", "dp", None, None),
            P("dp", None, None),
            P("state", "dp", None, None),
            P("state", "dp", None, None),
            P("state", "dp", None, None),
            P("dp", None, None),
            P("state", "dp", None, None),
            P("state", "dp", None, None),
            P("state", "dp", None, None),
            P("dp", None, None),
        ),
        out_specs=(
            P("state", "dp", None, None),
            P("state", "dp", None, None),
            P("state", "dp", None, None),
            P("dp", None, None),
            P("state", "dp", None, None),
            P("state", "dp", None, None),
            P("state", "dp", None, None),
            P("dp", None, None),
            P("state", "dp", None, None),
            P("state", "dp", None, None),
            P("state", "dp", None, None),
            P("dp", None, None),
            P("state", "dp", None, None),
            P("state", "dp", None, None),
            P("state", "dp", None, None),
            P("dp", None, None),
            P(),
            P(),
            P(),
        ),
        check_vma=False,
    )
```
